32 devices in a mesh: ctx: 8 (over y, x, core), tp: 4 (over z).
Axes of the slice: x: 2, y: 2, z: 4, core: 2. Of those that a mesh axis runs over, the one named last changes fastest.
Arguments:
- hidden_in: bfloat16 [3072, 1024], P('ctx'), may hold values from -6 to 6
- doc_starts: int32 [8], replicated, may hold values from 0 to 3071, as said below
- norm1_gain: float32 [1024], replicated, may hold values from 0.5 to 1.5
- w_query: bfloat16 [1024, 1024], P(None, 'tp'), may hold values from -0.1875 to 0.1875
- w_key: bfloat16 [1024, 512], P(None, 'tp'), may hold values from -0.1875 to 0.1875
- w_value: bfloat16 [1024, 512], P(None, 'tp'), may hold values from -0.1875 to 0.1875
- query_gain: float32 [64], replicated, may hold values from 1 to 2
- key_gain: float32 [64], replicated, may hold values from 0.25 to 1.75
- w_out: bfloat16 [1024, 1024], P('tp'), may hold values from -1.25 to 1.25
- norm2_gain: float32 [1024], replicated, may hold values from 0.5 to 1.5
- w_gate: bfloat16 [1024, 4608], P(None, 'tp'), may hold values from -0.1875 to 0.1875
- w_up: bfloat16 [1024, 4608], P(None, 'tp'), may hold values from -0.1875 to 0.1875
- w_down: bfloat16 [4608, 1024], P('tp'), may hold values from -0.09375 to 0.09375
- out_grad: bfloat16 [3072, 1024], P('ctx'), may hold values from -6 to 6
Outputs:
- layer_out: bfloat16 [3072, 1024], P('ctx')
- input_grad: float32 [3072, 1024], P('ctx')
- norm1_gain_grad: float32 [1024], P('ctx')
- w_query_grad: float32 [1024, 1024], P('ctx', 'tp')
- w_key_grad: float32 [1024, 512], P('ctx', 'tp')
- w_value_grad: float32 [1024, 512], P('ctx', 'tp')
- query_gain_grad: float32 [64], replicated
- key_gain_grad: float32 [64], replicated
- w_out_grad: float32 [1024, 1024], P('tp', 'ctx')
- norm2_gain_grad: float32 [1024], P('ctx')
- w_gate_grad: float32 [1024, 4608], P('ctx', 'tp')
- w_up_grad: float32 [1024, 4608], P('ctx', 'tp')
- w_down_grad: float32 [4608, 1024], P('tp', 'ctx')
The draws below stay inside these ranges and needn't reach their ends.
Inputs may be any that keep to these rules, and one draw needn't show every extreme that they name: doc_starts[0] is 0, the last entry is 3071, and the entries rise strictly; the first 4 entries are below 384 and the others above 2688, so one document runs from the first block of the stream into the last.
All inputs are finite; a program needn't handle non-finite values.
Results may differ from the reference program's by a relative error of at most 0.023.
Values may be sent and summed in bfloat16 or wider, within the bound.
No kernel may reach another device: no remote copies, remote signals or barrier semaphores. Data moves between devices by JAX's collectives and lax.ppermute only.
A program may use at most 192 MiB of HBM per device.

```python
import jax
import jax.numpy as jnp
from jax import lax

D = 1024
HEADS = 16
KV_HEADS = 8
HEAD_DIM = 64
FF = 4608
TOK_DEV = 384
DOCS = 8
TOKENS = 3072


def draw_doc_starts(key, part):
    key = jax.random.fold_in(key, 11)
    leading_key, trailing_key = jax.random.split(key)
    halved = DOCS // 2
    leading = jnp.sort(jax.random.permutation(leading_key, TOK_DEV - 1)[:halved - 1] + 1)
    trailing = jnp.sort(jax.random.permutation(trailing_key, TOK_DEV - 2)[:halved - 1] + (TOKENS - TOK_DEV + 1))
    final_start = jnp.full((1,), TOKENS - 1, jnp.int32)
    return jnp.concatenate([jnp.zeros((1,), jnp.int32), leading.astype(jnp.int32), trailing.astype(jnp.int32), final_start])


def shard_levels(own_key, shape, cuts, low, top_value):
    def one(axis_at, parts):
        heights = jax.random.uniform(jax.random.fold_in(jax.random.fold_in(own_key, 6), axis_at), (parts,), jnp.float32, low / len(cuts), top_value / len(cuts))
        return jnp.repeat(jnp.exp(heights), shape[axis_at] // parts).reshape((-1,) + (1,) * (len(shape) - axis_at - 1))

    level = one(*cuts[0])
    for cut in cuts[1:]:
        level = level * one(*cut)
    return level


def gaussian(stream_key, dims, deviation, bound, pieces=(), kind=jnp.bfloat16):
    array = deviation * jax.random.normal(stream_key, dims, jnp.float32)
    if pieces:
        array = array * shard_levels(stream_key, dims, pieces, -0.22, 0.18)
    return jnp.clip(array, -bound, bound).astype(kind)


def setup_inputs(seed: int = 0) -> dict:
    arg_keys = jax.random.split(jax.random.key(seed), 15)
    return {
        "hidden_in": gaussian(arg_keys[0], (TOKENS, D), 1.0, 6.0, ((0, 8),)),
        "doc_starts": draw_doc_starts(jax.random.fold_in(arg_keys[14], 71), 0),
        "norm1_gain": jnp.clip(1.0 + 0.1 * jax.random.normal(arg_keys[2], (D,), jnp.float32), 0.5, 1.5),
        "w_query": gaussian(arg_keys[3], (D, HEADS * HEAD_DIM), D ** -0.5, 0.1875, ((1, 4),)),
        "w_key": gaussian(arg_keys[4], (D, KV_HEADS * HEAD_DIM), D ** -0.5, 0.1875, ((1, 4),)),
        "w_value": gaussian(arg_keys[5], (D, KV_HEADS * HEAD_DIM), D ** -0.5, 0.1875, ((1, 4),)),
        "query_gain": jnp.clip(jax.random.uniform(arg_keys[6], (HEAD_DIM,), jnp.float32, 1.0, 2.0), 1.0, 2.0),
        "key_gain": jnp.clip(1.0 + 0.15 * jax.random.normal(arg_keys[7], (HEAD_DIM,), jnp.float32), 0.25, 1.75),
        "w_out": gaussian(arg_keys[8], (HEADS * HEAD_DIM, D), (max(1, D * 64 // TOKENS)) ** -0.5, 1.25, ((0, 4),)),
        "norm2_gain": jnp.clip(1.0 + 0.1 * jax.random.normal(arg_keys[9], (D,), jnp.float32), 0.5, 1.5),
        "w_gate": gaussian(arg_keys[10], (D, FF), D ** -0.5, 0.1875, ((1, 4),)),
        "w_up": gaussian(arg_keys[11], (D, FF), D ** -0.5, 0.1875, ((1, 4),)),
        "w_down": gaussian(arg_keys[12], (FF, D), FF ** -0.5, 0.09375, ((0, 4),)),
        "out_grad": gaussian(arg_keys[13], (TOKENS, D), 1.0, 6.0, ((0, 8),)),
    }


norm_eps = 1e-05
rope_base = 1000000.0
masked_score = -1e+30

@jax.custom_vjp
def low(v):
    return lax.optimization_barrier(v.astype(jnp.bfloat16)).astype(jnp.float32)

@jax.custom_vjp
def low_back(v):
    return v

def low_keep(v):
    return (low(v), None)

def low_pass(kept, grad):
    return (grad,)

def back_keep(v):
    return (v, None)

def back_low(kept, grad):
    return (low(grad),)
low.defvjp(low_keep, low_pass)
low_back.defvjp(back_keep, back_low)

def matmul(left, right):
    return jnp.dot(left, right, precision=lax.Precision.HIGHEST, preferred_element_type=jnp.float32)

def rms_scale(values, gain):
    inverse = lax.rsqrt(lax.optimization_barrier(jnp.mean(values * values, axis=-1, keepdims=True)) + norm_eps)
    return values * inverse * gain

def rotate(values, cosine, sine):
    halfway = values.shape[-1] // 2
    first_half = values[..., :halfway]
    second_half = values[..., halfway:]
    return jnp.concatenate([first_half * cosine - second_half * sine, second_half * cosine + first_half * sine], axis=-1)

def attend(queries, keys, values, doc_ids):
    row_block = min(512, TOKENS)
    group_size = HEADS // KV_HEADS
    block_count = TOKENS // row_block
    block_starts = jnp.arange(block_count, dtype=jnp.int32) * row_block
    positions = jnp.arange(TOKENS, dtype=jnp.int32)
    score_scale = HEAD_DIM ** (-0.5)

    def one_head(head_items):
        head_queries, head_keys, head_values = head_items

        def one_block(block_parts):
            query_block, block_start = block_parts
            scores = jnp.einsum('qgd,kd->gqk', query_block, head_keys, precision=lax.Precision.HIGHEST) * score_scale
            scores = low_back(scores)
            query_pos = block_start + jnp.arange(row_block, dtype=jnp.int32)
            query_doc = lax.dynamic_slice_in_dim(doc_ids, block_start, row_block, 0)
            visible = (doc_ids[None, :] == query_doc[:, None]) & (positions[None, :] <= query_pos[:, None])
            row_peak = lax.optimization_barrier(jnp.max(jnp.where(visible, scores, masked_score), axis=-1, keepdims=True))
            weights = jnp.where(visible, jnp.exp(scores - row_peak), 0.0)
            attention_probs = weights / lax.optimization_barrier(jnp.sum(weights, axis=-1, keepdims=True))
            return jnp.einsum('gqk,kd->qgd', low(attention_probs), head_values, precision=lax.Precision.HIGHEST)
        blocked = lax.map(jax.checkpoint(one_block), (head_queries.reshape(block_count, row_block, group_size, HEAD_DIM), block_starts))
        return blocked.reshape(TOKENS, group_size, HEAD_DIM)
    outputs = lax.map(one_head, (jnp.transpose(queries, (1, 0, 2, 3)), jnp.transpose(keys, (1, 0, 2)), jnp.transpose(values, (1, 0, 2))))
    return jnp.transpose(outputs, (1, 0, 2, 3)).reshape(TOKENS, HEADS * HEAD_DIM)

def reference(hidden_in, doc_starts, norm1_gain, w_query, w_key, w_value, query_gain, key_gain, w_out, norm2_gain, w_gate, w_up, w_down, out_grad):
    positions = jnp.arange(TOKENS, dtype=jnp.int32)
    inside = doc_starts[None, :] <= positions[:, None]
    doc_ids = lax.optimization_barrier(jnp.sum(inside.astype(jnp.int32), axis=1)) - 1
    doc_begin = lax.optimization_barrier(jnp.max(jnp.where(inside, doc_starts[None, :], 0), axis=1))
    relative = (positions - doc_begin).astype(jnp.float32)
    frequency = rope_base ** (-2.0 * jnp.arange(HEAD_DIM // 2, dtype=jnp.float32) / HEAD_DIM)
    angles = relative[:, None] * frequency[None, :]
    cosine = jnp.cos(angles)[:, None, :]
    sine = jnp.sin(angles)[:, None, :]
    group_size = HEADS // KV_HEADS

    def forward(inputs, gain_one, query_w, key_w, value_w, query_g, key_g, out_w, gain_two, gate_w, up_w, down_w):
        normed = low(rms_scale(inputs, gain_one))
        query_pre = low_back(matmul(normed, query_w)).reshape(TOKENS, HEADS, HEAD_DIM)
        key_pre = low_back(matmul(normed, key_w)).reshape(TOKENS, KV_HEADS, HEAD_DIM)
        value_rows = low_back(low(matmul(normed, value_w))).reshape(TOKENS, KV_HEADS, HEAD_DIM)
        query_rows = low_back(low(rotate(rms_scale(query_pre, query_g), cosine, sine)))
        key_rows = low_back(low(rotate(rms_scale(key_pre, key_g), cosine, sine)))
        attended = attend(query_rows.reshape(TOKENS, KV_HEADS, group_size, HEAD_DIM), key_rows, value_rows, doc_ids)
        attended = low_back(low(attended))
        mixed = inputs + low_back(matmul(attended, out_w))
        normed_two = low(rms_scale(mixed, gain_two))
        gate_rows = low_back(matmul(normed_two, gate_w))
        up_rows = low_back(matmul(normed_two, up_w))
        activation = low(jax.nn.silu(gate_rows) * up_rows)
        return mixed + matmul(activation, down_w)
    result, pullback = jax.vjp(forward, hidden_in.astype(jnp.float32), norm1_gain.astype(jnp.float32), w_query.astype(jnp.float32), w_key.astype(jnp.float32), w_value.astype(jnp.float32), query_gain.astype(jnp.float32), key_gain.astype(jnp.float32), w_out.astype(jnp.float32), norm2_gain.astype(jnp.float32), w_gate.astype(jnp.float32), w_up.astype(jnp.float32), w_down.astype(jnp.float32))
    grads = pullback(out_grad.astype(jnp.float32))
    return (result.astype(jnp.bfloat16), grads[0], grads[1], grads[2], grads[3], grads[4], grads[5], grads[6], grads[7], grads[8], grads[9], grads[10], grads[11])
```

```python
import functools
import math

import jax
import jax.numpy as jnp
from jax import lax
from jax.experimental import pallas as pl
from jax.experimental.pallas import tpu as pltpu
from jax.sharding import PartitionSpec as P

norm_eps = 1e-05
rope_base = 1000000.0
f32 = jnp.float32
bf16 = jnp.bfloat16
NN = (((1,), (0,)), ((), ()))
NT = (((1,), (1,)), ((), ()))
TN = (((0,), (0,)), ((), ()))
VMEM = pl.BlockSpec(memory_space=pltpu.VMEM)
SMEM = pl.BlockSpec(memory_space=pltpu.SMEM)
vmem_limit = 56 * 1024 * 1024


def dot(left, right, dims=NN):
    return lax.dot_general(left, right, dims, preferred_element_type=f32)


def call(body, inputs, outs, scratch=(), flops=0, **kwargs):
    in_specs = kwargs.pop("in_specs", None)
    if in_specs is None:
        in_specs = [
            SMEM if (x.dtype == jnp.int32 and x.ndim == 1) else VMEM for x in inputs
        ]
    out_specs = kwargs.pop("out_specs", [VMEM] * len(outs))
    moved = sum(x.size * x.dtype.itemsize for x in inputs) + sum(
        math.prod(o.shape) * o.dtype.itemsize for o in outs
    )
    return pl.pallas_call(
        body,
        out_shape=outs,
        in_specs=in_specs,
        out_specs=out_specs,
        scratch_shapes=list(scratch),
        compiler_params=pltpu.CompilerParams(vmem_limit_bytes=vmem_limit),
        cost_estimate=pl.CostEstimate(flops=flops, bytes_accessed=moved, transcendentals=0),
        **kwargs,
    )(*inputs)


def shape(dims, dtype):
    return jax.ShapeDtypeStruct(dims, dtype)


def lanes(x):
    return lax.broadcasted_iota(jnp.int32, x.shape, 1)


def head_mean(x):
    first = lanes(x) < 64
    low = jnp.sum(jnp.where(first, x, 0.0), axis=1, keepdims=True)
    high = jnp.sum(jnp.where(first, 0.0, x), axis=1, keepdims=True)
    return jnp.where(first, low, high) * (1.0 / 64.0)


def swap_halves(x):
    return jnp.where(lanes(x) % 64 < 32, pltpu.roll(x, 96, 1), pltpu.roll(x, 32, 1))


def head_norm(pre, gain):
    inverse = lax.rsqrt(head_mean(pre * pre) + norm_eps)
    return pre * inverse * gain


def head_norm_back(pre, gain, grads):
    inverse = lax.rsqrt(head_mean(pre * pre) + norm_eps)
    normed = pre * inverse
    scaled = grads * gain
    inner = head_mean(scaled * normed)
    return inverse * (scaled - normed * inner), grads * normed


def row_norm(x):
    return lax.rsqrt(jnp.mean(x * x, axis=1, keepdims=True) + norm_eps)


def kv_kernel(x_ref, gain_ref, wk_ref, wv_ref, cos_ref, sin_ref, kgain_ref, h_ref, kv_ref, kpre_ref):
    x = x_ref[...].astype(f32)
    h = (x * row_norm(x) * gain_ref[...]).astype(bf16)
    h_ref[...] = h
    kpre = dot(h, wk_ref[...])
    kpre_ref[...] = kpre
    kn = head_norm(kpre, kgain_ref[...])
    key = kn * cos_ref[...] + swap_halves(kn) * sin_ref[...]
    kv_ref[:, :128] = key.astype(bf16)
    kv_ref[:, 128:] = dot(h, wv_ref[...]).astype(bf16)


def spread(x, half, out_ref, base, rows):
    rolled = pltpu.roll(x, 64, 1)
    keep = (lanes(x) < 64) if half == 0 else (lanes(x) >= 64)
    first, second = (x, rolled) if half == 0 else (rolled, x)
    out_ref[pl.ds(base, rows), :] = jnp.where(keep, first, 0.0).astype(bf16)
    return jnp.where(keep, second, 0.0).astype(bf16)


def q_kernel(h_ref, wq_ref, cos_ref, sin_ref, qgain_ref, qpad_ref, qpre_ref):
    rows = h_ref.shape[0]
    qpre = dot(h_ref[...], wq_ref[...])
    qpre_ref[...] = qpre
    for half in range(2):
        qn = head_norm(qpre[:, 128 * half : 128 * half + 128], qgain_ref[...])
        x = qn * cos_ref[...] + swap_halves(qn) * sin_ref[...]
        base = 2 * half * rows
        qpad_ref[pl.ds(base + rows, rows), :] = spread(x, half, qpad_ref, base, rows)


def block_id(index, parity, mine, relative):
    return jnp.bitwise_xor(mine, 2 * index + parity) if relative else index


def block_mask(scal_ref, begin_ref, block, rows):
    dims = (rows, 2 * rows)
    key_pos = lax.broadcasted_iota(jnp.int32, dims, 0) + block * rows
    across = lax.broadcasted_iota(jnp.int32, (1, 2 * rows), 1)
    query_pos = scal_ref[0] * rows + jnp.where(across < rows, across, across - rows)
    return (key_pos <= query_pos) & (key_pos >= begin_ref[...])


def attend_kernel(relative, scale, scal_ref, begin_ref, qpad_ref, *refs):
    count = 2 if relative else 1
    kv_refs = refs[:count]
    o_ref, o32_ref, lse_ref, acc_ref, mass_ref = refs[count:]
    rows = o_ref.shape[0]
    mine = scal_ref[0]
    acc_ref[...] = jnp.zeros_like(acc_ref)
    mass_ref[...] = jnp.zeros_like(mass_ref)
    factor = scale * math.log2(math.e)

    for parity, kv_ref in enumerate(kv_refs):

        def visit(index, masked, kv_ref=kv_ref, parity=parity):
            block = block_id(index, parity, mine, relative)
            at = pl.ds(pl.multiple_of(index * rows, rows), rows)
            keys = kv_ref[at, :128]
            values_t = kv_ref[at, 128:].T
            for j in range(2):
                s = dot(keys, qpad_ref[2 * rows * j : 2 * rows * (j + 1), :], NT)
                p = jnp.exp2(s * factor)
                if masked:
                    p = jnp.where(block_mask(scal_ref, begin_ref, block, rows), p, 0.0)
                mass_ref[j : j + 1, :] += jnp.sum(p, axis=0, keepdims=True)
                acc_ref[j] += dot(values_t, p.astype(bf16))

        def step(index, carry, visit=visit, parity=parity):
            block = block_id(index, parity, mine, relative)
            start = block * rows
            seen = (block <= mine) & (start + rows - 1 >= scal_ref[2])
            whole = (block < mine) & (start >= scal_ref[3])
            pl.when(seen & whole)(lambda: visit(index, False))
            pl.when(seen & jnp.logical_not(whole))(lambda: visit(index, True))
            return carry

        lax.fori_loop(0, kv_ref.shape[0] // rows, step, 0)

    mass = mass_ref[...]
    lse_ref[...] = jnp.log2(mass)
    parts = []
    for j in range(2):
        normed = acc_ref[j, 64 * j : 64 * j + 64, :] / mass[j : j + 1, :]
        parts += [normed[:, :rows], normed[:, rows:]]
    o32 = jnp.concatenate(parts, axis=0).T
    o32_ref[...] = o32
    o_ref[...] = o32.astype(bf16)


def attend_back_kernel(relative, scale, n_tp, scal_ref, begin_ref, qpad_ref, o32_ref, lse_ref, *refs):
    count = 2 if relative else 1
    kv_refs, refs = refs[:count], refs[count:]
    dout_refs, refs = refs[:n_tp], refs[n_tp:]
    dq_ref, refs = refs[0], refs[1:]
    dkv_refs, refs = refs[:count], refs[count:]
    dout_ref, dopad_ref, dqt_ref = refs
    rows = dq_ref.shape[0]
    own = rows // n_tp
    mine = scal_ref[0]
    factor = scale * math.log2(math.e)
    for k in range(n_tp):
        at = pl.multiple_of(jnp.bitwise_xor(scal_ref[1], k) * own, own)
        dout_ref[pl.ds(at, own), :] = dout_refs[k][...].astype(f32)
    dout = dout_ref[...]
    for half in range(2):
        x = dout[:, 128 * half : 128 * half + 128]
        base = 2 * half * rows
        dopad_ref[pl.ds(base + rows, rows), :] = spread(x, half, dopad_ref, base, rows)
    weighted = (dout * o32_ref[...]).T
    deltas = [jnp.sum(weighted[64 * h : 64 * h + 64], axis=0, keepdims=True) for h in range(4)]
    delta = [jnp.concatenate(deltas[2 * j : 2 * j + 2], axis=1) for j in range(2)]
    dqt_ref[...] = jnp.zeros_like(dqt_ref)

    for parity in range(count):
        kv_ref, dkv_ref = kv_refs[parity], dkv_refs[parity]

        def visit(index, masked, kv_ref=kv_ref, dkv_ref=dkv_ref, parity=parity):
            block = block_id(index, parity, mine, relative)
            at = pl.ds(pl.multiple_of(index * rows, rows), rows)
            keys = kv_ref[at, :128]
            values = kv_ref[at, 128:]
            keys_t = keys.T
            dk = jnp.zeros((rows, 128), f32)
            dv = jnp.zeros((rows, 128), f32)
            for j in range(2):
                qpad = qpad_ref[2 * rows * j : 2 * rows * (j + 1), :]
                dopad = dopad_ref[2 * rows * j : 2 * rows * (j + 1), :]
                p = jnp.exp2(dot(keys, qpad, NT) * factor - lse_ref[j : j + 1, :])
                if masked:
                    p = jnp.where(block_mask(scal_ref, begin_ref, block, rows), p, 0.0)
                ds = (p * (dot(values, dopad, NT) - delta[j])).astype(bf16)
                dv += dot(p.astype(bf16), dopad)
                dk += dot(ds, qpad)
                dqt_ref[j] += dot(keys_t, ds)
            dkv_ref[at, :128] = (dk * scale).astype(bf16)
            dkv_ref[at, 128:] = dv.astype(bf16)

        def skip(index, dkv_ref=dkv_ref):
            at = pl.ds(pl.multiple_of(index * rows, rows), rows)
            dkv_ref[at, :] = jnp.zeros((rows, 256), bf16)

        def step(index, carry, visit=visit, skip=skip, parity=parity):
            block = block_id(index, parity, mine, relative)
            start = block * rows
            seen = (block <= mine) & (start + rows - 1 >= scal_ref[2])
            whole = (block < mine) & (start >= scal_ref[3])
            pl.when(seen & whole)(lambda: visit(index, False))
            pl.when(seen & jnp.logical_not(whole))(lambda: visit(index, True))
            pl.when(jnp.logical_not(seen))(lambda: skip(index))
            return carry

        lax.fori_loop(0, kv_ref.shape[0] // rows, step, 0)

    parts = []
    for j in range(2):
        part = dqt_ref[j, 64 * j : 64 * j + 64, :]
        parts += [part[:, :rows], part[:, rows:]]
    dq_ref[...] = (jnp.concatenate(parts, axis=0).T * scale).astype(bf16)


def mix_kernel(n_tp, n_ctx, relative, scal_ref, x_ref, gain_ref, w0_ref, *refs):
    wm_ref, wp_ref = refs[:2]
    o_refs = refs[2 : 2 + n_tp]
    h_ref, hp_ref, y_ref, acc_ref = refs[2 + n_tp :]
    rows = x_ref.shape[0]
    own = rows // n_tp
    acc = x_ref[...].astype(f32) + dot(o_refs[0][...], w0_ref[...])
    core = scal_ref[4]
    half = o_refs[0].shape[1] // 2
    for k in range(1, n_tp):
        first = pl.multiple_of(core * half, half)
        second = pl.multiple_of((1 - core) * half, half)
        acc += dot(o_refs[k][:, pl.ds(first, half)], wm_ref[k - 1])
        acc += dot(o_refs[k][:, pl.ds(second, half)], wp_ref[k - 1])
    acc_ref[...] = acc
    y_ref[...] = acc_ref[pl.ds(pl.multiple_of(scal_ref[1] * own, own), own), :]
    h_ref[...] = (acc * row_norm(acc) * gain_ref[...]).astype(bf16)
    permute_columns(n_ctx, relative, scal_ref[0], h_ref, hp_ref)


def permute_columns(n_ctx, relative, mine, src_ref, dst_ref):
    if not relative:
        dst_ref[...] = src_ref[...]
        return
    width = src_ref.shape[1] // n_ctx
    for place, k in enumerate([*range(0, n_ctx, 2), *range(1, n_ctx, 2)]):
        at = pl.multiple_of(jnp.bitwise_xor(mine, k) * width, width)
        dst_ref[:, place * width : (place + 1) * width] = src_ref[:, pl.ds(at, width)]


def order_kernel(n_ctx, relative, scal_ref, a_ref, b_ref, ap_ref, bp_ref):
    permute_columns(n_ctx, relative, scal_ref[0], a_ref, ap_ref)
    permute_columns(n_ctx, relative, scal_ref[0], b_ref, bp_ref)


def feed_kernel(n_tp, scal_ref, h_ref, g_ref, wg_ref, wu_ref, wd_ref, act_ref, dg_ref, du_ref, dh_ref, acc_ref):
    step = pl.program_id(0)
    gate = dot(h_ref[...], wg_ref[...])
    up = dot(h_ref[...], wu_ref[...])
    dact = dot(g_ref[...], wd_ref[...], NT)
    sigma = jax.nn.sigmoid(gate)
    silu = gate * sigma
    act_ref[...] = (silu * up).astype(bf16)
    dgate = (dact * up * sigma * (1.0 + gate * (1.0 - sigma))).astype(bf16)
    dup = (dact * silu).astype(bf16)
    dg_ref[...] = dgate
    du_ref[...] = dup
    total = dot(dgate, wg_ref[...], NT) + dot(dup, wu_ref[...], NT)

    @pl.when(step == 0)
    def _():
        acc_ref[...] = total

    @pl.when(step > 0)
    def _():
        acc_ref[...] += total

    @pl.when(step == pl.num_programs(0) - 1)
    def _():
        own = acc_ref.shape[0] // n_tp
        for k in range(n_tp):
            at = pl.multiple_of(jnp.bitwise_xor(scal_ref[1], k) * own, own)
            dh_ref[k] = acc_ref[pl.ds(at, own), :].astype(bf16)


def mid_kernel(n_tp, n_ctx, relative, scal_ref, g_ref, y_ref, gain_ref, w0_ref, wm_ref, wp_ref, *refs):
    dh_refs = refs[:n_tp]
    dy_ref, dattn_ref, gaing_ref, dout_ref, low_ref = refs[n_tp:]
    own = y_ref.shape[0]
    dh = dh_refs[0][...].astype(f32)
    for k in range(1, n_tp):
        dh += dh_refs[k][...].astype(f32)
    y = y_ref[...]
    inverse = row_norm(y)
    z = y * inverse
    gaing_ref[...] = jnp.sum(dh * z, axis=0, keepdims=True)
    e = dh * gain_ref[...]
    inner = jnp.mean(e * z, axis=1, keepdims=True)
    at = pl.multiple_of(scal_ref[1] * own, own)
    dy = g_ref[pl.ds(at, own), :].astype(f32) + inverse * (e - z * inner)
    dy_ref[...] = dy
    low = dy.astype(bf16)
    low_ref[...] = low
    permute_columns(n_ctx, relative, scal_ref[0], low_ref, dattn_ref)
    dout_ref[0] = dot(low, w0_ref[...], NT).astype(bf16)
    core = scal_ref[4]
    half = w0_ref.shape[0] // 2
    for k in range(1, n_tp):
        first = pl.multiple_of(core * half, half)
        second = pl.multiple_of((1 - core) * half, half)
        dout_ref[k, :, pl.ds(first, half)] = dot(low, wm_ref[k - 1], NT).astype(bf16)
        dout_ref[k, :, pl.ds(second, half)] = dot(low, wp_ref[k - 1], NT).astype(bf16)


def q_back_kernel(dq_ref, qpre_ref, cos_ref, sin_ref, qgain_ref, wq_ref, low_ref, gaing_ref, dh_ref):
    total = jnp.zeros((1, 128), f32)
    for half in range(2):
        cut = slice(128 * half, 128 * half + 128)
        x = dq_ref[:, cut].astype(f32)
        dqn = x * cos_ref[...] - swap_halves(x) * sin_ref[...]
        dpre, weighted = head_norm_back(qpre_ref[:, cut], qgain_ref[...], dqn)
        low_ref[:, cut] = dpre.astype(bf16)
        total += jnp.sum(weighted, axis=0, keepdims=True)
    gaing_ref[...] = total + pltpu.roll(total, 64, 1)
    dh_ref[...] = dot(low_ref[...], wq_ref[...], NT)


def k_back_kernel(n_tp, n_parts, scal_ref, *refs):
    parts, refs = refs[:n_parts], refs[n_parts:]
    kpre_ref, cos_ref, sin_ref, kgain_ref, wk_ref, wv_ref, dhq_ref, x_ref = refs[:8]
    low_ref, gaing_ref, gain1_ref, dh_ref, acc_ref = refs[8:]
    total = parts[0][...].astype(f32)
    for part in parts[1:]:
        total += part[...].astype(f32)
    low = total.astype(bf16)
    x = low[:, :128].astype(f32)
    dkn = x * cos_ref[...] - swap_halves(x) * sin_ref[...]
    dpre, weighted = head_norm_back(kpre_ref[...], kgain_ref[...], dkn)
    gains = jnp.sum(weighted, axis=0, keepdims=True)
    gaing_ref[...] = gains + pltpu.roll(gains, 64, 1)
    dk = dpre.astype(bf16)
    dv = low[:, 128:]
    low_ref[:, :128] = dk
    low_ref[:, 128:] = dv
    dh = dhq_ref[...] + dot(dk, wk_ref[...], NT) + dot(dv, wv_ref[...], NT)
    acc_ref[...] = dh
    x_in = x_ref[...].astype(f32)
    gain1_ref[...] = jnp.sum(dh * (x_in * row_norm(x_in)), axis=0, keepdims=True)
    own = acc_ref.shape[0] // n_tp
    for k in range(n_tp):
        at = pl.multiple_of(jnp.bitwise_xor(scal_ref[1], k) * own, own)
        dh_ref[k] = acc_ref[pl.ds(at, own), :].astype(bf16)


def last_kernel(n_tp, scal_ref, x_ref, dy_ref, gain_ref, *refs):
    dh_refs, out_ref = refs[:n_tp], refs[n_tp]
    own = dy_ref.shape[0]
    dh = dh_refs[0][...].astype(f32)
    for k in range(1, n_tp):
        dh += dh_refs[k][...].astype(f32)
    x = x_ref[pl.ds(pl.multiple_of(scal_ref[1] * own, own), own), :].astype(f32)
    inverse = row_norm(x)
    z = x * inverse
    e = dh * gain_ref[...]
    inner = jnp.mean(e * z, axis=1, keepdims=True)
    out_ref[...] = (dy_ref[...] + inverse * (e - z * inner)).astype(bf16)


def join_kernel(n_tp, scal_ref, *refs):
    out_ref = refs[n_tp]
    own = refs[0].shape[0]
    for k in range(n_tp):
        at = pl.multiple_of(jnp.bitwise_xor(scal_ref[1], k) * own, own)
        out_ref[pl.ds(at, own), :] = refs[k][...].astype(out_ref.dtype)


def swap(x, axis, k):
    size = lax.axis_size(axis)
    return lax.ppermute(x, axis, [(i, i ^ k) for i in range(size)])


def shards(
    hidden_in,
    doc_starts,
    norm1_gain,
    w_query,
    w_key,
    w_value,
    query_gain,
    key_gain,
    w_out,
    norm2_gain,
    w_gate,
    w_up,
    w_down,
    out_grad,
):
    rows, width = hidden_in.shape
    n_ctx, n_tp = lax.axis_size("ctx"), lax.axis_size("tp")
    head_dim = query_gain.shape[0]
    scale = head_dim ** (-0.5)
    relative = n_ctx <= 8 and (width // n_ctx) % 128 == 0
    own = rows // n_tp
    hidden_units = w_gate.shape[1]
    others = range(1, n_tp)
    mine, place = lax.axis_index("ctx"), lax.axis_index("tp")

    positions = mine * rows + jnp.arange(rows, dtype=jnp.int32)
    inside = doc_starts[None, :] <= positions[:, None]
    begin = jnp.max(jnp.where(inside, doc_starts[None, :], 0), axis=1)
    frequency = rope_base ** (-2.0 * jnp.arange(head_dim // 2, dtype=f32) / head_dim)
    angles = (positions - begin).astype(f32)[:, None] * frequency[None, :]
    cosine, sine = jnp.cos(angles), jnp.sin(angles)
    cosine = jnp.concatenate([cosine] * 4, axis=1)
    sine = jnp.concatenate([-sine, sine, -sine, sine], axis=1)
    scal = jnp.stack([mine, place, begin[0], begin[rows - 1], mine % 2]).astype(jnp.int32)
    begin_row = jnp.concatenate([begin, begin])[None, :]
    gain_one, gain_two = norm1_gain[None, :], norm2_gain[None, :]
    q_gain = jnp.concatenate([query_gain, query_gain])[None, :]
    k_gain = jnp.concatenate([key_gain, key_gain])[None, :]

    h_one, kv, key_pre = call(
        kv_kernel,
        [hidden_in, gain_one, w_key, w_value, cosine, sine, k_gain],
        [shape((rows, width), bf16), shape((rows, 256), bf16), shape((rows, 128), f32)],
        flops=2 * rows * width * 256,
    )
    if relative:
        even = jnp.concatenate([kv] + [swap(kv, "ctx", k) for k in range(2, n_ctx, 2)], axis=0)
        kv_all = [even, swap(even, "ctx", 1)]
    else:
        kv_all = [lax.all_gather(kv, "ctx", axis=0, tiled=True)]
    half = w_out.shape[0] // 2
    w_half = lax.dynamic_slice_in_dim(w_out, (mine % 2) * half, half, 0)
    w_mine = jnp.stack([swap(w_half, "tp", k) for k in others])
    w_pair = swap(w_mine, "ctx", 1)

    qpad, query_pre = call(
        q_kernel,
        [h_one, w_query, cosine, sine, q_gain],
        [shape((4 * rows, 128), bf16), shape((rows, 256), f32)],
        flops=2 * rows * width * 256,
    )
    attend_flops = 2 * 2 * (2 * rows) * (rows * n_ctx) * 128 * 2
    attended, attended32, log_mass = call(
        functools.partial(attend_kernel, relative, scale),
        [scal, begin_row, qpad, *kv_all],
        [shape((rows, 256), bf16), shape((rows, 256), f32), shape((2, 2 * rows), f32)],
        [pltpu.VMEM((2, 128, 2 * rows), f32), pltpu.VMEM((2, 2 * rows), f32)],
        flops=attend_flops,
    )
    o_parts = [attended] + [swap(attended, "tp", k) for k in others]
    h_two, h_two_p, mixed_own = call(
        functools.partial(mix_kernel, n_tp, n_ctx, relative),
        [scal, hidden_in, gain_two, w_out, w_mine, w_pair, *o_parts],
        [shape((rows, width), bf16), shape((rows, width), bf16), shape((own, width), f32)],
        [pltpu.VMEM((rows, width), f32)],
        flops=2 * rows * width * width,
    )
    h_one_p, out_grad_p = call(
        functools.partial(order_kernel, n_ctx, relative),
        [scal, h_one, out_grad],
        [shape((rows, width), bf16)] * 2,
    )

    cut = 384 if hidden_units % 384 == 0 else 128
    whole = lambda *dims: pl.BlockSpec(dims, lambda i: (0,) * len(dims))
    down = pl.BlockSpec((width, cut), lambda i: (0, i))
    part = pl.BlockSpec((rows, cut), lambda i: (0, i))
    act, gate_grad, up_grad, two_parts = call(
        functools.partial(feed_kernel, n_tp),
        [scal, h_two, out_grad, w_gate, w_up, w_down],
        [shape((rows, hidden_units), bf16)] * 3 + [shape((n_tp, own, width), bf16)],
        [pltpu.VMEM((rows, width), f32)],
        flops=2 * rows * width * hidden_units * 5,
        grid=(hidden_units // cut,),
        in_specs=[
            SMEM,
            whole(rows, width),
            whole(rows, width),
            down,
            down,
            pl.BlockSpec((cut, width), lambda i: (i, 0)),
        ],
        out_specs=[part, part, part, whole(n_tp, own, width)],
    )
    two_got = [two_parts[0]] + [swap(two_parts[k], "tp", k) for k in others]
    mixed_grad, attn_grad_p, gain_two_part, out_parts = call(
        functools.partial(mid_kernel, n_tp, n_ctx, relative),
        [scal, out_grad, mixed_own, gain_two, w_out, w_mine, w_pair, *two_got],
        [
            shape((own, width), f32),
            shape((own, width), bf16),
            shape((1, width), f32),
            shape((n_tp, own, 256), bf16),
        ],
        [pltpu.VMEM((own, width), bf16)],
        flops=2 * own * width * width,
    )
    dout = [out_parts[0]] + [swap(out_parts[k], "tp", k) for k in others]

    got = call(
        functools.partial(attend_back_kernel, relative, scale, n_tp),
        [scal, begin_row, qpad, attended32, log_mass, *kv_all, *dout],
        [shape((rows, 256), bf16)] + [shape(x.shape, bf16) for x in kv_all],
        [
            pltpu.VMEM((rows, 256), f32),
            pltpu.VMEM((4 * rows, 128), bf16),
            pltpu.VMEM((2, 128, 2 * rows), f32),
        ],
        flops=attend_flops * 5 // 2,
    )
    query_low, dkv = got[0], got[1:]
    if relative:
        chip = dkv[0] + swap(dkv[1], "ctx", 1)
        pieces = [chip[i * rows : (i + 1) * rows] for i in range(n_ctx // 2)]
        kv_parts = [pieces[0]] + [swap(pieces[i], "ctx", 2 * i) for i in range(1, n_ctx // 2)]
    else:
        kv_parts = [lax.psum_scatter(dkv[0], "ctx", scatter_dimension=0, tiled=True)]
    query_pre_low, q_gain_part, one_query = call(
        q_back_kernel,
        [query_low, query_pre, cosine, sine, q_gain, w_query],
        [shape((rows, 256), bf16), shape((1, 128), f32), shape((rows, width), f32)],
        flops=2 * rows * width * 256,
    )
    kv_pre_low, k_gain_part, gain_one_part, one_parts = call(
        functools.partial(k_back_kernel, n_tp, len(kv_parts)),
        [scal, *kv_parts, key_pre, cosine, sine, k_gain, w_key, w_value, one_query, hidden_in],
        [
            shape((rows, 256), bf16),
            shape((1, 128), f32),
            shape((1, width), f32),
            shape((n_tp, own, width), bf16),
        ],
        [pltpu.VMEM((rows, width), f32)],
        flops=2 * rows * width * 256,
    )
    one_got = [one_parts[0]] + [swap(one_parts[k], "tp", k) for k in others]
    input_own = call(
        functools.partial(last_kernel, n_tp),
        [scal, hidden_in, mixed_grad, gain_one, *one_got],
        [shape((own, width), bf16)],
    )[0]
    input_parts = [input_own] + [swap(input_own, "tp", k) for k in others]
    input_grad = call(
        functools.partial(join_kernel, n_tp), [scal, *input_parts], [shape((rows, width), f32)]
    )[0]

    feed = dot(act, w_down).astype(bf16)
    feed_parts = [
        lax.dynamic_slice_in_dim(feed, jnp.bitwise_xor(place, k) * own, own, 0) for k in range(n_tp)
    ]
    feed_got = [feed_parts[0]] + [swap(feed_parts[k], "tp", k) for k in others]
    layer_own = (mixed_own + sum(x.astype(f32) for x in feed_got)).astype(bf16)
    layer_parts = [layer_own] + [swap(layer_own, "tp", k) for k in others]
    layer_out = call(
        functools.partial(join_kernel, n_tp), [scal, *layer_parts], [shape((rows, width), bf16)]
    )[0]

    def ctx_sum(grad):
        if not relative:
            return lax.psum_scatter(grad, "ctx", scatter_dimension=0, tiled=True).astype(f32)
        block = grad.shape[0] // n_ctx
        chip = grad[: width // 2] + swap(grad[width // 2 :], "ctx", 1)
        total = chip[:block].astype(f32)
        for i in range(1, n_ctx // 2):
            total += swap(chip[i * block : (i + 1) * block], "ctx", 2 * i).astype(f32)
        return total

    attn_grad_all = jnp.concatenate(
        [attn_grad_p] + [swap(attn_grad_p, "tp", k) for k in others], axis=0
    )
    attended_rel = jnp.concatenate(
        [
            lax.dynamic_slice_in_dim(attended, jnp.bitwise_xor(place, k) * own, own, 0)
            for k in range(n_tp)
        ],
        axis=0,
    )
    down_w = ctx_sum(dot(out_grad_p, act, TN).astype(bf16)).T
    gate_w = ctx_sum(dot(h_two_p, gate_grad, TN).astype(bf16))
    up_w = ctx_sum(dot(h_two_p, up_grad, TN).astype(bf16))
    out_w = ctx_sum(dot(attn_grad_all, attended_rel, TN).astype(bf16)).T
    query_w = ctx_sum(dot(h_one_p, query_pre_low, TN).astype(bf16))
    key_value_w = ctx_sum(dot(h_one_p, kv_pre_low, TN).astype(bf16))

    gains = jnp.concatenate(
        [
            gain_one_part.reshape(-1, 128),
            gain_two_part.reshape(-1, 128),
            jnp.concatenate([q_gain_part[:, :64], k_gain_part[:, :64]], axis=1),
        ],
        axis=0,
    )
    for axis, size in (("ctx", n_ctx), ("tp", n_tp)):
        k = 1
        while k < size:
            gains = gains + swap(gains, axis, k)
            k *= 2
    lots = width // 128
    block = width // n_ctx
    gain_one_sum = lax.dynamic_slice_in_dim(gains[:lots].reshape(width), mine * block, block, 0)
    gain_two_sum = lax.dynamic_slice_in_dim(
        gains[lots : 2 * lots].reshape(width), mine * block, block, 0
    )
    return (
        layer_out,
        input_grad,
        gain_one_sum,
        query_w,
        key_value_w[:, :128],
        key_value_w[:, 128:],
        gains[2 * lots, :64],
        gains[2 * lots, 64:],
        out_w,
        gain_two_sum,
        gate_w,
        up_w,
        down_w,
    )


def solution(mesh):
    in_specs = (
        P("ctx", None),
        P(),
        P(),
        P(None, "tp"),
        P(None, "tp"),
        P(None, "tp"),
        P(),
        P(),
        P("tp", None),
        P(),
        P(None, "tp"),
        P(None, "tp"),
        P("tp", None),
        P("ctx", None),
    )
    out_specs = (
        P("ctx", None),
        P("ctx", None),
        P("ctx"),
        P("ctx", "tp"),
        P("ctx", "tp"),
        P("ctx", "tp"),
        P(),
        P(),
        P("tp", "ctx"),
        P("ctx"),
        P("ctx", "tp"),
        P("ctx", "tp"),
        P("tp", "ctx"),
    )
    return jax.shard_map(shards, mesh=mesh, in_specs=in_specs, out_specs=out_specs, check_vma=False)
```

```python
import functools
import math

import jax
import jax.numpy as jnp
from jax import lax
from jax.experimental import pallas as pl
from jax.experimental.pallas import tpu as pltpu
from jax.sharding import PartitionSpec as P

norm_eps = 1e-05
rope_base = 1000000.0
f32 = jnp.float32
bf16 = jnp.bfloat16
NN = (((1,), (0,)), ((), ()))
NT = (((1,), (1,)), ((), ()))
TN = (((0,), (0,)), ((), ()))
VMEM = pl.BlockSpec(memory_space=pltpu.VMEM)
SMEM = pl.BlockSpec(memory_space=pltpu.SMEM)
vmem_limit = 56 * 1024 * 1024
work = 5 * 10**10


def dot(left, right, dims=NN):
    return lax.dot_general(left, right, dims, preferred_element_type=f32)


def call(body, inputs, outs, scratch=(), work=work, **kwargs):
    in_specs = kwargs.pop("in_specs", None)
    if in_specs is None:
        in_specs = [
            SMEM if (x.dtype == jnp.int32 and x.ndim == 1) else VMEM for x in inputs
        ]
    out_specs = kwargs.pop("out_specs", [VMEM] * len(outs))
    moved = sum(x.size * x.dtype.itemsize for x in inputs) + sum(
        math.prod(o.shape) * o.dtype.itemsize for o in outs
    )
    return pl.pallas_call(
        body,
        out_shape=outs,
        in_specs=in_specs,
        out_specs=out_specs,
        scratch_shapes=list(scratch),
        compiler_params=pltpu.CompilerParams(vmem_limit_bytes=vmem_limit),
        cost_estimate=pl.CostEstimate(flops=work, bytes_accessed=moved, transcendentals=0),
        **kwargs,
    )(*inputs)


def shape(dims, dtype):
    return jax.ShapeDtypeStruct(dims, dtype)


def lanes(x):
    return lax.broadcasted_iota(jnp.int32, x.shape, 1)


def head_mean(x):
    first = lanes(x) < 64
    low = jnp.sum(jnp.where(first, x, 0.0), axis=1, keepdims=True)
    high = jnp.sum(jnp.where(first, 0.0, x), axis=1, keepdims=True)
    return jnp.where(first, low, high) * (1.0 / 64.0)


def swap_halves(x):
    return jnp.where(lanes(x) % 64 < 32, pltpu.roll(x, 96, 1), pltpu.roll(x, 32, 1))


def head_norm(pre, gain):
    inverse = lax.rsqrt(head_mean(pre * pre) + norm_eps)
    return pre * inverse * gain


def head_norm_back(pre, gain, grads):
    inverse = lax.rsqrt(head_mean(pre * pre) + norm_eps)
    normed = pre * inverse
    scaled = grads * gain
    inner = head_mean(scaled * normed)
    return inverse * (scaled - normed * inner), grads * normed


def doc_begin(positions, starts_ref):
    begin = jnp.zeros_like(positions)
    for i in range(starts_ref.shape[0]):
        begin = jnp.where(starts_ref[i] <= positions, starts_ref[i], begin)
    return begin


def twice(gain_ref):
    return jnp.concatenate([gain_ref[...], gain_ref[...]], axis=1)


def quarter(partner, size):
    place = jnp.bitwise_xor(lax.axis_index("tp"), partner)
    return pl.ds(pl.multiple_of(place * size, size), size)


def row_norm(x):
    return lax.rsqrt(jnp.mean(x * x, axis=1, keepdims=True) + norm_eps)


def kv_kernel(
    starts_ref, x_ref, gain_ref, wk_ref, wv_ref, freq_ref, kgain_ref, h_ref, kv_ref, kpre_ref, cos_ref, sin_ref
):
    rows = x_ref.shape[0]
    positions = lax.axis_index("ctx") * rows + lax.broadcasted_iota(jnp.int32, (rows, 128), 0)
    angles = (positions - doc_begin(positions, starts_ref)).astype(f32) * freq_ref[...]
    cosine, sine = jnp.cos(angles), jnp.sin(angles)
    sine = jnp.where(lanes(sine) % 64 < 32, -sine, sine)
    cos_ref[...] = cosine
    sin_ref[...] = sine
    x = x_ref[...].astype(f32)
    h = (x * row_norm(x) * gain_ref[...]).astype(bf16)
    h_ref[...] = h
    kpre = dot(h, wk_ref[...])
    kpre_ref[...] = kpre
    kn = head_norm(kpre, twice(kgain_ref))
    key = kn * cosine + swap_halves(kn) * sine
    kv_ref[:, :128] = key.astype(bf16)
    kv_ref[:, 128:] = dot(h, wv_ref[...]).astype(bf16)


def spread(x, half, out_ref, base, rows):
    rolled = pltpu.roll(x, 64, 1)
    keep = (lanes(x) < 64) if half == 0 else (lanes(x) >= 64)
    first, second = (x, rolled) if half == 0 else (rolled, x)
    out_ref[pl.ds(base, rows), :] = jnp.where(keep, first, 0.0).astype(bf16)
    out_ref[pl.ds(base + rows, rows), :] = jnp.where(keep, second, 0.0).astype(bf16)


def q_kernel(h_ref, wq_ref, cos_ref, sin_ref, qgain_ref, qpad_ref, qpre_ref):
    rows = h_ref.shape[0]
    qpre = dot(h_ref[...], wq_ref[...])
    qpre_ref[...] = qpre
    for half in range(2):
        qn = head_norm(qpre[:, 128 * half : 128 * half + 128], twice(qgain_ref))
        x = qn * cos_ref[...] + swap_halves(qn) * sin_ref[...]
        spread(x, half, qpad_ref, 2 * half * rows, rows)


def visit_blocks(near, rows, starts_ref, count, lists, visit, skip=None):
    mine = lax.axis_index("ctx")
    first, last = mine * rows, mine * rows + rows - 1
    first_begin, last_begin = doc_begin(first, starts_ref), doc_begin(last, starts_ref)
    for which in range(lists):

        def step(index, carry, which=which):
            block = jnp.bitwise_xor(mine, 2 * index + which) if near else index
            start = block * rows
            seen = (block <= mine) & (start + rows - 1 >= first_begin)
            whole = (block < mine) & (start >= last_begin)

            def mask():
                dims = (rows, 2 * rows)
                key_pos = lax.broadcasted_iota(jnp.int32, dims, 0) + start
                across = lax.broadcasted_iota(jnp.int32, (1, 2 * rows), 1)
                query_pos = first + jnp.where(across < rows, across, across - rows)
                return (key_pos <= query_pos) & (key_pos >= doc_begin(query_pos, starts_ref))

            pl.when(seen & whole)(lambda: visit(which, index, None))
            pl.when(seen & jnp.logical_not(whole))(lambda: visit(which, index, mask))
            if skip is not None:
                pl.when(jnp.logical_not(seen))(lambda: skip(which, index))
            return carry

        lax.fori_loop(0, count, step, 0)


def attend_kernel(near, scale, starts_ref, qpad_ref, *refs):
    lists = 2 if near else 1
    kv_refs = refs[:lists]
    o_ref, o32_ref, lse_ref, acc_ref, mass_ref = refs[lists:]
    rows = o_ref.shape[0]
    acc_ref[...] = jnp.zeros_like(acc_ref)
    mass_ref[...] = jnp.zeros_like(mass_ref)
    factor = scale * math.log2(math.e)

    def visit(which, index, mask):
        at = pl.ds(pl.multiple_of(index * rows, rows), rows)
        keys = kv_refs[which][at, :128]
        values_t = kv_refs[which][at, 128:].T
        for j in range(2):
            p = jnp.exp2(dot(keys, qpad_ref[2 * rows * j : 2 * rows * (j + 1), :], NT) * factor)
            if mask is not None:
                p = jnp.where(mask(), p, 0.0)
            mass_ref[j : j + 1, :] += jnp.sum(p, axis=0, keepdims=True)
            acc_ref[j] += dot(values_t, p.astype(bf16))

    visit_blocks(near, rows, starts_ref, kv_refs[0].shape[0] // rows, lists, visit)
    mass = mass_ref[...]
    lse_ref[...] = jnp.log2(mass)
    parts = []
    for j in range(2):
        normed = acc_ref[j, 64 * j : 64 * j + 64, :] / mass[j : j + 1, :]
        parts += [normed[:, :rows], normed[:, rows:]]
    o32 = jnp.concatenate(parts, axis=0).T
    o32_ref[...] = o32
    o_ref[...] = o32.astype(bf16)


def attend_back_kernel(near, scale, n_tp, starts_ref, qpad_ref, o32_ref, lse_ref, *refs):
    lists = 2 if near else 1
    kv_refs, refs = refs[:lists], refs[lists:]
    dout_refs, refs = refs[:n_tp], refs[n_tp:]
    dq_ref, refs = refs[0], refs[1:]
    dkv_refs, refs = refs[:lists], refs[lists:]
    dout_ref, dopad_ref, dqt_ref = refs
    rows = dq_ref.shape[0]
    factor = scale * math.log2(math.e)
    for k in range(n_tp):
        dout_ref[quarter(k, rows // n_tp), :] = dout_refs[k][...].astype(f32)
    dout = dout_ref[...]
    for half in range(2):
        spread(dout[:, 128 * half : 128 * half + 128], half, dopad_ref, 2 * half * rows, rows)
    weighted = (dout * o32_ref[...]).T
    deltas = [jnp.sum(weighted[64 * h : 64 * h + 64], axis=0, keepdims=True) for h in range(4)]
    delta = [jnp.concatenate(deltas[2 * j : 2 * j + 2], axis=1) for j in range(2)]
    dqt_ref[...] = jnp.zeros_like(dqt_ref)

    def visit(which, index, mask):
        at = pl.ds(pl.multiple_of(index * rows, rows), rows)
        keys = kv_refs[which][at, :128]
        values = kv_refs[which][at, 128:]
        keys_t = keys.T
        dk = jnp.zeros((rows, 128), f32)
        dv = jnp.zeros((rows, 128), f32)
        for j in range(2):
            qpad = qpad_ref[2 * rows * j : 2 * rows * (j + 1), :]
            dopad = dopad_ref[2 * rows * j : 2 * rows * (j + 1), :]
            p = jnp.exp2(dot(keys, qpad, NT) * factor - lse_ref[j : j + 1, :])
            if mask is not None:
                p = jnp.where(mask(), p, 0.0)
            ds = (p * (dot(values, dopad, NT) - delta[j])).astype(bf16)
            dv += dot(p.astype(bf16), dopad)
            dk += dot(ds, qpad)
            dqt_ref[j] += dot(keys_t, ds)
        dkv_refs[which][at, :128] = (dk * scale).astype(bf16)
        dkv_refs[which][at, 128:] = dv.astype(bf16)

    def skip(which, index):
        at = pl.ds(pl.multiple_of(index * rows, rows), rows)
        dkv_refs[which][at, :] = jnp.zeros((rows, 256), bf16)

    visit_blocks(near, rows, starts_ref, kv_refs[0].shape[0] // rows, lists, visit, skip)
    parts = []
    for j in range(2):
        part = dqt_ref[j, 64 * j : 64 * j + 64, :]
        parts += [part[:, :rows], part[:, rows:]]
    dq_ref[...] = (jnp.concatenate(parts, axis=0).T * scale).astype(bf16)


def core_halves(size):
    core = lax.axis_index("ctx") % 2
    return (
        pl.ds(pl.multiple_of(core * size, size), size),
        pl.ds(pl.multiple_of((1 - core) * size, size), size),
    )


def mix_kernel(n_tp, x_ref, gain_ref, w0_ref, *refs):
    wm_refs, wp_refs, o_refs = refs[: n_tp - 1], refs[n_tp - 1 : 2 * n_tp - 2], refs[2 * n_tp - 2 : 3 * n_tp - 2]
    h_ref, y_ref, acc_ref = refs[3 * n_tp - 2 :]
    acc = x_ref[...].astype(f32) + dot(o_refs[0][...], w0_ref[...])
    first, second = core_halves(w0_ref.shape[0] // 2)
    for k in range(1, n_tp):
        acc += dot(o_refs[k][:, first], wm_refs[k - 1][...])
        acc += dot(o_refs[k][:, second], wp_refs[k - 1][...])
    acc_ref[...] = acc
    y_ref[...] = acc_ref[quarter(0, y_ref.shape[0]), :]
    h_ref[...] = (acc * row_norm(acc) * gain_ref[...]).astype(bf16)


def feed_kernel(n_tp, h_ref, g_ref, wg_ref, wu_ref, wd_ref, act_ref, dg_ref, du_ref, *refs):
    dh_refs, acc_ref = refs[:n_tp], refs[n_tp]
    step = pl.program_id(0)
    gate = dot(h_ref[...], wg_ref[...])
    up = dot(h_ref[...], wu_ref[...])
    dact = dot(g_ref[...], wd_ref[...], NT)
    sigma = jax.nn.sigmoid(gate)
    silu = gate * sigma
    act_ref[...] = (silu * up).astype(bf16)
    dgate = (dact * up * sigma * (1.0 + gate * (1.0 - sigma))).astype(bf16)
    dup = (dact * silu).astype(bf16)
    dg_ref[...] = dgate
    du_ref[...] = dup
    total = dot(dgate, wg_ref[...], NT) + dot(dup, wu_ref[...], NT)

    @pl.when(step == 0)
    def _():
        acc_ref[...] = total

    @pl.when(step > 0)
    def _():
        acc_ref[...] += total

    @pl.when(step == pl.num_programs(0) - 1)
    def _():
        for k in range(n_tp):
            dh_refs[k][...] = acc_ref[quarter(k, dh_refs[k].shape[0]), :].astype(bf16)


def mid_kernel(n_tp, g_ref, y_ref, gain_ref, w0_ref, *refs):
    wm_refs, wp_refs, refs = refs[: n_tp - 1], refs[n_tp - 1 : 2 * n_tp - 2], refs[2 * n_tp - 2 :]
    dh_refs, refs = refs[:n_tp], refs[n_tp:]
    dy_ref, dattn_ref, gaing_ref = refs[:3]
    dout_refs = refs[3:]
    dh = dh_refs[0][...].astype(f32)
    for k in range(1, n_tp):
        dh += dh_refs[k][...].astype(f32)
    y = y_ref[...]
    inverse = row_norm(y)
    z = y * inverse
    gaing_ref[...] = jnp.sum(dh * z, axis=0, keepdims=True)
    e = dh * gain_ref[...]
    inner = jnp.mean(e * z, axis=1, keepdims=True)
    dy = g_ref[quarter(0, y_ref.shape[0]), :].astype(f32) + inverse * (e - z * inner)
    dy_ref[...] = dy
    low = dy.astype(bf16)
    dattn_ref[...] = low
    dout_refs[0][...] = dot(low, w0_ref[...], NT).astype(bf16)
    first, second = core_halves(w0_ref.shape[0] // 2)
    for k in range(1, n_tp):
        dout_refs[k][:, first] = dot(low, wm_refs[k - 1][...], NT).astype(bf16)
        dout_refs[k][:, second] = dot(low, wp_refs[k - 1][...], NT).astype(bf16)


def down_kernel(n_tp, act_ref, wd_ref, dattn_ref, *refs):
    out_refs, acc_ref = refs[:n_tp], refs[n_tp]
    own, width = dattn_ref.shape
    acc_ref[...] = dot(act_ref[...], wd_ref[...])
    for k in range(n_tp):
        out_refs[k][:, :width] = acc_ref[quarter(k, own), :].astype(bf16)
        out_refs[k][:, width:] = dattn_ref[:, quarter(k, width // n_tp)]


def layer_kernel(n_tp, y_ref, *refs):
    own, width = y_ref.shape
    out_ref, cut_ref = refs[n_tp:]
    total = y_ref[...]
    for k in range(n_tp):
        total += refs[k][:, :width].astype(f32)
        cut_ref[quarter(k, own), :] = refs[k][:, width:]
    out_ref[...] = total.astype(bf16)


def q_back_kernel(near, n_tp, dq_ref, qpre_ref, cos_ref, sin_ref, qgain_ref, wq_ref, h_ref, *refs):
    if near:
        dattn_ref, o_refs, refs = refs[0], refs[1 : 1 + n_tp], refs[1 + n_tp :]
        odd_ref, even_ref, hp_ref, oall_ref = refs[3:]
    low_ref, gaing_ref, dh_ref = refs[:3]
    total = jnp.zeros((1, 128), f32)
    for half in range(2):
        cut = slice(128 * half, 128 * half + 128)
        x = dq_ref[:, cut].astype(f32)
        dqn = x * cos_ref[...] - swap_halves(x) * sin_ref[...]
        dpre, weighted = head_norm_back(qpre_ref[:, cut], twice(qgain_ref), dqn)
        low_ref[:, cut] = dpre.astype(bf16)
        total += jnp.sum(weighted, axis=0, keepdims=True)
    gaing_ref[...] = total + pltpu.roll(total, 64, 1)
    dh_ref[...] = dot(low_ref[...], wq_ref[...], NT)
    if near:
        mine, place = lax.axis_index("ctx"), lax.axis_index("tp")
        for k in range(n_tp):
            oall_ref[k] = o_refs[k][...]
        for parity, out_ref in ((1, odd_ref), (0, even_ref)):
            gather_columns(parity, h_ref, hp_ref)
            out_ref[:, :256] = dot(hp_ref[...], low_ref[...], TN).astype(bf16)
            left = columns(dattn_ref, jnp.bitwise_xor(mine % 2, parity)).T
            for at, chip in enumerate(block_order(parity)):
                heads = jnp.bitwise_xor(jnp.bitwise_xor(mine // 2, chip), place)
                out_ref[128 * at : 128 * at + 128, 256:] = dot(left, oall_ref[heads]).astype(bf16)


def k_back_kernel(near, n_tp, n_parts, *refs):
    parts, refs = refs[:n_parts], refs[n_parts:]
    kpre_ref, cos_ref, sin_ref, kgain_ref, wk_ref, wv_ref, dhq_ref, x_ref, gain2_ref, qg_ref, h_ref = refs[:11]
    low_ref, gains_ref = refs[11:13]
    dh_refs, refs = refs[13 : 13 + n_tp], refs[13 + n_tp :]
    acc_ref = refs[-1]
    total = parts[0][...].astype(f32)
    for part in parts[1:]:
        total += part[...].astype(f32)
    low = total.astype(bf16)
    x = low[:, :128].astype(f32)
    dkn = x * cos_ref[...] - swap_halves(x) * sin_ref[...]
    dpre, weighted = head_norm_back(kpre_ref[...], twice(kgain_ref), dkn)
    dk = dpre.astype(bf16)
    dv = low[:, 128:]
    low_ref[:, :128] = dk
    low_ref[:, 128:] = dv
    dh = dhq_ref[...] + dot(dk, wk_ref[...], NT) + dot(dv, wv_ref[...], NT)
    acc_ref[...] = dh
    for k in range(n_tp):
        dh_refs[k][...] = acc_ref[quarter(k, dh_refs[k].shape[0]), :].astype(bf16)
    x_in = x_ref[...].astype(f32)
    width = x_in.shape[1]
    lots = width // 128
    gain_one = jnp.sum(dh * (x_in * row_norm(x_in)), axis=0, keepdims=True)
    for i in range(lots):
        gains_ref[i : i + 1, :] = gain_one[:, 128 * i : 128 * i + 128]
        gains_ref[lots + i : lots + i + 1, :] = gain2_ref[:, 128 * i : 128 * i + 128]
    gains = jnp.sum(weighted, axis=0, keepdims=True)
    gains_ref[2 * lots : 2 * lots + 1, :] = qg_ref[...]
    gains_ref[2 * lots + 1 : 2 * lots + 2, :] = gains + pltpu.roll(gains, 64, 1)
    gains_ref[2 * lots + 2 :, :] = jnp.zeros((gains_ref.shape[0] - 2 * lots - 2, 128), f32)
    if near:
        odd_ref, even_ref, hp_ref = refs[:3]
        mine = lax.axis_index("ctx")
        for parity, out_ref in ((1, odd_ref), (0, even_ref)):
            gather_columns(parity, h_ref, hp_ref)
            out_ref[:, :256] = dot(hp_ref[...], low_ref[...], TN).astype(bf16)
            for at, chip in enumerate(block_order(parity)):
                block = jnp.bitwise_xor(mine, 2 * chip + parity)
                out_ref[128 * at : 128 * at + 128, 256:] = parted(gain_columns(gains_ref, block, lots))


def last_kernel(n_tp, x_ref, dy_ref, gain_ref, *refs):
    dh_refs, out_ref = refs[:n_tp], refs[n_tp]
    dh = dh_refs[0][...].astype(f32)
    for k in range(1, n_tp):
        dh += dh_refs[k][...].astype(f32)
    x = x_ref[quarter(0, dy_ref.shape[0]), :].astype(f32)
    inverse = row_norm(x)
    z = x * inverse
    e = dh * gain_ref[...]
    inner = jnp.mean(e * z, axis=1, keepdims=True)
    out_ref[...] = (dy_ref[...] + inverse * (e - z * inner)).astype(bf16)


def join_kernel(n_tp, *refs):
    out_ref = refs[n_tp]
    for k in range(n_tp):
        out_ref[quarter(k, refs[k].shape[0]), :] = refs[k][...].astype(out_ref.dtype)


def block_order(parity):
    core = lax.axis_index("ctx") % 2
    first, second = 1 + core, 2 - core
    return (0, first, second, 3) if parity else (0, second, first, 3)


def columns(src_ref, block):
    return src_ref[:, pl.ds(pl.multiple_of(block * 128, 128), 128)]


def gather_columns(parity, src_ref, dst_ref):
    mine = lax.axis_index("ctx")
    for place, chip in enumerate(block_order(parity)):
        dst_ref[:, 128 * place : 128 * place + 128] = columns(src_ref, jnp.bitwise_xor(mine, 2 * chip + parity))


def feed_grad_kernel(h_ref, g_ref, act_ref, dg_ref, du_ref, odd_ref, even_ref, hp_ref, gp_ref):
    units = act_ref.shape[1]
    for parity, out_ref in ((1, odd_ref), (0, even_ref)):
        gather_columns(parity, h_ref, hp_ref)
        gather_columns(parity, g_ref, gp_ref)
        for i, (left_ref, right_ref) in enumerate(((hp_ref, dg_ref), (hp_ref, du_ref), (gp_ref, act_ref))):
            out_ref[:, units * i : units * (i + 1)] = dot(left_ref[...], right_ref[...], TN).astype(bf16)


def feed_grad_sum_kernel(keep_ref, got_ref, gate_ref, up_ref, down_ref):
    units = gate_ref.shape[1]
    for i, out_ref in enumerate((gate_ref, up_ref, down_ref)):
        cut = slice(units * i, units * (i + 1))
        total = keep_ref[:, cut].astype(f32) + got_ref[:, cut].astype(f32)
        out_ref[...] = total.T if i == 2 else total


def joined(x):
    x = x.astype(f32)
    return x + pltpu.roll(x, 64, 1)


def parted(x):
    high = x.astype(bf16).astype(f32)
    return jnp.where(lanes(x) < 64, high, x - high).astype(bf16)


def gain_columns(gains_ref, block, lots):
    row = lambda i: gains_ref[pl.ds(i, 1), :]
    heads = jnp.where(lanes(row(0)) < 64, row(2 * lots), row(2 * lots + 1))
    rows = jnp.concatenate([row(block), row(lots + block), heads, jnp.zeros((125, 128), f32)], axis=0)
    total = rows.T
    return total + pltpu.roll(total, 64, 1)


def attn_grad_chip_kernel(q_ref, q_got_ref, kv_ref, kv_got_ref, here_ref, send_ref):
    half = here_ref.shape[0]
    for i, out_ref in enumerate((here_ref, send_ref)):
        row = slice(half * i, half * (i + 1))
        out_ref[:, :512] = (q_ref[row, :].astype(f32) + q_got_ref[row, :].astype(f32)).astype(bf16)
        out_ref[:, 512:768] = (kv_ref[row, :256].astype(f32) + kv_got_ref[row, :256].astype(f32)).astype(bf16)
        out_ref[:, 768:] = parted(joined(kv_ref[row, 256:]) + joined(kv_got_ref[row, 256:]))


def attn_grad_pass_kernel(keep_ref, got_ref, here_ref, send_ref):
    half = here_ref.shape[0]
    for i, out_ref in enumerate((here_ref, send_ref)):
        row = slice(half * i, half * (i + 1))
        out_ref[:, :768] = (keep_ref[row, :768].astype(f32) + got_ref[row, :768].astype(f32)).astype(bf16)
        out_ref[:, 768:] = parted(joined(keep_ref[row, 768:]) + joined(got_ref[row, 768:]))


def attn_grad_sum_kernel(keep_ref, got_ref, q_ref, k_ref, v_ref, o_ref, gains_ref):
    total = keep_ref[:, :768].astype(f32) + got_ref[:, :768].astype(f32)
    q_ref[...] = total[:, :256]
    o_ref[...] = total[:, 256:512].T.astype(bf16)
    k_ref[...] = total[:, 512:640]
    v_ref[...] = total[:, 640:]
    gains_ref[...] = (joined(keep_ref[:, 768:]) + joined(got_ref[:, 768:])).T[:8]


def gain_kernel(block, a_ref, b_ref, w_ref, one_ref, two_ref, q_ref, k_ref, out_ref):
    out_ref[...] = w_ref[...].astype(f32)
    total = a_ref[...] + b_ref[...]
    one_ref[...] = total[0:1, :block]
    two_ref[...] = total[1:2, :block]
    q_ref[...] = total[2:3, :64]
    k_ref[...] = total[2:3, 64:]


def swap(x, axis, k):
    size = lax.axis_size(axis)
    return lax.ppermute(x, axis, [(i, i ^ k) for i in range(size)])


def swap_across(x, step):
    size = lax.axis_size("ctx")
    return lax.ppermute(x, "ctx", [(i, i ^ (2 << ((i + step) % 2))) for i in range(size)])


def after(x, *first):
    return lax.optimization_barrier((x, *first))[0]


def shards(
    hidden_in,
    doc_starts,
    norm1_gain,
    w_query,
    w_key,
    w_value,
    query_gain,
    key_gain,
    w_out,
    norm2_gain,
    w_gate,
    w_up,
    w_down,
    out_grad,
):
    rows, width = hidden_in.shape
    n_ctx, n_tp = lax.axis_size("ctx"), lax.axis_size("tp")
    head_dim = query_gain.shape[0]
    scale = head_dim ** (-0.5)
    near = n_ctx == 2 * n_tp and width == 128 * n_ctx
    own = rows // n_tp
    units = w_gate.shape[1]
    others = range(1, n_tp)
    chips = range(1, n_ctx // 2)
    mine, place = lax.axis_index("ctx"), lax.axis_index("tp")
    gain_one, gain_two = norm1_gain[None, :], norm2_gain[None, :]
    q_gain, k_gain = query_gain[None, :], key_gain[None, :]
    frequency = rope_base ** (-2.0 * jnp.arange(head_dim // 2, dtype=f32) / head_dim)
    frequency = jnp.concatenate([frequency] * 4)[None, :]

    def exchange(parts):
        return [parts[0]] + [swap(parts[k], "tp", k) for k in others]

    h_one, kv, key_pre, cosine, sine = call(
        kv_kernel,
        [doc_starts, hidden_in, gain_one, w_key, w_value, frequency, k_gain],
        [
            shape((rows, width), bf16),
            shape((rows, 256), bf16),
            shape((rows, 128), f32),
            shape((rows, 128), f32),
            shape((rows, 128), f32),
        ],
    )
    if near:
        kv_got = [swap(kv, "ctx", 2 * i) for i in chips]
    else:
        kv_all = [lax.all_gather(kv, "ctx", axis=0, tiled=True)]
    half = w_out.shape[0] // 2
    w_half = lax.dynamic_slice_in_dim(w_out, (mine % 2) * half, half, 0)
    w_two = swap(w_half, "tp", 2)
    qpad, query_pre = call(
        q_kernel,
        [h_one, w_query, cosine, sine, q_gain],
        [shape((4 * rows, 128), bf16), shape((rows, 256), f32)],
        work=1,
    )
    w_rest = swap(jnp.stack([w_half, w_two]), "tp", 1)
    if near:
        even = jnp.concatenate([after(kv, qpad, w_two), *kv_got], axis=0)
        kv_all = [even, swap(even, "ctx", 1)]
    attended, attended32, log_mass = call(
        functools.partial(attend_kernel, near, scale),
        [doc_starts, qpad, *kv_all],
        [shape((rows, 256), bf16), shape((rows, 256), f32), shape((2, 2 * rows), f32)],
        [pltpu.VMEM((2, 128, 2 * rows), f32), pltpu.VMEM((2, 2 * rows), f32)],
    )
    o_parts = exchange([attended] * n_tp)
    w_two, w_rest = lax.optimization_barrier((w_two, w_rest, attended))[:2]
    w_two_pair, w_rest_pair = swap(w_two, "ctx", 1), swap(w_rest, "ctx", 1)
    w_all = [w_rest[0], w_two, w_rest[1], w_rest_pair[0], w_two_pair, w_rest_pair[1]]
    h_two, mixed_own = call(
        functools.partial(mix_kernel, n_tp),
        [hidden_in, gain_two, w_out, *w_all, *o_parts],
        [shape((rows, width), bf16), shape((own, width), f32)],
        [pltpu.VMEM((rows, width), f32)],
    )

    cut = 384 if units % 384 == 0 else 128
    whole = lambda *dims: pl.BlockSpec(dims, lambda i: (0,) * len(dims))
    across = pl.BlockSpec((width, cut), lambda i: (0, i))
    part = pl.BlockSpec((rows, cut), lambda i: (0, i))
    got = call(
        functools.partial(feed_kernel, n_tp),
        [h_two, out_grad, w_gate, w_up, w_down],
        [shape((rows, units), bf16)] * 3 + [shape((own, width), bf16)] * n_tp,
        [pltpu.VMEM((rows, width), f32)],
        grid=(units // cut,),
        in_specs=[
            whole(rows, width),
            whole(rows, width),
            across,
            across,
            pl.BlockSpec((cut, width), lambda i: (i, 0)),
        ],
        out_specs=[part, part, part] + [whole(own, width)] * n_tp,
    )
    act, gate_grad, up_grad = got[:3]
    two_got = exchange(got[3:])
    block = width // n_ctx
    if near:
        ordered = pltpu.VMEM((rows, 4 * block), bf16)
        feed_odd, feed_even = call(
            feed_grad_kernel,
            [h_two, out_grad, act, gate_grad, up_grad],
            [shape((4 * block, 3 * units), bf16)] * 2,
            [ordered, ordered],
        )
        mixed_own = after(mixed_own, feed_even)
    got = call(
        functools.partial(mid_kernel, n_tp),
        [out_grad, mixed_own, gain_two, w_out, *w_all, *two_got],
        [shape((own, width), f32), shape((own, width), bf16), shape((1, width), f32)]
        + [shape((own, 256), bf16)] * n_tp,
    )
    mixed_grad, attn_grad, gain_two_part = got[:3]
    dout = exchange(got[3:])

    down = call(
        functools.partial(down_kernel, n_tp),
        [act, w_down, attn_grad],
        [shape((own, width + width // n_tp), bf16)] * n_tp,
        [pltpu.VMEM((rows, width), f32)],
    )
    if near:
        half = 2 * block
        feed_other = swap(feed_odd, "ctx", 1)
        feed_send = feed_even[half:] + feed_other[half:]
        feed_got = swap_across(feed_send, 0)
        qpad = after(qpad, feed_send)
    down_got = exchange(list(lax.optimization_barrier((*down, *dout[1:]))[:n_tp]))

    got = call(
        functools.partial(attend_back_kernel, near, scale, n_tp),
        [doc_starts, qpad, attended32, log_mass, *kv_all, *dout],
        [shape((rows, 256), bf16)] + [shape(x.shape, bf16) for x in kv_all],
        [
            pltpu.VMEM((rows, 256), f32),
            pltpu.VMEM((4 * rows, 128), bf16),
            pltpu.VMEM((2, 128, 2 * rows), f32),
        ],
    )
    query_low, dkv = got[0], got[1:]
    if near:
        other = swap(dkv[1], "ctx", 1)
        pieces = [
            dkv[0][i * rows : (i + 1) * rows] + other[i * rows : (i + 1) * rows] for i in range(n_ctx // 2)
        ]
        kv_parts = [pieces[0]] + [swap(pieces[i], "ctx", 2 * i) for i in chips]
    else:
        kv_parts = [lax.psum_scatter(dkv[0], "ctx", scatter_dimension=0, tiled=True)]
    down_got = list(lax.optimization_barrier((*down_got, query_low))[:n_tp])
    layer_own, attn_grad_cut = call(
        functools.partial(layer_kernel, n_tp),
        [mixed_own, *down_got],
        [shape((own, width), bf16), shape((rows, width // n_tp), bf16)],
    )
    layer_two = swap(layer_own, "tp", 2)

    if near:
        feed_parts = lax.optimization_barrier((feed_even, feed_other, feed_got, query_low))[:3]
        feed_here = sum(x[:half].astype(f32) for x in feed_parts).astype(bf16)
        query_low = after(query_low, *pieces)
    more = [attn_grad_cut, *o_parts] if near else []
    got = call(
        functools.partial(q_back_kernel, near, n_tp),
        [query_low, query_pre, cosine, sine, q_gain, w_query, h_one, *more],
        [shape((rows, 256), bf16), shape((1, 128), f32), shape((rows, width), f32)]
        + ([shape((4 * block, 512), bf16)] * 2 if near else []),
        [ordered, pltpu.VMEM((n_tp, rows, 256), bf16)] if near else [],
    )
    query_pre_low, q_gain_part, one_query = got[:3]
    layer_pair = jnp.stack([layer_own, after(layer_two, one_query)])
    layer_rest = swap(layer_pair, "tp", 1)
    done = [layer_pair, feed_here] if near else [layer_pair]
    if near:
        q_odd, q_even = got[3:]
        q_other = swap(q_odd, "ctx", 1)
        done.append(q_other)
    lots = width // 128
    gain_rows = 2 * lots + 8
    got = call(
        functools.partial(k_back_kernel, near, n_tp, len(kv_parts)),
        [
            *kv_parts,
            after(key_pre, *done),
            cosine,
            sine,
            k_gain,
            w_key,
            w_value,
            one_query,
            hidden_in,
            gain_two_part,
            q_gain_part,
            h_one,
        ],
        [shape((rows, 256), bf16), shape((gain_rows, 128), f32)]
        + [shape((own, width), bf16)] * n_tp
        + ([shape((4 * block, 384), bf16)] * 2 if near else []),
        ([ordered] if near else []) + [pltpu.VMEM((rows, width), f32)],
    )
    kv_pre_low, gains = got[:2]
    one_parts = got[2 : 2 + n_tp]
    one_got = exchange(one_parts)
    if near:
        kv_odd, kv_even = got[2 + n_tp :]
        attn_here, attn_send = call(
            attn_grad_chip_kernel,
            [q_even, q_other, kv_even, swap(kv_odd, "ctx", 1)],
            [shape((2 * block, 896), bf16)] * 2,
        )
        attn_here, attn_send = call(
            attn_grad_pass_kernel,
            [attn_here, swap_across(attn_send, 0)],
            [shape((block, 896), bf16)] * 2,
            work=1,
        )
        mixed_grad = after(mixed_grad, attn_here)
    input_own = call(
        functools.partial(last_kernel, n_tp),
        [hidden_in, mixed_grad, gain_one, *one_got],
        [shape((own, width), bf16)],
    )[0]
    input_parts = exchange([input_own] * n_tp)
    layer_rest = after(layer_rest, input_own)
    layer_out = call(
        functools.partial(join_kernel, n_tp),
        [layer_own, layer_rest[0], layer_two, layer_rest[1]],
        [shape((rows, width), bf16)],
        work=1,
    )[0]
    if near:
        feed_send = after(feed_here[block:], one_parts[0])
        feed_here = feed_here[:block]
        gate_w, up_w, down_w = call(
            feed_grad_sum_kernel,
            [after(feed_here, input_own), swap_across(feed_send, 1)],
            [shape((block, units), f32), shape((block, units), f32), shape((units, block), f32)],
            work=1,
        )
        query_w, key_w, value_w, out_w, gains = call(
            attn_grad_sum_kernel,
            [after(attn_here, input_own), swap_across(attn_send, 1)],
            [
                shape((block, 256), f32),
                shape((block, 128), f32),
                shape((block, 128), f32),
                shape((256, block), bf16),
                shape((8, 128), f32),
            ],
            work=1,
        )
        out_w, gains = lax.optimization_barrier((out_w, gains, input_parts[1]))[:2]
        turn = []
        for a in range(n_tp):
            for b in range(2):
                for t in range(n_tp):
                    turn.append(((2 * a + b) * n_tp + t, (2 * t + b) * n_tp + a))
        out_w = lax.ppermute(out_w, ("ctx", "tp"), turn)
    else:

        def scatter(left, right, dim=0):
            grad = dot(left, right, TN).astype(bf16)
            return lax.psum_scatter(grad, "ctx", scatter_dimension=dim, tiled=True).astype(f32)

        attn_grad_all = lax.all_gather(attn_grad, "tp", axis=0, tiled=True)
        down_w = scatter(act, out_grad, 1)
        gate_w = scatter(h_two, gate_grad)
        up_w = scatter(h_two, up_grad)
        out_w = scatter(attended, attn_grad_all, 1)
        query_w = scatter(h_one, query_pre_low)
        kv_w = scatter(h_one, kv_pre_low)
        key_w, value_w = kv_w[:, :128], kv_w[:, 128:]

    if not near:
        gains = lax.psum(gains, "ctx")
        cut = lambda row: lax.dynamic_slice_in_dim(
            gains[row : row + lots].reshape(width), mine * block, block, 0
        )
        heads = jnp.concatenate([gains[2 * lots, :64], gains[2 * lots + 1, :64]])
        gains = jnp.stack([jnp.pad(cut(0), (0, 128 - block)), jnp.pad(cut(lots), (0, 128 - block)), heads])
        gains = jnp.pad(gains, ((0, 5), (0, 0)))
    gains = gains + swap(gains, "tp", 1)
    gain_one_sum, gain_two_sum, q_gain_sum, k_gain_sum, out_w = call(
        functools.partial(gain_kernel, block),
        [gains, swap(gains, "tp", 2), out_w],
        [shape((1, block), f32)] * 2 + [shape((1, 64), f32)] * 2 + [shape(out_w.shape, f32)],
        work=1,
    )
    input_parts[0] = after(input_parts[0], gate_w, layer_out, out_w)
    input_grad = call(
        functools.partial(join_kernel, n_tp), input_parts, [shape((rows, width), f32)]
    )[0]

    return (
        layer_out,
        input_grad,
        gain_one_sum[0],
        query_w,
        key_w,
        value_w,
        q_gain_sum[0],
        k_gain_sum[0],
        out_w,
        gain_two_sum[0],
        gate_w,
        up_w,
        down_w,
    )


def solution(mesh):
    in_specs = (
        P("ctx", None),
        P(),
        P(),
        P(None, "tp"),
        P(None, "tp"),
        P(None, "tp"),
        P(),
        P(),
        P("tp", None),
        P(),
        P(None, "tp"),
        P(None, "tp"),
        P("tp", None),
        P("ctx", None),
    )
    out_specs = (
        P("ctx", None),
        P("ctx", None),
        P("ctx"),
        P("ctx", "tp"),
        P("ctx", "tp"),
        P("ctx", "tp"),
        P(),
        P(),
        P("tp", "ctx"),
        P("ctx"),
        P("ctx", "tp"),
        P("ctx", "tp"),
        P("tp", "ctx"),
    )
    return jax.shard_map(shards, mesh=mesh, in_specs=in_specs, out_specs=out_specs, check_vma=False)
```

```python
import functools
import math

import jax
import jax.numpy as jnp
from jax import lax
from jax.experimental import pallas as pl
from jax.experimental.pallas import tpu as pltpu
from jax.sharding import PartitionSpec as P

norm_eps = 1e-05
rope_base = 1000000.0
f32 = jnp.float32
bf16 = jnp.bfloat16
NN = (((1,), (0,)), ((), ()))
NT = (((1,), (1,)), ((), ()))
TN = (((0,), (0,)), ((), ()))
VMEM = pl.BlockSpec(memory_space=pltpu.VMEM)
SMEM = pl.BlockSpec(memory_space=pltpu.SMEM)
megabyte = 1024 * 1024
work = 5 * 10**10


def dot(left, right, dims=NN):
    return lax.dot_general(left, right, dims, preferred_element_type=f32)


def call(body, inputs, outs, scratch=(), work=work, limit=18, **kwargs):
    in_specs = kwargs.pop("in_specs", None)
    if in_specs is None:
        in_specs = [
            SMEM if (x.dtype == jnp.int32 and x.ndim == 1) else VMEM for x in inputs
        ]
    out_specs = kwargs.pop("out_specs", [VMEM] * len(outs))
    moved = sum(x.size * x.dtype.itemsize for x in inputs) + sum(
        math.prod(o.shape) * o.dtype.itemsize for o in outs
    )
    return pl.pallas_call(
        body,
        out_shape=outs,
        in_specs=in_specs,
        out_specs=out_specs,
        scratch_shapes=list(scratch),
        compiler_params=pltpu.CompilerParams(vmem_limit_bytes=limit * megabyte),
        cost_estimate=pl.CostEstimate(flops=work, bytes_accessed=moved, transcendentals=0),
        **kwargs,
    )(*inputs)


def shape(dims, dtype):
    return jax.ShapeDtypeStruct(dims, dtype)


def lanes(x):
    return lax.broadcasted_iota(jnp.int32, x.shape, 1)


def head_mean(x):
    first = lanes(x) < 64
    low = jnp.sum(jnp.where(first, x, 0.0), axis=1, keepdims=True)
    high = jnp.sum(jnp.where(first, 0.0, x), axis=1, keepdims=True)
    return jnp.where(first, low, high) * (1.0 / 64.0)


def swap_halves(x):
    return jnp.where(lanes(x) % 64 < 32, pltpu.roll(x, 96, 1), pltpu.roll(x, 32, 1))


def head_norm(pre, gain):
    inverse = lax.rsqrt(head_mean(pre * pre) + norm_eps)
    return pre * inverse * gain


def head_norm_back(pre, gain, grads):
    inverse = lax.rsqrt(head_mean(pre * pre) + norm_eps)
    normed = pre * inverse
    scaled = grads * gain
    inner = head_mean(scaled * normed)
    return inverse * (scaled - normed * inner), grads * normed


def doc_begin(positions, starts_ref):
    begin = jnp.zeros_like(positions)
    for i in range(starts_ref.shape[0]):
        begin = jnp.where(starts_ref[i] <= positions, starts_ref[i], begin)
    return begin


def twice(gain_ref):
    return jnp.concatenate([gain_ref[...], gain_ref[...]], axis=1)


def quarter(partner, size):
    place = jnp.bitwise_xor(lax.axis_index("tp"), partner)
    return pl.ds(pl.multiple_of(place * size, size), size)


def around(refs):
    return [
        refs[0][...],
        refs[1][...],
        jnp.concatenate([refs[2][...], refs[3][...]], axis=0),
        refs[4][...],
    ]


def store_around(acc_ref, refs):
    own = refs[0].shape[0]
    half = own // 2
    refs[0][...] = acc_ref[quarter(0, own), :].astype(bf16)
    refs[1][...] = acc_ref[quarter(1, own), :].astype(bf16)
    far = acc_ref[quarter(2, own), :].astype(bf16)
    refs[2][...] = far[:half]
    refs[3][...] = far[half:]
    refs[4][...] = acc_ref[quarter(3, own), :].astype(bf16)


def row_norm(x):
    return lax.rsqrt(jnp.mean(x * x, axis=1, keepdims=True) + norm_eps)


def kv_kernel(
    starts_ref, x_ref, gain_ref, wk_ref, wv_ref, freq_ref, kgain_ref, h_ref, kv_ref, kpre_ref, cos_ref, sin_ref
):
    rows = x_ref.shape[0]
    positions = lax.axis_index("ctx") * rows + lax.broadcasted_iota(jnp.int32, (rows, 128), 0)
    angles = (positions - doc_begin(positions, starts_ref)).astype(f32) * freq_ref[...]
    cosine, sine = jnp.cos(angles), jnp.sin(angles)
    sine = jnp.where(lanes(sine) % 64 < 32, -sine, sine)
    cos_ref[...] = cosine
    sin_ref[...] = sine
    x = x_ref[...].astype(f32)
    h = (x * row_norm(x) * gain_ref[...]).astype(bf16)
    h_ref[...] = h
    kpre = dot(h, wk_ref[...])
    kpre_ref[...] = kpre
    kn = head_norm(kpre, twice(kgain_ref))
    key = kn * cosine + swap_halves(kn) * sine
    kv_ref[:, :128] = key.astype(bf16)
    kv_ref[:, 128:] = dot(h, wv_ref[...]).astype(bf16)


def spread(x, half, out_ref, base, rows):
    rolled = pltpu.roll(x, 64, 1)
    keep = (lanes(x) < 64) if half == 0 else (lanes(x) >= 64)
    first, second = (x, rolled) if half == 0 else (rolled, x)
    out_ref[pl.ds(base, rows), :] = jnp.where(keep, first, 0.0).astype(bf16)
    out_ref[pl.ds(base + rows, rows), :] = jnp.where(keep, second, 0.0).astype(bf16)


def q_kernel(h_ref, wq_ref, cos_ref, sin_ref, qgain_ref, qpad_ref, qpre_ref):
    rows = h_ref.shape[0]
    qpre = dot(h_ref[...], wq_ref[...])
    qpre_ref[...] = qpre
    for half in range(2):
        qn = head_norm(qpre[:, 128 * half : 128 * half + 128], twice(qgain_ref))
        x = qn * cos_ref[...] + swap_halves(qn) * sin_ref[...]
        spread(x, half, qpad_ref, 2 * half * rows, rows)


def visit_blocks(near, rows, starts_ref, count, lists, visit, skip=None):
    mine = lax.axis_index("ctx")
    first, last = mine * rows, mine * rows + rows - 1
    first_begin, last_begin = doc_begin(first, starts_ref), doc_begin(last, starts_ref)
    for which in range(lists):

        def step(index, carry, which=which):
            block = jnp.bitwise_xor(mine, 2 * index + which) if near else index
            start = block * rows
            seen = (block <= mine) & (start + rows - 1 >= first_begin)
            whole = (block < mine) & (start >= last_begin)

            def mask():
                dims = (rows, 2 * rows)
                key_pos = lax.broadcasted_iota(jnp.int32, dims, 0) + start
                across = lax.broadcasted_iota(jnp.int32, (1, 2 * rows), 1)
                query_pos = first + jnp.where(across < rows, across, across - rows)
                return (key_pos <= query_pos) & (key_pos >= doc_begin(query_pos, starts_ref))

            pl.when(seen & whole)(lambda: visit(which, index, None))
            pl.when(seen & jnp.logical_not(whole))(lambda: visit(which, index, mask))
            if skip is not None:
                pl.when(jnp.logical_not(seen))(lambda: skip(which, index))
            return carry

        lax.fori_loop(0, count, step, 0)


def attend_kernel(near, scale, starts_ref, qpad_ref, *refs):
    lists = 2 if near else 1
    kv_refs = refs[:lists]
    o_ref, o32_ref, lse_ref, acc_ref, mass_ref = refs[lists:]
    rows = o_ref.shape[0]
    acc_ref[...] = jnp.zeros_like(acc_ref)
    mass_ref[...] = jnp.zeros_like(mass_ref)
    factor = scale * math.log2(math.e)

    def visit(which, index, mask):
        at = pl.ds(pl.multiple_of(index * rows, rows), rows)
        keys = kv_refs[which][at, :128]
        values_t = kv_refs[which][at, 128:].T
        for j in range(2):
            p = jnp.exp2(dot(keys, qpad_ref[2 * rows * j : 2 * rows * (j + 1), :], NT) * factor)
            if mask is not None:
                p = jnp.where(mask(), p, 0.0)
            mass_ref[j : j + 1, :] += jnp.sum(p, axis=0, keepdims=True)
            acc_ref[j] += dot(values_t, p.astype(bf16))

    visit_blocks(near, rows, starts_ref, kv_refs[0].shape[0] // rows, lists, visit)
    mass = mass_ref[...]
    lse_ref[...] = jnp.log2(mass)
    parts = []
    for j in range(2):
        normed = acc_ref[j, 64 * j : 64 * j + 64, :] / mass[j : j + 1, :]
        parts += [normed[:, :rows], normed[:, rows:]]
    o32 = jnp.concatenate(parts, axis=0).T
    o32_ref[...] = o32
    o_ref[...] = o32.astype(bf16)


def attend_back_kernel(near, scale, n_tp, starts_ref, qpad_ref, o32_ref, lse_ref, *refs):
    lists = 2 if near else 1
    kv_refs, refs = refs[:lists], refs[lists:]
    dout_refs, refs = refs[:n_tp], refs[n_tp:]
    dq_ref, refs = refs[0], refs[1:]
    dkv_refs, refs = refs[:lists], refs[lists:]
    dout_ref, dopad_ref, dqt_ref = refs
    rows = dq_ref.shape[0]
    factor = scale * math.log2(math.e)
    for k in range(n_tp):
        dout_ref[quarter(k, rows // n_tp), :] = dout_refs[k][...].astype(f32)
    dout = dout_ref[...]
    for half in range(2):
        spread(dout[:, 128 * half : 128 * half + 128], half, dopad_ref, 2 * half * rows, rows)
    weighted = (dout * o32_ref[...]).T
    deltas = [jnp.sum(weighted[64 * h : 64 * h + 64], axis=0, keepdims=True) for h in range(4)]
    delta = [jnp.concatenate(deltas[2 * j : 2 * j + 2], axis=1) for j in range(2)]
    dqt_ref[...] = jnp.zeros_like(dqt_ref)

    def visit(which, index, mask):
        at = pl.ds(pl.multiple_of(index * rows, rows), rows)
        keys = kv_refs[which][at, :128]
        values = kv_refs[which][at, 128:]
        keys_t = keys.T
        dk = jnp.zeros((rows, 128), f32)
        dv = jnp.zeros((rows, 128), f32)
        for j in range(2):
            qpad = qpad_ref[2 * rows * j : 2 * rows * (j + 1), :]
            dopad = dopad_ref[2 * rows * j : 2 * rows * (j + 1), :]
            p = jnp.exp2(dot(keys, qpad, NT) * factor - lse_ref[j : j + 1, :])
            if mask is not None:
                p = jnp.where(mask(), p, 0.0)
            ds = (p * (dot(values, dopad, NT) - delta[j])).astype(bf16)
            dv += dot(p.astype(bf16), dopad)
            dk += dot(ds, qpad)
            dqt_ref[j] += dot(keys_t, ds)
        dkv_refs[which][at, :128] = (dk * scale).astype(bf16)
        dkv_refs[which][at, 128:] = dv.astype(bf16)

    def skip(which, index):
        at = pl.ds(pl.multiple_of(index * rows, rows), rows)
        dkv_refs[which][at, :] = jnp.zeros((rows, 256), bf16)

    visit_blocks(near, rows, starts_ref, kv_refs[0].shape[0] // rows, lists, visit, skip)
    parts = []
    for j in range(2):
        part = dqt_ref[j, 64 * j : 64 * j + 64, :]
        parts += [part[:, :rows], part[:, rows:]]
    dq_ref[...] = (jnp.concatenate(parts, axis=0).T * scale).astype(bf16)


def core_halves(size):
    core = lax.axis_index("ctx") % 2
    return (
        pl.ds(pl.multiple_of(core * size, size), size),
        pl.ds(pl.multiple_of((1 - core) * size, size), size),
    )


def mix_kernel(x_ref, gain_ref, w0_ref, wm_ref, wp_ref, *refs):
    parts = around(refs[:5])
    h_ref, y_ref, acc_ref = refs[5:]
    acc = x_ref[...].astype(f32) + dot(parts[0], w0_ref[...])
    core = lax.axis_index("ctx") % 2
    half = w0_ref.shape[0] // 2
    for k in range(1, 4):
        low, high = parts[k][:, :half], parts[k][:, half:]
        acc += dot(jnp.where(core == 0, low, high), wm_ref[k - 1])
        acc += dot(jnp.where(core == 0, high, low), wp_ref[k - 1])
    acc_ref[...] = acc
    y_ref[...] = acc_ref[quarter(0, y_ref.shape[0]), :]
    h_ref[...] = (acc * row_norm(acc) * gain_ref[...]).astype(bf16)


def feed_kernel(h_ref, g_ref, wg_ref, wu_ref, wd_ref, act_ref, dg_ref, du_ref, *refs):
    dh_refs, acc_ref = refs[:5], refs[5]
    gate = dot(h_ref[...], wg_ref[...])
    up = dot(h_ref[...], wu_ref[...])
    dact = dot(g_ref[...], wd_ref[...], NT)
    sigma = jax.nn.sigmoid(gate)
    silu = gate * sigma
    act_ref[...] = (silu * up).astype(bf16)
    dgate = (dact * up * sigma * (1.0 + gate * (1.0 - sigma))).astype(bf16)
    dup = (dact * silu).astype(bf16)
    dg_ref[...] = dgate
    du_ref[...] = dup
    acc_ref[...] = dot(dgate, wg_ref[...], NT) + dot(dup, wu_ref[...], NT)
    store_around(acc_ref, dh_refs)


def reduce_kernel(one_ref, three_ref, got_one_ref, got_three_ref, to_one_ref, to_three_ref):
    half = got_one_ref.shape[0]
    to_one_ref[:half, :] = one_ref[:half, :]
    to_one_ref[half:, :] = (one_ref[half:, :].astype(f32) + got_three_ref[...].astype(f32)).astype(bf16)
    to_three_ref[:half, :] = (three_ref[:half, :].astype(f32) + got_one_ref[...].astype(f32)).astype(bf16)
    to_three_ref[half:, :] = three_ref[half:, :]


def mid_kernel(g_ref, y_ref, gain_ref, w0_ref, wm_ref, wp_ref, *refs):
    dh_refs, refs = refs[:3], refs[3:]
    dy_ref, dattn_ref, gaing_ref = refs[:3]
    dout_refs = refs[3:]
    dh = sum(ref[...].astype(f32) for ref in dh_refs)
    y = y_ref[...]
    inverse = row_norm(y)
    z = y * inverse
    gaing_ref[...] = jnp.sum(dh * z, axis=0, keepdims=True)
    e = dh * gain_ref[...]
    inner = jnp.mean(e * z, axis=1, keepdims=True)
    dy = g_ref[quarter(0, y_ref.shape[0]), :].astype(f32) + inverse * (e - z * inner)
    dy_ref[...] = dy
    low = dy.astype(bf16)
    dattn_ref[...] = low
    dout_refs[0][...] = dot(low, w0_ref[...], NT).astype(bf16)
    first, second = core_halves(w0_ref.shape[0] // 2)
    for k in range(1, 4):
        dout_refs[k][:, first] = dot(low, wm_ref[k - 1], NT).astype(bf16)
        dout_refs[k][:, second] = dot(low, wp_ref[k - 1], NT).astype(bf16)


def down_kernel(n_tp, act_ref, wd_ref, dattn_ref, *refs):
    out_refs, acc_ref = refs[:n_tp], refs[n_tp]
    own, width = dattn_ref.shape
    acc_ref[...] = dot(act_ref[...], wd_ref[...])
    for k in range(n_tp):
        out_refs[k][:, :width] = acc_ref[quarter(k, own), :].astype(bf16)
        out_refs[k][:, width:] = dattn_ref[:, quarter(k, width // n_tp)]


def layer_kernel(n_tp, y_ref, *refs):
    own, width = y_ref.shape
    out_ref, cut_ref = refs[n_tp:]
    total = y_ref[...]
    for k in range(n_tp):
        total += refs[k][:, :width].astype(f32)
        cut_ref[quarter(k, own), :] = refs[k][:, width:]
    out_ref[...] = total.astype(bf16)


def q_back_kernel(near, dq_ref, qpre_ref, cos_ref, sin_ref, qgain_ref, wq_ref, h_ref, *refs):
    if near:
        dattn_ref, parts, refs = refs[0], around(refs[1:6]), refs[6:]
        odd_ref, even_ref, hp_ref, oall_ref = refs[3:]
    low_ref, gaing_ref, dh_ref = refs[:3]
    total = jnp.zeros((1, 128), f32)
    for half in range(2):
        cut = slice(128 * half, 128 * half + 128)
        x = dq_ref[:, cut].astype(f32)
        dqn = x * cos_ref[...] - swap_halves(x) * sin_ref[...]
        dpre, weighted = head_norm_back(qpre_ref[:, cut], twice(qgain_ref), dqn)
        low_ref[:, cut] = dpre.astype(bf16)
        total += jnp.sum(weighted, axis=0, keepdims=True)
    gaing_ref[...] = total + pltpu.roll(total, 64, 1)
    dh_ref[...] = dot(low_ref[...], wq_ref[...], NT)
    if near:
        mine, place = lax.axis_index("ctx"), lax.axis_index("tp")
        for k, part in enumerate(parts):
            oall_ref[k] = part
        for parity, out_ref in ((1, odd_ref), (0, even_ref)):
            gather_columns(parity, h_ref, hp_ref)
            out_ref[:, :256] = dot(hp_ref[...], low_ref[...], TN).astype(bf16)
            left = columns(dattn_ref, jnp.bitwise_xor(mine % 2, parity)).T
            for at, chip in enumerate(block_order(parity)):
                heads = jnp.bitwise_xor(jnp.bitwise_xor(mine // 2, chip), place)
                out_ref[128 * at : 128 * at + 128, 256:] = dot(left, oall_ref[heads]).astype(bf16)


def k_back_kernel(near, n_parts, *refs):
    parts, refs = refs[:n_parts], refs[n_parts:]
    kpre_ref, cos_ref, sin_ref, kgain_ref, wk_ref, wv_ref, dhq_ref, x_ref, gain2_ref, qg_ref, h_ref = refs[:11]
    low_ref, gains_ref = refs[11:13]
    dh_refs, refs = refs[13:18], refs[18:]
    acc_ref = refs[-1]
    total = parts[0][...].astype(f32)
    for part in parts[1:]:
        total += part[...].astype(f32)
    low = total.astype(bf16)
    x = low[:, :128].astype(f32)
    dkn = x * cos_ref[...] - swap_halves(x) * sin_ref[...]
    dpre, weighted = head_norm_back(kpre_ref[...], twice(kgain_ref), dkn)
    dk = dpre.astype(bf16)
    dv = low[:, 128:]
    low_ref[:, :128] = dk
    low_ref[:, 128:] = dv
    dh = dhq_ref[...] + dot(dk, wk_ref[...], NT) + dot(dv, wv_ref[...], NT)
    acc_ref[...] = dh
    store_around(acc_ref, dh_refs)
    x_in = x_ref[...].astype(f32)
    width = x_in.shape[1]
    lots = width // 128
    gain_one = jnp.sum(dh * (x_in * row_norm(x_in)), axis=0, keepdims=True)
    for i in range(lots):
        gains_ref[i : i + 1, :] = gain_one[:, 128 * i : 128 * i + 128]
        gains_ref[lots + i : lots + i + 1, :] = gain2_ref[:, 128 * i : 128 * i + 128]
    gains = jnp.sum(weighted, axis=0, keepdims=True)
    gains_ref[2 * lots : 2 * lots + 1, :] = qg_ref[...]
    gains_ref[2 * lots + 1 : 2 * lots + 2, :] = gains + pltpu.roll(gains, 64, 1)
    gains_ref[2 * lots + 2 :, :] = jnp.zeros((gains_ref.shape[0] - 2 * lots - 2, 128), f32)
    if near:
        odd_ref, even_ref, hp_ref = refs[:3]
        mine = lax.axis_index("ctx")
        for parity, out_ref in ((1, odd_ref), (0, even_ref)):
            gather_columns(parity, h_ref, hp_ref)
            out_ref[:, :256] = dot(hp_ref[...], low_ref[...], TN).astype(bf16)
            for at, chip in enumerate(block_order(parity)):
                block = jnp.bitwise_xor(mine, 2 * chip + parity)
                out_ref[128 * at : 128 * at + 128, 256:] = parted(gain_columns(gains_ref, block, lots))


def last_kernel(x_ref, dy_ref, gain_ref, *refs):
    dh_refs, out_ref = refs[:3], refs[3]
    dh = sum(ref[...].astype(f32) for ref in dh_refs)
    x = x_ref[quarter(0, dy_ref.shape[0]), :].astype(f32)
    inverse = row_norm(x)
    z = x * inverse
    e = dh * gain_ref[...]
    inner = jnp.mean(e * z, axis=1, keepdims=True)
    out_ref[...] = (dy_ref[...] + inverse * (e - z * inner)).astype(bf16)


def join_kernel(*refs):
    out_ref = refs[5]
    for k, part in enumerate(around(refs[:5])):
        out_ref[quarter(k, part.shape[0]), :] = part.astype(out_ref.dtype)


def block_order(parity):
    core = lax.axis_index("ctx") % 2
    first, second = 1 + core, 2 - core
    return (0, first, second, 3) if parity else (0, second, first, 3)


def columns(src_ref, block):
    return src_ref[:, pl.ds(pl.multiple_of(block * 128, 128), 128)]


def gather_columns(parity, src_ref, dst_ref):
    mine = lax.axis_index("ctx")
    for place, chip in enumerate(block_order(parity)):
        dst_ref[:, 128 * place : 128 * place + 128] = columns(src_ref, jnp.bitwise_xor(mine, 2 * chip + parity))


def feed_grad_kernel(h_ref, g_ref, act_ref, dg_ref, du_ref, odd_ref, even_ref, hp_ref, gp_ref):
    units = act_ref.shape[1]
    for parity, out_ref in ((1, odd_ref), (0, even_ref)):
        gather_columns(parity, h_ref, hp_ref)
        gather_columns(parity, g_ref, gp_ref)
        for i, (left_ref, right_ref) in enumerate(((hp_ref, dg_ref), (hp_ref, du_ref), (gp_ref, act_ref))):
            out_ref[:, units * i : units * (i + 1)] = dot(left_ref[...], right_ref[...], TN).astype(bf16)


def feed_grad_sum_kernel(keep_ref, got_ref, gate_ref, up_ref, down_ref):
    units = gate_ref.shape[1]
    for i, out_ref in enumerate((gate_ref, up_ref, down_ref)):
        cut = slice(units * i, units * (i + 1))
        total = keep_ref[:, cut].astype(f32) + got_ref[:, cut].astype(f32)
        out_ref[...] = total.T if i == 2 else total


def joined(x):
    x = x.astype(f32)
    return x + pltpu.roll(x, 64, 1)


def parted(x):
    high = x.astype(bf16).astype(f32)
    return jnp.where(lanes(x) < 64, high, x - high).astype(bf16)


def gain_columns(gains_ref, block, lots):
    row = lambda i: gains_ref[pl.ds(i, 1), :]
    heads = jnp.where(lanes(row(0)) < 64, row(2 * lots), row(2 * lots + 1))
    rows = jnp.concatenate([row(block), row(lots + block), heads, jnp.zeros((125, 128), f32)], axis=0)
    total = rows.T
    return total + pltpu.roll(total, 64, 1)


def attn_grad_chip_kernel(q_ref, q_got_ref, kv_ref, kv_got_ref, here_ref, send_ref):
    half = here_ref.shape[0]
    for i, out_ref in enumerate((here_ref, send_ref)):
        row = slice(half * i, half * (i + 1))
        out_ref[:, :512] = (q_ref[row, :].astype(f32) + q_got_ref[row, :].astype(f32)).astype(bf16)
        out_ref[:, 512:768] = (kv_ref[row, :256].astype(f32) + kv_got_ref[row, :256].astype(f32)).astype(bf16)
        out_ref[:, 768:] = parted(joined(kv_ref[row, 256:]) + joined(kv_got_ref[row, 256:]))


def attn_grad_pass_kernel(keep_ref, got_ref, here_ref, send_ref):
    half = here_ref.shape[0]
    for i, out_ref in enumerate((here_ref, send_ref)):
        row = slice(half * i, half * (i + 1))
        out_ref[:, :768] = (keep_ref[row, :768].astype(f32) + got_ref[row, :768].astype(f32)).astype(bf16)
        out_ref[:, 768:] = parted(joined(keep_ref[row, 768:]) + joined(got_ref[row, 768:]))


def attn_grad_sum_kernel(keep_ref, got_ref, q_ref, k_ref, v_ref, o_ref, gains_ref):
    total = keep_ref[:, :768].astype(f32) + got_ref[:, :768].astype(f32)
    q_ref[...] = total[:, :256]
    o_ref[...] = total[:, 256:512].T.astype(bf16)
    k_ref[...] = total[:, 512:640]
    v_ref[...] = total[:, 640:]
    gains_ref[...] = (joined(keep_ref[:, 768:]) + joined(got_ref[:, 768:])).T[:8]


def gain_kernel(block, a_ref, b_ref, w_ref, one_ref, two_ref, q_ref, k_ref, out_ref):
    out_ref[...] = w_ref[...].astype(f32)
    total = a_ref[...] + b_ref[...]
    one_ref[...] = total[0:1, :block]
    two_ref[...] = total[1:2, :block]
    q_ref[...] = total[2:3, :64]
    k_ref[...] = total[2:3, 64:]


def swap(x, axis, k):
    size = lax.axis_size(axis)
    return lax.ppermute(x, axis, [(i, i ^ k) for i in range(size)])


def swap_across(x, step):
    size = lax.axis_size("ctx")
    return lax.ppermute(x, "ctx", [(i, i ^ (2 << ((i + step) % 2))) for i in range(size)])


def after(x, *first):
    return lax.optimization_barrier((x, *first))[0]


def shards(
    hidden_in,
    doc_starts,
    norm1_gain,
    w_query,
    w_key,
    w_value,
    query_gain,
    key_gain,
    w_out,
    norm2_gain,
    w_gate,
    w_up,
    w_down,
    out_grad,
):
    rows, width = hidden_in.shape
    n_ctx, n_tp = lax.axis_size("ctx"), lax.axis_size("tp")
    head_dim = query_gain.shape[0]
    scale = head_dim ** (-0.5)
    near = n_ctx == 2 * n_tp and width == 128 * n_ctx
    own = rows // n_tp
    units = w_gate.shape[1]
    others = range(1, n_tp)
    chips = range(1, n_ctx // 2)
    mine, place = lax.axis_index("ctx"), lax.axis_index("tp")
    gain_one, gain_two = norm1_gain[None, :], norm2_gain[None, :]
    q_gain, k_gain = query_gain[None, :], key_gain[None, :]
    frequency = rope_base ** (-2.0 * jnp.arange(head_dim // 2, dtype=f32) / head_dim)
    frequency = jnp.concatenate([frequency] * 4)[None, :]

    def exchange(parts):
        return [parts[0]] + [swap(parts[k], "tp", k) for k in others]

    def gather(x, *first):
        one, three = swap(x, "tp", 1), swap(x, "tp", 3)
        half = x.shape[0] // 2
        near_one, near_three = lax.optimization_barrier((one, three, *first))[:2] if first else (one, three)
        return [x, one, swap(near_three[:half], "tp", 1), swap(near_one[half:], "tp", 3), three]

    def reduce(parts, *first):
        here, one, far_low, far_high, three = parts
        got_one, got_three = swap(far_low, "tp", 1), swap(far_high, "tp", 3)
        if first:
            one = after(one, *first)
        to_one, to_three = call(
            reduce_kernel,
            [one, three, got_one, got_three],
            [shape(one.shape, bf16)] * 2,
            work=1,
        )
        return [here, swap(to_one, "tp", 1), swap(to_three, "tp", 3)], to_one

    quarters = [shape((own, width), bf16)] * 2 + [shape((own // 2, width), bf16)] * 2 + [shape((own, width), bf16)]

    h_one, kv, key_pre, cosine, sine = call(
        kv_kernel,
        [doc_starts, hidden_in, gain_one, w_key, w_value, frequency, k_gain],
        [
            shape((rows, width), bf16),
            shape((rows, 256), bf16),
            shape((rows, 128), f32),
            shape((rows, 128), f32),
            shape((rows, 128), f32),
        ],
        limit=56,
    )
    if near:
        kv_got = [swap(kv, "ctx", 2 * i) for i in chips]
    else:
        kv_all = [lax.all_gather(kv, "ctx", axis=0, tiled=True)]
    half = w_out.shape[0] // 2
    w_half = lax.dynamic_slice_in_dim(w_out, (mine % 2) * half, half, 0)
    w_around = gather(w_half)
    qpad, query_pre = call(
        q_kernel,
        [h_one, w_query, cosine, sine, q_gain],
        [shape((4 * rows, 128), bf16), shape((rows, 256), f32)],
    )
    if near:
        even = jnp.concatenate([after(kv, qpad, w_around[1], w_around[4]), *kv_got], axis=0)
        kv_all = [even, swap(even, "ctx", 1)]
    attended, attended32, log_mass = call(
        functools.partial(attend_kernel, near, scale),
        [doc_starts, qpad, *kv_all],
        [shape((rows, 256), bf16), shape((rows, 256), f32), shape((2, 2 * rows), f32)],
        [pltpu.VMEM((2, 128, 2 * rows), f32), pltpu.VMEM((2, 2 * rows), f32)],
    )
    o_parts = gather(attended)
    w_around = lax.optimization_barrier((*w_around, attended))[:5]
    w_mine = jnp.stack([w_around[1], jnp.concatenate(w_around[2:4], axis=0), w_around[4]])
    w_all = [w_mine, swap(w_mine, "ctx", 1)]
    h_two, mixed_own = call(
        mix_kernel,
        [hidden_in, gain_two, w_out, *w_all, *o_parts],
        [shape((rows, width), bf16), shape((own, width), f32)],
        [pltpu.VMEM((rows, width), f32)],
    )

    got = call(
        feed_kernel,
        [h_two, out_grad, w_gate, w_up, w_down],
        [shape((rows, units), bf16)] * 3 + quarters,
        [pltpu.VMEM((rows, width), f32)],
        limit=24,
    )
    act, gate_grad, up_grad = got[:3]
    two_parts = got[3:]
    block = width // n_ctx
    if near:
        ordered = pltpu.VMEM((rows, 4 * block), bf16)
        feed_odd, feed_even = call(
            feed_grad_kernel,
            [h_two, out_grad, act, gate_grad, up_grad],
            [shape((4 * block, 3 * units), bf16)] * 2,
            [ordered, ordered],
        )
    two_got, _ = reduce(two_parts, *([feed_even] if near else []))
    got = call(
        mid_kernel,
        [out_grad, mixed_own, gain_two, w_out, *w_all, *two_got],
        [shape((own, width), f32), shape((own, width), bf16), shape((1, width), f32)]
        + [shape((own, 256), bf16)] * n_tp,
    )
    mixed_grad, attn_grad, gain_two_part = got[:3]
    dout = exchange(got[3:])

    down = call(
        functools.partial(down_kernel, n_tp),
        [act, w_down, attn_grad],
        [shape((own, width + width // n_tp), bf16)] * n_tp,
        [pltpu.VMEM((rows, width), f32)],
    )
    if near:
        half = 2 * block
        feed_other = swap(feed_odd, "ctx", 1)
        feed_send = feed_even[half:] + feed_other[half:]
        feed_got = swap_across(feed_send, 0)
        qpad = after(qpad, feed_send, down[1])
    down_got = exchange(list(lax.optimization_barrier((*down, *dout[1:]))[:n_tp]))

    got = call(
        functools.partial(attend_back_kernel, near, scale, n_tp),
        [doc_starts, qpad, attended32, log_mass, *kv_all, *dout],
        [shape((rows, 256), bf16)] + [shape(x.shape, bf16) for x in kv_all],
        [
            pltpu.VMEM((rows, 256), f32),
            pltpu.VMEM((4 * rows, 128), bf16),
            pltpu.VMEM((2, 128, 2 * rows), f32),
        ],
    )
    query_low, dkv = got[0], got[1:]
    if near:
        other = swap(after(dkv[1], *down_got[1:]), "ctx", 1)
        pieces = [
            dkv[0][i * rows : (i + 1) * rows] + other[i * rows : (i + 1) * rows] for i in range(n_ctx // 2)
        ]
        kv_parts = [pieces[0]] + [swap(pieces[i], "ctx", 2 * i) for i in chips]
    else:
        kv_parts = [lax.psum_scatter(dkv[0], "ctx", scatter_dimension=0, tiled=True)]
    down_got = list(lax.optimization_barrier((*down_got, query_low))[:n_tp])
    layer_own, attn_grad_cut = call(
        functools.partial(layer_kernel, n_tp),
        [mixed_own, *down_got],
        [shape((own, width), bf16), shape((rows, width // n_tp), bf16)],
        work=1,
    )
    layer_one, layer_three = swap(layer_own, "tp", 1), swap(layer_own, "tp", 3)

    if near:
        feed_parts = lax.optimization_barrier((feed_even, feed_other, feed_got, query_low))[:3]
        feed_here = sum(x[:half].astype(f32) for x in feed_parts).astype(bf16)
        query_low = after(query_low, *pieces)
    more = [attn_grad_cut, *o_parts] if near else []
    got = call(
        functools.partial(q_back_kernel, near),
        [query_low, query_pre, cosine, sine, q_gain, w_query, h_one, *more],
        [shape((rows, 256), bf16), shape((1, 128), f32), shape((rows, width), f32)]
        + ([shape((4 * block, 512), bf16)] * 2 if near else []),
        [ordered, pltpu.VMEM((n_tp, rows, 256), bf16)] if near else [],
        work=1,
    )
    query_pre_low, q_gain_part, one_query = got[:3]
    done = [layer_one, layer_three, feed_here] if near else [layer_one, layer_three]
    if near:
        q_odd, q_even = got[3:]
        q_other = swap(q_odd, "ctx", 1)
        done.append(q_other)
    lots = width // 128
    gain_rows = 2 * lots + 8
    got = call(
        functools.partial(k_back_kernel, near, len(kv_parts)),
        [
            *kv_parts,
            after(key_pre, *done),
            cosine,
            sine,
            k_gain,
            w_key,
            w_value,
            one_query,
            hidden_in,
            gain_two_part,
            q_gain_part,
            h_one,
        ],
        [shape((rows, 256), bf16), shape((gain_rows, 128), f32)]
        + quarters
        + ([shape((4 * block, 384), bf16)] * 2 if near else []),
        ([ordered] if near else []) + [pltpu.VMEM((rows, width), f32)],
    )
    kv_pre_low, gains = got[:2]
    one_parts = got[2:7]
    one_got, token = reduce(one_parts)
    if near:
        kv_odd, kv_even = got[7:]
        kv_odd = after(kv_odd, token)
        attn_here, attn_send = call(
            attn_grad_chip_kernel,
            [q_even, q_other, kv_even, swap(kv_odd, "ctx", 1)],
            [shape((2 * block, 896), bf16)] * 2,
            work=1,
        )
        attn_here, attn_send = call(
            attn_grad_pass_kernel,
            [attn_here, swap_across(attn_send, 0)],
            [shape((block, 896), bf16)] * 2,
            work=1,
        )
        mixed_grad = after(mixed_grad, attn_here)
    far_one, far_three, _ = lax.optimization_barrier((layer_one, layer_three, token))
    half = own // 2
    layer_parts = [
        layer_own,
        layer_one,
        swap(far_three[:half], "tp", 1),
        swap(far_one[half:], "tp", 3),
        layer_three,
    ]
    mixed_grad = after(mixed_grad, *layer_parts[2:4])
    input_own = call(
        last_kernel,
        [hidden_in, mixed_grad, gain_one, *one_got],
        [shape((own, width), bf16)],
    )[0]
    input_parts = gather(input_own)
    layer_parts[4] = after(layer_parts[4], input_own)
    layer_out = call(
        join_kernel,
        layer_parts,
        [shape((rows, width), bf16)],
        work=1,
    )[0]
    if near:
        feed_send = after(feed_here[block:], one_parts[0])
        feed_here = feed_here[:block]
        gate_w, up_w, down_w = call(
            feed_grad_sum_kernel,
            [after(feed_here, input_own), swap_across(feed_send, 1)],
            [shape((block, units), f32), shape((block, units), f32), shape((units, block), f32)],
            work=1,
        )
        query_w, key_w, value_w, out_w, gains = call(
            attn_grad_sum_kernel,
            [after(attn_here, input_parts[1]), swap_across(attn_send, 1)],
            [
                shape((block, 256), f32),
                shape((block, 128), f32),
                shape((block, 128), f32),
                shape((256, block), bf16),
                shape((8, 128), f32),
            ],
            work=1,
        )
        turn = []
        for a in range(n_tp):
            for b in range(2):
                for t in range(n_tp):
                    turn.append(((2 * a + b) * n_tp + t, (2 * t + b) * n_tp + a))
        out_w = lax.ppermute(out_w, ("ctx", "tp"), turn)
    else:

        def scatter(left, right, dim=0):
            grad = dot(left, right, TN).astype(bf16)
            return lax.psum_scatter(grad, "ctx", scatter_dimension=dim, tiled=True).astype(f32)

        attn_grad_all = lax.all_gather(attn_grad, "tp", axis=0, tiled=True)
        down_w = scatter(act, out_grad, 1)
        gate_w = scatter(h_two, gate_grad)
        up_w = scatter(h_two, up_grad)
        out_w = scatter(attended, attn_grad_all, 1)
        query_w = scatter(h_one, query_pre_low)
        kv_w = scatter(h_one, kv_pre_low)
        key_w, value_w = kv_w[:, :128], kv_w[:, 128:]

    if not near:
        gains = lax.psum(gains, "ctx")
        cut = lambda row: lax.dynamic_slice_in_dim(
            gains[row : row + lots].reshape(width), mine * block, block, 0
        )
        heads = jnp.concatenate([gains[2 * lots, :64], gains[2 * lots + 1, :64]])
        gains = jnp.stack([jnp.pad(cut(0), (0, 128 - block)), jnp.pad(cut(lots), (0, 128 - block)), heads])
        gains = jnp.pad(gains, ((0, 5), (0, 0)))
    gains = gains + swap(gains, "tp", 1)
    gain_one_sum, gain_two_sum, q_gain_sum, k_gain_sum, out_w = call(
        functools.partial(gain_kernel, block),
        [gains, swap(gains, "tp", 3), out_w],
        [shape((1, block), f32)] * 2 + [shape((1, 64), f32)] * 2 + [shape(out_w.shape, f32)],
        work=1,
    )
    input_parts[0] = after(input_parts[0], gate_w, layer_out, out_w)
    input_grad = call(
        join_kernel, input_parts, [shape((rows, width), f32)]
    )[0]

    return (
        layer_out,
        input_grad,
        gain_one_sum[0],
        query_w,
        key_w,
        value_w,
        q_gain_sum[0],
        k_gain_sum[0],
        out_w,
        gain_two_sum[0],
        gate_w,
        up_w,
        down_w,
    )


def solution(mesh):
    in_specs = (
        P("ctx", None),
        P(),
        P(),
        P(None, "tp"),
        P(None, "tp"),
        P(None, "tp"),
        P(),
        P(),
        P("tp", None),
        P(),
        P(None, "tp"),
        P(None, "tp"),
        P("tp", None),
        P("ctx", None),
    )
    out_specs = (
        P("ctx", None),
        P("ctx", None),
        P("ctx"),
        P("ctx", "tp"),
        P("ctx", "tp"),
        P("ctx", "tp"),
        P(),
        P(),
        P("tp", "ctx"),
        P("ctx"),
        P("ctx", "tp"),
        P("ctx", "tp"),
        P("tp", "ctx"),
    )
    return jax.shard_map(shards, mesh=mesh, in_specs=in_specs, out_specs=out_specs, check_vma=False)
```

```python
import functools
import math

import jax
import jax.numpy as jnp
import numpy as np
from jax import lax
from jax.experimental import pallas as pl
from jax.experimental.pallas import tpu as pltpu
from jax.sharding import PartitionSpec as P

norm_eps = 1e-05
rope_base = 1000000.0
f32 = jnp.float32
bf16 = jnp.bfloat16
NN = (((1,), (0,)), ((), ()))
NT = (((1,), (1,)), ((), ()))
TN = (((0,), (0,)), ((), ()))
VMEM = pl.BlockSpec(memory_space=pltpu.VMEM)
SMEM = pl.BlockSpec(memory_space=pltpu.SMEM)
megabyte = 1024 * 1024
work = 5 * 10**10


def dot(left, right, dims=NN):
    return lax.dot_general(left, right, dims, preferred_element_type=f32)


def call(body, inputs, outs, scratch=(), work=work, limit=18, **kwargs):
    in_specs = kwargs.pop("in_specs", None)
    if in_specs is None:
        in_specs = [
            SMEM if (x.dtype == jnp.int32 and x.ndim == 1) else VMEM for x in inputs
        ]
    out_specs = kwargs.pop("out_specs", [VMEM] * len(outs))
    moved = sum(x.size * x.dtype.itemsize for x in inputs) + sum(
        math.prod(o.shape) * o.dtype.itemsize for o in outs
    )
    return pl.pallas_call(
        body,
        out_shape=outs,
        in_specs=in_specs,
        out_specs=out_specs,
        scratch_shapes=list(scratch),
        compiler_params=pltpu.CompilerParams(vmem_limit_bytes=limit * megabyte),
        cost_estimate=pl.CostEstimate(flops=work, bytes_accessed=moved, transcendentals=0),
        **kwargs,
    )(*inputs)


def shape(dims, dtype):
    return jax.ShapeDtypeStruct(dims, dtype)


def lanes(x):
    return lax.broadcasted_iota(jnp.int32, x.shape, 1)


def head_mean(x):
    first = lanes(x) < 64
    low = jnp.sum(jnp.where(first, x, 0.0), axis=1, keepdims=True)
    high = jnp.sum(jnp.where(first, 0.0, x), axis=1, keepdims=True)
    return jnp.where(first, low, high) * (1.0 / 64.0)


def swap_halves(x):
    return jnp.where(lanes(x) % 64 < 32, pltpu.roll(x, 96, 1), pltpu.roll(x, 32, 1))


def head_norm(pre, gain):
    inverse = lax.rsqrt(head_mean(pre * pre) + norm_eps)
    return pre * inverse * gain


def head_norm_back(pre, gain, grads):
    inverse = lax.rsqrt(head_mean(pre * pre) + norm_eps)
    normed = pre * inverse
    scaled = grads * gain
    inner = head_mean(scaled * normed)
    return inverse * (scaled - normed * inner), grads * normed


def doc_begin(positions, starts_ref):
    begin = jnp.zeros_like(positions)
    for i in range(starts_ref.shape[0]):
        begin = jnp.where(starts_ref[i] <= positions, starts_ref[i], begin)
    return begin


def twice(gain_ref):
    return jnp.concatenate([gain_ref[...], gain_ref[...]], axis=1)


def quarter(partner, size):
    place = jnp.bitwise_xor(lax.axis_index("tp"), partner)
    return pl.ds(pl.multiple_of(place * size, size), size)


def around(refs):
    return [
        refs[0][...],
        refs[1][...],
        refs[2][...],
        jnp.concatenate([refs[3][...], refs[4][...]], axis=0),
    ]


def store_around(acc_ref, refs):
    own = refs[0].shape[0]
    half = own // 2
    for k in range(3):
        refs[k][...] = acc_ref[quarter(k, own), :].astype(bf16)
    far = acc_ref[quarter(3, own), :].astype(bf16)
    refs[3][...] = far[:half]
    refs[4][...] = far[half:]


def row_norm(x):
    return lax.rsqrt(jnp.mean(x * x, axis=1, keepdims=True) + norm_eps)


def kv_kernel(
    starts_ref, x_ref, gain_ref, wk_ref, wv_ref, freq_ref, kgain_ref, h_ref, kv_ref, kpre_ref, cos_ref, sin_ref
):
    rows = x_ref.shape[0]
    positions = lax.axis_index("ctx") * rows + lax.broadcasted_iota(jnp.int32, (rows, 128), 0)
    angles = (positions - doc_begin(positions, starts_ref)).astype(f32) * freq_ref[...]
    cosine, sine = jnp.cos(angles), jnp.sin(angles)
    sine = jnp.where(lanes(sine) % 64 < 32, -sine, sine)
    cos_ref[...] = cosine
    sin_ref[...] = sine
    x = x_ref[...].astype(f32)
    h = (x * row_norm(x) * gain_ref[...]).astype(bf16)
    h_ref[...] = h
    kpre = dot(h, wk_ref[...])
    kpre_ref[...] = kpre
    kn = head_norm(kpre, twice(kgain_ref))
    key = kn * cosine + swap_halves(kn) * sine
    kv_ref[:, :128] = key.astype(bf16)
    kv_ref[:, 128:] = dot(h, wv_ref[...]).astype(bf16)


def spread(x, half, out_ref, base, rows):
    rolled = pltpu.roll(x, 64, 1)
    keep = (lanes(x) < 64) if half == 0 else (lanes(x) >= 64)
    first, second = (x, rolled) if half == 0 else (rolled, x)
    out_ref[pl.ds(base, rows), :] = jnp.where(keep, first, 0.0).astype(bf16)
    out_ref[pl.ds(base + rows, rows), :] = jnp.where(keep, second, 0.0).astype(bf16)


def q_kernel(h_ref, wq_ref, cos_ref, sin_ref, qgain_ref, qpad_ref, qpre_ref):
    rows = h_ref.shape[0]
    qpre = dot(h_ref[...], wq_ref[...])
    qpre_ref[...] = qpre
    for half in range(2):
        qn = head_norm(qpre[:, 128 * half : 128 * half + 128], twice(qgain_ref))
        x = qn * cos_ref[...] + swap_halves(qn) * sin_ref[...]
        spread(x, half, qpad_ref, 2 * half * rows, rows)


def visit_blocks(near, rows, starts_ref, count, lists, visit, skip=None):
    mine = lax.axis_index("ctx")
    first, last = mine * rows, mine * rows + rows - 1
    first_begin, last_begin = doc_begin(first, starts_ref), doc_begin(last, starts_ref)
    for which in range(lists):

        def step(index, carry, which=which):
            block = jnp.bitwise_xor(mine, 2 * index + which) if near else index
            start = block * rows
            seen = (block <= mine) & (start + rows - 1 >= first_begin)
            whole = (block < mine) & (start >= last_begin)

            def mask():
                dims = (rows, 2 * rows)
                key_pos = lax.broadcasted_iota(jnp.int32, dims, 0) + start
                across = lax.broadcasted_iota(jnp.int32, (1, 2 * rows), 1)
                query_pos = first + jnp.where(across < rows, across, across - rows)
                return (key_pos <= query_pos) & (key_pos >= doc_begin(query_pos, starts_ref))

            pl.when(seen & whole)(lambda: visit(which, index, None))
            pl.when(seen & jnp.logical_not(whole))(lambda: visit(which, index, mask))
            if skip is not None:
                pl.when(jnp.logical_not(seen))(lambda: skip(which, index))
            return carry

        lax.fori_loop(0, count, step, 0)


def attend_kernel(near, scale, starts_ref, qpad_ref, *refs):
    lists = 2 if near else 1
    kv_refs = refs[:lists]
    o_ref, o32_ref, lse_ref, acc_ref, mass_ref = refs[lists:]
    rows = o_ref.shape[0]
    acc_ref[...] = jnp.zeros_like(acc_ref)
    mass_ref[...] = jnp.zeros_like(mass_ref)
    factor = scale * math.log2(math.e)

    def visit(which, index, mask):
        at = pl.ds(pl.multiple_of(index * rows, rows), rows)
        keys = kv_refs[which][at, :128]
        values_t = kv_refs[which][at, 128:].T
        for j in range(2):
            p = jnp.exp2(dot(keys, qpad_ref[2 * rows * j : 2 * rows * (j + 1), :], NT) * factor)
            if mask is not None:
                p = jnp.where(mask(), p, 0.0)
            mass_ref[j : j + 1, :] += jnp.sum(p, axis=0, keepdims=True)
            acc_ref[j] += dot(values_t[64 * j : 64 * j + 64, :], p.astype(bf16))

    visit_blocks(near, rows, starts_ref, kv_refs[0].shape[0] // rows, lists, visit)
    mass = mass_ref[...]
    lse_ref[...] = jnp.log2(mass)
    parts = []
    for j in range(2):
        normed = acc_ref[j] / mass[j : j + 1, :]
        parts += [normed[:, :rows], normed[:, rows:]]
    o32 = jnp.concatenate(parts, axis=0).T
    o32_ref[...] = o32
    o_ref[...] = o32.astype(bf16)


def attend_back_kernel(near, scale, n_tp, starts_ref, qpad_ref, o32_ref, lse_ref, *refs):
    lists = 2 if near else 1
    kv_refs, refs = refs[:lists], refs[lists:]
    dout_refs, refs = refs[:n_tp], refs[n_tp:]
    dq_ref, refs = refs[0], refs[1:]
    dkv_refs, refs = refs[:lists], refs[lists:]
    dout_ref, dopad_ref, dqt_ref = refs
    rows = dq_ref.shape[0]
    factor = scale * math.log2(math.e)
    for k in range(n_tp):
        dout_ref[quarter(k, rows // n_tp), :] = dout_refs[k][...].astype(f32)
    dout = dout_ref[...]
    for half in range(2):
        spread(dout[:, 128 * half : 128 * half + 128], half, dopad_ref, 2 * half * rows, rows)
    weighted = (dout * o32_ref[...]).T
    deltas = [jnp.sum(weighted[64 * h : 64 * h + 64], axis=0, keepdims=True) for h in range(4)]
    delta = [jnp.concatenate(deltas[2 * j : 2 * j + 2], axis=1) for j in range(2)]
    dqt_ref[...] = jnp.zeros_like(dqt_ref)

    def visit(which, index, mask):
        at = pl.ds(pl.multiple_of(index * rows, rows), rows)
        keys = kv_refs[which][at, :128]
        values = kv_refs[which][at, 128:]
        keys_t = keys.T
        dk = jnp.zeros((rows, 128), f32)
        dv = jnp.zeros((rows, 128), f32)
        for j in range(2):
            qpad = qpad_ref[2 * rows * j : 2 * rows * (j + 1), :]
            dopad = dopad_ref[2 * rows * j : 2 * rows * (j + 1), :]
            p = jnp.exp2(dot(keys, qpad, NT) * factor - lse_ref[j : j + 1, :])
            if mask is not None:
                p = jnp.where(mask(), p, 0.0)
            ds = (p * (dot(values, dopad, NT) - delta[j])).astype(bf16)
            dv += dot(p.astype(bf16), dopad)
            dk += dot(ds, qpad)
            dqt_ref[j] += dot(keys_t[64 * j : 64 * j + 64, :], ds)
        dkv_refs[which][at, :128] = (dk * scale).astype(bf16)
        dkv_refs[which][at, 128:] = dv.astype(bf16)

    def skip(which, index):
        at = pl.ds(pl.multiple_of(index * rows, rows), rows)
        dkv_refs[which][at, :] = jnp.zeros((rows, 256), bf16)

    visit_blocks(near, rows, starts_ref, kv_refs[0].shape[0] // rows, lists, visit, skip)
    parts = []
    for j in range(2):
        part = dqt_ref[j]
        parts += [part[:, :rows], part[:, rows:]]
    dq_ref[...] = (jnp.concatenate(parts, axis=0).T * scale).astype(bf16)


def core_halves(size):
    core = lax.axis_index("ctx") % 2
    return (
        pl.ds(pl.multiple_of(core * size, size), size),
        pl.ds(pl.multiple_of((1 - core) * size, size), size),
    )


def mix_kernel(x_ref, gain_ref, w0_ref, wm_ref, wp_ref, *refs):
    parts = around(refs[:5])
    h_ref, y_ref, acc_ref = refs[5:]
    acc = x_ref[...].astype(f32) + dot(parts[0], w0_ref[...])
    core = lax.axis_index("ctx") % 2
    half = w0_ref.shape[0] // 2
    for k in range(1, 4):
        low, high = parts[k][:, :half], parts[k][:, half:]
        acc += dot(jnp.where(core == 0, low, high), wm_ref[k - 1])
        acc += dot(jnp.where(core == 0, high, low), wp_ref[k - 1])
    acc_ref[...] = acc
    y_ref[...] = acc_ref[quarter(0, y_ref.shape[0]), :]
    h_ref[...] = (acc * row_norm(acc) * gain_ref[...]).astype(bf16)


def feed_kernel(h_ref, g_ref, wg_ref, wu_ref, wd_ref, act_ref, dg_ref, du_ref, *refs):
    dh_refs, acc_ref = refs[:5], refs[5]
    gate = dot(h_ref[...], wg_ref[...])
    up = dot(h_ref[...], wu_ref[...])
    dact = dot(g_ref[...], wd_ref[...], NT)
    sigma = jax.nn.sigmoid(gate)
    silu = gate * sigma
    act_ref[...] = (silu * up).astype(bf16)
    dgate = (dact * up * sigma * (1.0 + gate * (1.0 - sigma))).astype(bf16)
    dup = (dact * silu).astype(bf16)
    dg_ref[...] = dgate
    du_ref[...] = dup
    acc_ref[...] = dot(dgate, wg_ref[...], NT) + dot(dup, wu_ref[...], NT)
    store_around(acc_ref, dh_refs)


def reduce_kernel(one_ref, two_ref, got_one_ref, got_two_ref, to_one_ref, to_two_ref):
    half = got_one_ref.shape[0]
    to_one_ref[:half, :] = one_ref[:half, :]
    to_one_ref[half:, :] = (one_ref[half:, :].astype(f32) + got_two_ref[...].astype(f32)).astype(bf16)
    to_two_ref[:half, :] = (two_ref[:half, :].astype(f32) + got_one_ref[...].astype(f32)).astype(bf16)
    to_two_ref[half:, :] = two_ref[half:, :]


def mid_kernel(g_ref, y_ref, gain_ref, w0_ref, wm_ref, wp_ref, *refs):
    dh_refs, refs = refs[:3], refs[3:]
    dy_ref, dattn_ref, gaing_ref = refs[:3]
    dout_refs = refs[3:]
    dh = sum(ref[...].astype(f32) for ref in dh_refs)
    y = y_ref[...]
    inverse = row_norm(y)
    z = y * inverse
    gaing_ref[...] = jnp.sum(dh * z, axis=0, keepdims=True)
    e = dh * gain_ref[...]
    inner = jnp.mean(e * z, axis=1, keepdims=True)
    dy = g_ref[quarter(0, y_ref.shape[0]), :].astype(f32) + inverse * (e - z * inner)
    dy_ref[...] = dy
    low = dy.astype(bf16)
    dattn_ref[...] = low
    dout_refs[0][...] = dot(low, w0_ref[...], NT).astype(bf16)
    first, second = core_halves(w0_ref.shape[0] // 2)
    for k in range(1, 4):
        dout_refs[k][:, first] = dot(low, wm_ref[k - 1], NT).astype(bf16)
        dout_refs[k][:, second] = dot(low, wp_ref[k - 1], NT).astype(bf16)


def down_kernel(n_tp, act_ref, wd_ref, dattn_ref, *refs):
    out_refs, acc_ref = refs[:n_tp], refs[n_tp]
    own, width = dattn_ref.shape
    acc_ref[...] = dot(act_ref[...], wd_ref[...])
    for k in range(n_tp):
        out_refs[k][:, :width] = acc_ref[quarter(k, own), :].astype(bf16)
        out_refs[k][:, width:] = dattn_ref[:, quarter(k, width // n_tp)]


def layer_kernel(n_tp, y_ref, *refs):
    own, width = y_ref.shape
    out_ref, cut_ref = refs[n_tp:]
    total = y_ref[...]
    for k in range(n_tp):
        total += refs[k][:, :width].astype(f32)
        cut_ref[quarter(k, own), :] = refs[k][:, width:]
    out_ref[...] = total.astype(bf16)


def q_back_kernel(near, dq_ref, qpre_ref, cos_ref, sin_ref, qgain_ref, wq_ref, h_ref, *refs):
    if near:
        dattn_ref, parts, refs = refs[0], around(refs[1:6]), refs[6:]
        odd_ref, even_ref, hp_ref, oall_ref = refs[3:]
    low_ref, gaing_ref, dh_ref = refs[:3]
    total = jnp.zeros((1, 128), f32)
    for half in range(2):
        cut = slice(128 * half, 128 * half + 128)
        x = dq_ref[:, cut].astype(f32)
        dqn = x * cos_ref[...] - swap_halves(x) * sin_ref[...]
        dpre, weighted = head_norm_back(qpre_ref[:, cut], twice(qgain_ref), dqn)
        low_ref[:, cut] = dpre.astype(bf16)
        total += jnp.sum(weighted, axis=0, keepdims=True)
    gaing_ref[...] = total + pltpu.roll(total, 64, 1)
    dh_ref[...] = dot(low_ref[...], wq_ref[...], NT)
    if near:
        mine, place = lax.axis_index("ctx"), lax.axis_index("tp")
        for k, part in enumerate(parts):
            oall_ref[k] = part
        for parity, out_ref in ((1, odd_ref), (0, even_ref)):
            gather_columns(parity, h_ref, hp_ref)
            out_ref[:, :256] = dot(hp_ref[...], low_ref[...], TN).astype(bf16)
            left = columns(dattn_ref, jnp.bitwise_xor(mine % 2, parity)).T
            for at, chip in enumerate(block_order(parity)):
                heads = jnp.bitwise_xor(jnp.bitwise_xor(mine // 2, chip), place)
                out_ref[128 * at : 128 * at + 128, 256:] = dot(left, oall_ref[heads]).astype(bf16)


def k_back_kernel(near, n_parts, *refs):
    parts, refs = refs[:n_parts], refs[n_parts:]
    kpre_ref, cos_ref, sin_ref, kgain_ref, wk_ref, wv_ref, dhq_ref, x_ref, gain2_ref, qg_ref, h_ref = refs[:11]
    low_ref, gains_ref = refs[11:13]
    dh_refs, refs = refs[13:18], refs[18:]
    acc_ref = refs[-1]
    total = parts[0][...].astype(f32)
    for part in parts[1:]:
        total += part[...].astype(f32)
    low = total.astype(bf16)
    x = low[:, :128].astype(f32)
    dkn = x * cos_ref[...] - swap_halves(x) * sin_ref[...]
    dpre, weighted = head_norm_back(kpre_ref[...], twice(kgain_ref), dkn)
    dk = dpre.astype(bf16)
    dv = low[:, 128:]
    low_ref[:, :128] = dk
    low_ref[:, 128:] = dv
    dh = dhq_ref[...] + dot(dk, wk_ref[...], NT) + dot(dv, wv_ref[...], NT)
    acc_ref[...] = dh
    store_around(acc_ref, dh_refs)
    x_in = x_ref[...].astype(f32)
    width = x_in.shape[1]
    lots = width // 128
    gain_one = jnp.sum(dh * (x_in * row_norm(x_in)), axis=0, keepdims=True)
    for i in range(lots):
        gains_ref[i : i + 1, :] = gain_one[:, 128 * i : 128 * i + 128]
        gains_ref[lots + i : lots + i + 1, :] = gain2_ref[:, 128 * i : 128 * i + 128]
    gains = jnp.sum(weighted, axis=0, keepdims=True)
    gains_ref[2 * lots : 2 * lots + 1, :] = qg_ref[...]
    gains_ref[2 * lots + 1 : 2 * lots + 2, :] = gains + pltpu.roll(gains, 64, 1)
    gains_ref[2 * lots + 2 :, :] = jnp.zeros((gains_ref.shape[0] - 2 * lots - 2, 128), f32)
    if near:
        odd_ref, even_ref, hp_ref = refs[:3]
        mine = lax.axis_index("ctx")
        for parity, out_ref in ((1, odd_ref), (0, even_ref)):
            gather_columns(parity, h_ref, hp_ref)
            out_ref[:, :256] = dot(hp_ref[...], low_ref[...], TN).astype(bf16)
            for at, chip in enumerate(block_order(parity)):
                block = jnp.bitwise_xor(mine, 2 * chip + parity)
                out_ref[128 * at : 128 * at + 128, 256:] = parted(gain_columns(gains_ref, block, lots))


def last_kernel(x_ref, dy_ref, gain_ref, *refs):
    dh_refs, out_ref = refs[:3], refs[3]
    dh = sum(ref[...].astype(f32) for ref in dh_refs)
    x = x_ref[quarter(0, dy_ref.shape[0]), :].astype(f32)
    inverse = row_norm(x)
    z = x * inverse
    e = dh * gain_ref[...]
    inner = jnp.mean(e * z, axis=1, keepdims=True)
    out_ref[...] = (dy_ref[...] + inverse * (e - z * inner)).astype(bf16)


def join_kernel(*refs):
    out_ref = refs[5]
    for k, part in enumerate(around(refs[:5])):
        out_ref[quarter(k, part.shape[0]), :] = part.astype(out_ref.dtype)


def block_order(parity):
    core = lax.axis_index("ctx") % 2
    first, second = 1 + core, 2 - core
    return (0, first, second, 3) if parity else (0, second, first, 3)


def columns(src_ref, block):
    return src_ref[:, pl.ds(pl.multiple_of(block * 128, 128), 128)]


def gather_columns(parity, src_ref, dst_ref):
    mine = lax.axis_index("ctx")
    for place, chip in enumerate(block_order(parity)):
        dst_ref[:, 128 * place : 128 * place + 128] = columns(src_ref, jnp.bitwise_xor(mine, 2 * chip + parity))


def feed_grad_kernel(h_ref, g_ref, act_ref, dg_ref, du_ref, odd_ref, even_ref, hp_ref, gp_ref):
    units = act_ref.shape[1]
    for parity, out_ref in ((1, odd_ref), (0, even_ref)):
        gather_columns(parity, h_ref, hp_ref)
        gather_columns(parity, g_ref, gp_ref)
        for i, (left_ref, right_ref) in enumerate(((hp_ref, dg_ref), (hp_ref, du_ref), (gp_ref, act_ref))):
            out_ref[:, units * i : units * (i + 1)] = dot(left_ref[...], right_ref[...], TN).astype(bf16)


def feed_grad_sum_kernel(keep_ref, got_ref, gate_ref, up_ref, down_ref):
    units = gate_ref.shape[1]
    for i, out_ref in enumerate((gate_ref, up_ref, down_ref)):
        cut = slice(units * i, units * (i + 1))
        total = keep_ref[:, cut].astype(f32) + got_ref[:, cut].astype(f32)
        out_ref[...] = total.T if i == 2 else total


def joined(x):
    x = x.astype(f32)
    return x + pltpu.roll(x, 64, 1)


def parted(x):
    high = x.astype(bf16).astype(f32)
    return jnp.where(lanes(x) < 64, high, x - high).astype(bf16)


def gain_columns(gains_ref, block, lots):
    row = lambda i: gains_ref[pl.ds(i, 1), :]
    heads = jnp.where(lanes(row(0)) < 64, row(2 * lots), row(2 * lots + 1))
    rows = jnp.concatenate([row(block), row(lots + block), heads, jnp.zeros((125, 128), f32)], axis=0)
    total = rows.T
    return total + pltpu.roll(total, 64, 1)


def attn_grad_chip_kernel(q_ref, q_got_ref, kv_ref, kv_got_ref, here_ref, send_ref):
    half = here_ref.shape[0]
    for i, out_ref in enumerate((here_ref, send_ref)):
        row = slice(half * i, half * (i + 1))
        out_ref[:, :512] = (q_ref[row, :].astype(f32) + q_got_ref[row, :].astype(f32)).astype(bf16)
        out_ref[:, 512:768] = (kv_ref[row, :256].astype(f32) + kv_got_ref[row, :256].astype(f32)).astype(bf16)
        out_ref[:, 768:] = parted(joined(kv_ref[row, 256:]) + joined(kv_got_ref[row, 256:]))


def attn_grad_pass_kernel(keep_ref, got_ref, here_ref, send_ref):
    half = here_ref.shape[0]
    for i, out_ref in enumerate((here_ref, send_ref)):
        row = slice(half * i, half * (i + 1))
        out_ref[:, :768] = (keep_ref[row, :768].astype(f32) + got_ref[row, :768].astype(f32)).astype(bf16)
        out_ref[:, 768:] = parted(joined(keep_ref[row, 768:]) + joined(got_ref[row, 768:]))


def attn_grad_sum_kernel(keep_ref, got_ref, q_ref, k_ref, v_ref, o_ref, gains_ref):
    total = keep_ref[:, :768].astype(f32) + got_ref[:, :768].astype(f32)
    q_ref[...] = total[:, :256]
    o_ref[...] = total[:, 256:512].T.astype(bf16)
    k_ref[...] = total[:, 512:640]
    v_ref[...] = total[:, 640:]
    gains_ref[...] = (joined(keep_ref[:, 768:]) + joined(got_ref[:, 768:])).T[:8]


def gain_kernel(block, a_ref, b_ref, w_ref, one_ref, two_ref, q_ref, k_ref, out_ref):
    out_ref[...] = w_ref[...].astype(f32)
    total = a_ref[...] + b_ref[...]
    one_ref[...] = total[0:1, :block]
    two_ref[...] = total[1:2, :block]
    q_ref[...] = total[2:3, :64]
    k_ref[...] = total[2:3, 64:]


def swap(x, axis, k):
    size = lax.axis_size(axis)
    return lax.ppermute(x, axis, [(i, i ^ k) for i in range(size)])


def swap_across(x, step):
    size = lax.axis_size("ctx")
    return lax.ppermute(x, "ctx", [(i, i ^ (2 << ((i + step) % 2))) for i in range(size)])


def after(x, *first):
    return lax.optimization_barrier((x, *first))[0]


def shards(
    hidden_in,
    doc_starts,
    norm1_gain,
    w_query,
    w_key,
    w_value,
    query_gain,
    key_gain,
    w_out,
    norm2_gain,
    w_gate,
    w_up,
    w_down,
    out_grad,
):
    rows, width = hidden_in.shape
    n_ctx, n_tp = lax.axis_size("ctx"), lax.axis_size("tp")
    head_dim = query_gain.shape[0]
    scale = head_dim ** (-0.5)
    near = n_ctx == 2 * n_tp and width == 128 * n_ctx
    own = rows // n_tp
    units = w_gate.shape[1]
    others = range(1, n_tp)
    chips = range(1, n_ctx // 2)
    mine, place = lax.axis_index("ctx"), lax.axis_index("tp")
    gain_one, gain_two = norm1_gain[None, :], norm2_gain[None, :]
    q_gain, k_gain = query_gain[None, :], key_gain[None, :]
    frequency = rope_base ** (-2.0 * np.arange(head_dim // 2) / head_dim)
    frequency = jnp.asarray(np.tile(frequency, 4)[None, :], f32)

    def exchange(parts):
        return [parts[0]] + [swap(parts[k], "tp", k) for k in others]

    def gather(x, *first):
        one, two = swap(x, "tp", 1), swap(x, "tp", 2)
        half = x.shape[0] // 2
        from_one, from_two = lax.optimization_barrier((one, two, *first))[:2] if first else (one, two)
        return [x, one, two, swap(from_two[:half], "tp", 1), swap(from_one[half:], "tp", 2)]

    def reduce(parts, *first):
        here, one, two, far_low, far_high = parts
        got_one, got_two = swap(far_low, "tp", 1), swap(far_high, "tp", 2)
        if first:
            one = after(one, *first)
        to_one, to_two = call(
            reduce_kernel,
            [one, two, got_one, got_two],
            [shape(one.shape, bf16)] * 2,
            work=1,
        )
        return [here, swap(to_one, "tp", 1), swap(to_two, "tp", 2)], to_one

    quarters = [shape((own, width), bf16)] * 3 + [shape((own // 2, width), bf16)] * 2

    h_one, kv, key_pre, cosine, sine = call(
        kv_kernel,
        [doc_starts, hidden_in, gain_one, w_key, w_value, frequency, k_gain],
        [
            shape((rows, width), bf16),
            shape((rows, 256), bf16),
            shape((rows, 128), f32),
            shape((rows, 128), f32),
            shape((rows, 128), f32),
        ],
        limit=56,
    )
    if near:
        kv_got = [swap(kv, "ctx", 2 * i) for i in chips]
    else:
        kv_all = [lax.all_gather(kv, "ctx", axis=0, tiled=True)]
    half = w_out.shape[0] // 2
    w_half = lax.dynamic_slice_in_dim(w_out, (mine % 2) * half, half, 0)
    w_around = gather(w_half)
    qpad, query_pre = call(
        q_kernel,
        [h_one, w_query, cosine, sine, q_gain],
        [shape((4 * rows, 128), bf16), shape((rows, 256), f32)],
    )
    if near:
        even = jnp.concatenate([after(kv, qpad, *w_around[1:3]), *kv_got], axis=0)
        kv_all = [even, swap(even, "ctx", 1)]
    attended, attended32, log_mass = call(
        functools.partial(attend_kernel, near, scale),
        [doc_starts, qpad, *kv_all],
        [shape((rows, 256), bf16), shape((rows, 256), f32), shape((2, 2 * rows), f32)],
        [pltpu.VMEM((2, 64, 2 * rows), f32), pltpu.VMEM((2, 2 * rows), f32)],
    )
    o_parts = gather(attended)
    w_around = lax.optimization_barrier((*w_around, attended))[:5]
    w_mine = jnp.stack([*w_around[1:3], jnp.concatenate(w_around[3:], axis=0)])
    w_all = [w_mine, swap(w_mine, "ctx", 1)]
    h_two, mixed_own = call(
        mix_kernel,
        [hidden_in, gain_two, w_out, *w_all, *o_parts],
        [shape((rows, width), bf16), shape((own, width), f32)],
        [pltpu.VMEM((rows, width), f32)],
    )

    got = call(
        feed_kernel,
        [h_two, out_grad, w_gate, w_up, w_down],
        [shape((rows, units), bf16)] * 3 + quarters,
        [pltpu.VMEM((rows, width), f32)],
        limit=24,
    )
    act, gate_grad, up_grad = got[:3]
    two_parts = got[3:]
    block = width // n_ctx
    if near:
        ordered = pltpu.VMEM((rows, 4 * block), bf16)
        feed_odd, feed_even = call(
            feed_grad_kernel,
            [h_two, out_grad, act, gate_grad, up_grad],
            [shape((4 * block, 3 * units), bf16)] * 2,
            [ordered, ordered],
        )
    two_got, _ = reduce(two_parts, *([feed_even] if near else []))
    got = call(
        mid_kernel,
        [out_grad, mixed_own, gain_two, w_out, *w_all, *two_got],
        [shape((own, width), f32), shape((own, width), bf16), shape((1, width), f32)]
        + [shape((own, 256), bf16)] * n_tp,
    )
    mixed_grad, attn_grad, gain_two_part = got[:3]
    dout = exchange(got[3:])

    down = call(
        functools.partial(down_kernel, n_tp),
        [act, w_down, attn_grad],
        [shape((own, width + width // n_tp), bf16)] * n_tp,
        [pltpu.VMEM((rows, width), f32)],
    )
    if near:
        half = 2 * block
        feed_other = swap(feed_odd, "ctx", 1)
        feed_send = feed_even[half:] + feed_other[half:]
        feed_got = swap_across(feed_send, 0)
        qpad = after(qpad, feed_send, down[1])
    down_got = exchange(down)

    got = call(
        functools.partial(attend_back_kernel, near, scale, n_tp),
        [doc_starts, qpad, attended32, log_mass, *kv_all, *dout],
        [shape((rows, 256), bf16)] + [shape(x.shape, bf16) for x in kv_all],
        [
            pltpu.VMEM((rows, 256), f32),
            pltpu.VMEM((4 * rows, 128), bf16),
            pltpu.VMEM((2, 64, 2 * rows), f32),
        ],
    )
    query_low, dkv = got[0], got[1:]
    if near:
        other = swap(after(dkv[1], *down_got[1:]), "ctx", 1)
        pieces = [
            dkv[0][i * rows : (i + 1) * rows] + other[i * rows : (i + 1) * rows] for i in range(n_ctx // 2)
        ]
        kv_parts = [pieces[0]] + [swap(pieces[i], "ctx", 2 * i) for i in chips]
    else:
        kv_parts = [lax.psum_scatter(dkv[0], "ctx", scatter_dimension=0, tiled=True)]
    down_got = list(lax.optimization_barrier((*down_got, query_low))[:n_tp])
    layer_own, attn_grad_cut = call(
        functools.partial(layer_kernel, n_tp),
        [mixed_own, *down_got],
        [shape((own, width), bf16), shape((rows, width // n_tp), bf16)],
        work=1,
    )
    layer_one, layer_two = swap(layer_own, "tp", 1), swap(layer_own, "tp", 2)

    if near:
        feed_parts = lax.optimization_barrier((feed_even, feed_other, feed_got, query_low))[:3]
        feed_here = sum(x[:half].astype(f32) for x in feed_parts).astype(bf16)
        query_low = after(query_low, *pieces)
    more = [attn_grad_cut, *o_parts] if near else []
    got = call(
        functools.partial(q_back_kernel, near),
        [query_low, query_pre, cosine, sine, q_gain, w_query, h_one, *more],
        [shape((rows, 256), bf16), shape((1, 128), f32), shape((rows, width), f32)]
        + ([shape((4 * block, 512), bf16)] * 2 if near else []),
        [ordered, pltpu.VMEM((n_tp, rows, 256), bf16)] if near else [],
        work=1,
    )
    query_pre_low, q_gain_part, one_query = got[:3]
    done = [layer_one, layer_two, feed_here] if near else [layer_one, layer_two]
    if near:
        q_odd, q_even = got[3:]
        q_other = swap(q_odd, "ctx", 1)
        done.append(q_other)
    lots = width // 128
    gain_rows = 2 * lots + 8
    got = call(
        functools.partial(k_back_kernel, near, len(kv_parts)),
        [
            *kv_parts,
            after(key_pre, *done),
            cosine,
            sine,
            k_gain,
            w_key,
            w_value,
            one_query,
            hidden_in,
            gain_two_part,
            q_gain_part,
            h_one,
        ],
        [shape((rows, 256), bf16), shape((gain_rows, 128), f32)]
        + quarters
        + ([shape((4 * block, 384), bf16)] * 2 if near else []),
        ([ordered] if near else []) + [pltpu.VMEM((rows, width), f32)],
    )
    kv_pre_low, gains = got[:2]
    one_parts = got[2:7]
    one_got, token = reduce(one_parts)
    if near:
        kv_odd, kv_even = got[7:]
        kv_odd = after(kv_odd, token)
        attn_here, attn_send = call(
            attn_grad_chip_kernel,
            [q_even, q_other, kv_even, swap(kv_odd, "ctx", 1)],
            [shape((2 * block, 896), bf16)] * 2,
            work=1,
        )
        attn_here, attn_send = call(
            attn_grad_pass_kernel,
            [attn_here, swap_across(attn_send, 0)],
            [shape((block, 896), bf16)] * 2,
            work=1,
        )
        mixed_grad = after(mixed_grad, attn_here)
    far_one, far_two, _ = lax.optimization_barrier((layer_one, layer_two, token))
    half = own // 2
    layer_parts = [
        layer_own,
        layer_one,
        layer_two,
        swap(far_two[:half], "tp", 1),
        swap(far_one[half:], "tp", 2),
    ]
    mixed_grad = after(mixed_grad, *layer_parts[3:])
    input_own = call(
        last_kernel,
        [hidden_in, mixed_grad, gain_one, *one_got],
        [shape((own, width), bf16)],
    )[0]
    input_parts = gather(input_own)
    layer_parts[4] = after(layer_parts[4], input_own)
    layer_out = call(
        join_kernel,
        layer_parts,
        [shape((rows, width), bf16)],
        work=1,
    )[0]
    if near:
        feed_send = after(feed_here[block:], one_parts[0])
        feed_here = feed_here[:block]
        gate_w, up_w, down_w = call(
            feed_grad_sum_kernel,
            [after(feed_here, input_own), swap_across(feed_send, 1)],
            [shape((block, units), f32), shape((block, units), f32), shape((units, block), f32)],
            work=1,
        )
        query_w, key_w, value_w, out_w, gains = call(
            attn_grad_sum_kernel,
            [after(attn_here, input_parts[1]), swap_across(attn_send, 1)],
            [
                shape((block, 256), f32),
                shape((block, 128), f32),
                shape((block, 128), f32),
                shape((256, block), bf16),
                shape((8, 128), f32),
            ],
            work=1,
        )
        turn = []
        for a in range(n_tp):
            for b in range(2):
                for t in range(n_tp):
                    turn.append(((2 * a + b) * n_tp + t, (2 * t + b) * n_tp + a))
        out_w = lax.ppermute(out_w, ("ctx", "tp"), turn)
    else:

        def scatter(left, right, dim=0):
            grad = dot(left, right, TN).astype(bf16)
            return lax.psum_scatter(grad, "ctx", scatter_dimension=dim, tiled=True).astype(f32)

        attn_grad_all = lax.all_gather(attn_grad, "tp", axis=0, tiled=True)
        down_w = scatter(act, out_grad, 1)
        gate_w = scatter(h_two, gate_grad)
        up_w = scatter(h_two, up_grad)
        out_w = scatter(attended, attn_grad_all, 1)
        query_w = scatter(h_one, query_pre_low)
        kv_w = scatter(h_one, kv_pre_low)
        key_w, value_w = kv_w[:, :128], kv_w[:, 128:]

    if not near:
        gains = lax.psum(gains, "ctx")
        cut = lambda row: lax.dynamic_slice_in_dim(
            gains[row : row + lots].reshape(width), mine * block, block, 0
        )
        heads = jnp.concatenate([gains[2 * lots, :64], gains[2 * lots + 1, :64]])
        gains = jnp.stack([jnp.pad(cut(0), (0, 128 - block)), jnp.pad(cut(lots), (0, 128 - block)), heads])
        gains = jnp.pad(gains, ((0, 5), (0, 0)))
    gains = gains + swap(gains, "tp", 1)
    gain_one_sum, gain_two_sum, q_gain_sum, k_gain_sum, out_w = call(
        functools.partial(gain_kernel, block),
        [gains, swap(gains, "tp", 2), out_w],
        [shape((1, block), f32)] * 2 + [shape((1, 64), f32)] * 2 + [shape(out_w.shape, f32)],
        work=1,
    )
    input_parts[0] = after(input_parts[0], gate_w, layer_out)
    input_grad = call(
        join_kernel, input_parts, [shape((rows, width), f32)]
    )[0]

    return (
        layer_out,
        input_grad,
        gain_one_sum[0],
        query_w,
        key_w,
        value_w,
        q_gain_sum[0],
        k_gain_sum[0],
        out_w,
        gain_two_sum[0],
        gate_w,
        up_w,
        down_w,
    )


def solution(mesh):
    in_specs = (
        P("ctx", None),
        P(),
        P(),
        P(None, "tp"),
        P(None, "tp"),
        P(None, "tp"),
        P(),
        P(),
        P("tp", None),
        P(),
        P(None, "tp"),
        P(None, "tp"),
        P("tp", None),
        P("ctx", None),
    )
    out_specs = (
        P("ctx", None),
        P("ctx", None),
        P("ctx"),
        P("ctx", "tp"),
        P("ctx", "tp"),
        P("ctx", "tp"),
        P(),
        P(),
        P("tp", "ctx"),
        P("ctx"),
        P("ctx", "tp"),
        P("ctx", "tp"),
        P("tp", "ctx"),
    )
    return jax.shard_map(shards, mesh=mesh, in_specs=in_specs, out_specs=out_specs, check_vma=False)
```

```python
import functools
import math

import jax
import jax.numpy as jnp
import numpy as np
from jax import lax
from jax.experimental import pallas as pl
from jax.experimental.pallas import tpu as pltpu
from jax.sharding import PartitionSpec as P

norm_eps = 1e-05
rope_base = 1000000.0
f32 = jnp.float32
bf16 = jnp.bfloat16
NN = (((1,), (0,)), ((), ()))
NT = (((1,), (1,)), ((), ()))
TN = (((0,), (0,)), ((), ()))
VMEM = pl.BlockSpec(memory_space=pltpu.VMEM)
SMEM = pl.BlockSpec(memory_space=pltpu.SMEM)
megabyte = 1024 * 1024
work = 5 * 10**10


def dot(left, right, dims=NN):
    return lax.dot_general(left, right, dims, preferred_element_type=f32)


def call(body, inputs, outs, scratch=(), work=work, limit=18, **kwargs):
    in_specs = kwargs.pop("in_specs", None)
    if in_specs is None:
        in_specs = [
            SMEM if (x.dtype == jnp.int32 and x.ndim == 1) else VMEM for x in inputs
        ]
    out_specs = kwargs.pop("out_specs", [VMEM] * len(outs))
    moved = sum(x.size * x.dtype.itemsize for x in inputs) + sum(
        math.prod(o.shape) * o.dtype.itemsize for o in outs
    )
    return pl.pallas_call(
        body,
        out_shape=outs,
        in_specs=in_specs,
        out_specs=out_specs,
        scratch_shapes=list(scratch),
        compiler_params=pltpu.CompilerParams(vmem_limit_bytes=limit * megabyte),
        cost_estimate=pl.CostEstimate(flops=work, bytes_accessed=moved, transcendentals=0),
        **kwargs,
    )(*inputs)


def shape(dims, dtype):
    return jax.ShapeDtypeStruct(dims, dtype)


def lanes(x):
    return lax.broadcasted_iota(jnp.int32, x.shape, 1)


def head_mean(x):
    first = lanes(x) < 64
    low = jnp.sum(jnp.where(first, x, 0.0), axis=1, keepdims=True)
    high = jnp.sum(jnp.where(first, 0.0, x), axis=1, keepdims=True)
    return jnp.where(first, low, high) * (1.0 / 64.0)


def swap_halves(x):
    return jnp.where(lanes(x) % 64 < 32, pltpu.roll(x, 96, 1), pltpu.roll(x, 32, 1))


def head_norm(pre, gain):
    inverse = lax.rsqrt(head_mean(pre * pre) + norm_eps)
    return pre * inverse * gain


def head_norm_back(pre, gain, grads):
    inverse = lax.rsqrt(head_mean(pre * pre) + norm_eps)
    normed = pre * inverse
    scaled = grads * gain
    inner = head_mean(scaled * normed)
    return inverse * (scaled - normed * inner), grads * normed


def doc_begin(positions, starts_ref):
    begin = jnp.zeros_like(positions)
    for i in range(starts_ref.shape[0]):
        begin = jnp.where(starts_ref[i] <= positions, starts_ref[i], begin)
    return begin


def twice(gain_ref):
    return jnp.concatenate([gain_ref[...], gain_ref[...]], axis=1)


def quarter(partner, size):
    place = jnp.bitwise_xor(lax.axis_index("tp"), partner)
    return pl.ds(pl.multiple_of(place * size, size), size)


def around(refs):
    return [
        refs[0][...],
        refs[1][...],
        refs[2][...],
        jnp.concatenate([refs[3][...], refs[4][...]], axis=0),
    ]


def store_around(acc_ref, refs):
    own = refs[0].shape[0]
    half = own // 2
    for k in range(3):
        refs[k][...] = acc_ref[quarter(k, own), :].astype(bf16)
    far = acc_ref[quarter(3, own), :].astype(bf16)
    refs[3][...] = far[:half]
    refs[4][...] = far[half:]


def row_norm(x):
    return lax.rsqrt(jnp.mean(x * x, axis=1, keepdims=True) + norm_eps)


def kv_kernel(
    starts_ref, x_ref, gain_ref, wk_ref, wv_ref, freq_ref, kgain_ref, h_ref, kv_ref, kpre_ref, cos_ref, sin_ref
):
    rows = x_ref.shape[0]
    positions = lax.axis_index("ctx") * rows + lax.broadcasted_iota(jnp.int32, (rows, 128), 0)
    angles = (positions - doc_begin(positions, starts_ref)).astype(f32) * freq_ref[...]
    cosine, sine = jnp.cos(angles), jnp.sin(angles)
    sine = jnp.where(lanes(sine) % 64 < 32, -sine, sine)
    cos_ref[...] = cosine
    sin_ref[...] = sine
    x = x_ref[...].astype(f32)
    h = (x * row_norm(x) * gain_ref[...]).astype(bf16)
    h_ref[...] = h
    kpre = dot(h, wk_ref[...])
    kpre_ref[...] = kpre
    kn = head_norm(kpre, twice(kgain_ref))
    key = kn * cosine + swap_halves(kn) * sine
    kv_ref[:, :128] = key.astype(bf16)
    kv_ref[:, 128:] = dot(h, wv_ref[...]).astype(bf16)


def spread(x, half, out_ref, base, rows):
    rolled = pltpu.roll(x, 64, 1)
    keep = (lanes(x) < 64) if half == 0 else (lanes(x) >= 64)
    first, second = (x, rolled) if half == 0 else (rolled, x)
    out_ref[pl.ds(base, rows), :] = jnp.where(keep, first, 0.0).astype(bf16)
    out_ref[pl.ds(base + rows, rows), :] = jnp.where(keep, second, 0.0).astype(bf16)


def q_kernel(h_ref, wq_ref, cos_ref, sin_ref, qgain_ref, qpad_ref, qpre_ref):
    rows = h_ref.shape[0]
    qpre = dot(h_ref[...], wq_ref[...])
    qpre_ref[...] = qpre
    for half in range(2):
        qn = head_norm(qpre[:, 128 * half : 128 * half + 128], twice(qgain_ref))
        x = qn * cos_ref[...] + swap_halves(qn) * sin_ref[...]
        spread(x, half, qpad_ref, 2 * half * rows, rows)


def visit_blocks(near, rows, starts_ref, count, lists, visit, skip=None):
    mine = lax.axis_index("ctx")
    first, last = mine * rows, mine * rows + rows - 1
    first_begin, last_begin = doc_begin(first, starts_ref), doc_begin(last, starts_ref)
    for which in range(lists):

        def step(index, carry, which=which):
            block = jnp.bitwise_xor(mine, 2 * index + which) if near else index
            start = block * rows
            seen = (block <= mine) & (start + rows - 1 >= first_begin)
            whole = (block < mine) & (start >= last_begin)

            def mask():
                dims = (rows, 2 * rows)
                key_pos = lax.broadcasted_iota(jnp.int32, dims, 0) + start
                across = lax.broadcasted_iota(jnp.int32, (1, 2 * rows), 1)
                query_pos = first + jnp.where(across < rows, across, across - rows)
                return (key_pos <= query_pos) & (key_pos >= doc_begin(query_pos, starts_ref))

            pl.when(seen & whole)(lambda: visit(which, index, None))
            pl.when(seen & jnp.logical_not(whole))(lambda: visit(which, index, mask))
            if skip is not None:
                pl.when(jnp.logical_not(seen))(lambda: skip(which, index))
            return carry

        lax.fori_loop(0, count, step, 0)


def attend_kernel(near, scale, starts_ref, qpad_ref, *refs):
    lists = 2 if near else 1
    kv_refs = refs[:lists]
    o_ref, o32_ref, lse_ref, acc_ref, mass_ref = refs[lists:]
    rows = o_ref.shape[0]
    acc_ref[...] = jnp.zeros_like(acc_ref)
    mass_ref[...] = jnp.zeros_like(mass_ref)
    factor = scale * math.log2(math.e)

    def visit(which, index, mask):
        at = pl.ds(pl.multiple_of(index * rows, rows), rows)
        keys = kv_refs[which][at, :128]
        values_t = kv_refs[which][at, 128:].T
        for j in range(2):
            p = jnp.exp2(dot(keys, qpad_ref[2 * rows * j : 2 * rows * (j + 1), :], NT) * factor)
            if mask is not None:
                p = jnp.where(mask(), p, 0.0)
            mass_ref[j : j + 1, :] += jnp.sum(p, axis=0, keepdims=True)
            acc_ref[j] += dot(values_t[64 * j : 64 * j + 64, :], p.astype(bf16))

    visit_blocks(near, rows, starts_ref, kv_refs[0].shape[0] // rows, lists, visit)
    mass = mass_ref[...]
    lse_ref[...] = jnp.log2(mass)
    parts = []
    for j in range(2):
        normed = acc_ref[j] / mass[j : j + 1, :]
        parts += [normed[:, :rows], normed[:, rows:]]
    o32 = jnp.concatenate(parts, axis=0).T
    o32_ref[...] = o32
    o_ref[...] = o32.astype(bf16)


def attend_back_kernel(near, scale, n_tp, starts_ref, qpad_ref, o32_ref, lse_ref, *refs):
    lists = 2 if near else 1
    kv_refs, refs = refs[:lists], refs[lists:]
    dout_refs, refs = refs[:n_tp], refs[n_tp:]
    dq_ref, refs = refs[0], refs[1:]
    dkv_refs, refs = refs[:lists], refs[lists:]
    dout_ref, dopad_ref, dqt_ref = refs
    rows = dq_ref.shape[0]
    factor = scale * math.log2(math.e)
    for k in range(n_tp):
        dout_ref[quarter(k, rows // n_tp), :] = dout_refs[k][...].astype(f32)
    dout = dout_ref[...]
    for half in range(2):
        spread(dout[:, 128 * half : 128 * half + 128], half, dopad_ref, 2 * half * rows, rows)
    weighted = (dout * o32_ref[...]).T
    deltas = [jnp.sum(weighted[64 * h : 64 * h + 64], axis=0, keepdims=True) for h in range(4)]
    delta = [jnp.concatenate(deltas[2 * j : 2 * j + 2], axis=1) for j in range(2)]
    dqt_ref[...] = jnp.zeros_like(dqt_ref)

    def visit(which, index, mask):
        at = pl.ds(pl.multiple_of(index * rows, rows), rows)
        keys = kv_refs[which][at, :128]
        values = kv_refs[which][at, 128:]
        keys_t = keys.T
        dk = jnp.zeros((rows, 128), f32)
        dv = jnp.zeros((rows, 128), f32)
        for j in range(2):
            qpad = qpad_ref[2 * rows * j : 2 * rows * (j + 1), :]
            dopad = dopad_ref[2 * rows * j : 2 * rows * (j + 1), :]
            p = jnp.exp2(dot(keys, qpad, NT) * factor - lse_ref[j : j + 1, :])
            if mask is not None:
                p = jnp.where(mask(), p, 0.0)
            ds = (p * (dot(values, dopad, NT) - delta[j])).astype(bf16)
            dv += dot(p.astype(bf16), dopad)
            dk += dot(ds, qpad)
            dqt_ref[j] += dot(keys_t[64 * j : 64 * j + 64, :], ds)
        dkv_refs[which][at, :128] = (dk * scale).astype(bf16)
        dkv_refs[which][at, 128:] = dv.astype(bf16)

    def skip(which, index):
        at = pl.ds(pl.multiple_of(index * rows, rows), rows)
        dkv_refs[which][at, :] = jnp.zeros((rows, 256), bf16)

    visit_blocks(near, rows, starts_ref, kv_refs[0].shape[0] // rows, lists, visit, skip)
    parts = []
    for j in range(2):
        part = dqt_ref[j]
        parts += [part[:, :rows], part[:, rows:]]
    dq_ref[...] = (jnp.concatenate(parts, axis=0).T * scale).astype(bf16)


def core_halves(size):
    core = lax.axis_index("ctx") % 2
    return (
        pl.ds(pl.multiple_of(core * size, size), size),
        pl.ds(pl.multiple_of((1 - core) * size, size), size),
    )


def mix_kernel(x_ref, gain_ref, w0_ref, wm_ref, wp_ref, *refs):
    parts = around(refs[:5])
    h_ref, y_ref, acc_ref = refs[5:]
    acc = x_ref[...].astype(f32) + dot(parts[0], w0_ref[...])
    core = lax.axis_index("ctx") % 2
    half = w0_ref.shape[0] // 2
    for k in range(1, 4):
        low, high = parts[k][:, :half], parts[k][:, half:]
        acc += dot(jnp.where(core == 0, low, high), wm_ref[k - 1])
        acc += dot(jnp.where(core == 0, high, low), wp_ref[k - 1])
    acc_ref[...] = acc
    y_ref[...] = acc_ref[quarter(0, y_ref.shape[0]), :]
    h_ref[...] = (acc * row_norm(acc) * gain_ref[...]).astype(bf16)


def feed_kernel(h_ref, g_ref, wg_ref, wu_ref, wd_ref, act_ref, dg_ref, du_ref, *refs):
    dh_refs, acc_ref = refs[:5], refs[5]
    gate = dot(h_ref[...], wg_ref[...])
    up = dot(h_ref[...], wu_ref[...])
    dact = dot(g_ref[...], wd_ref[...], NT)
    sigma = jax.nn.sigmoid(gate)
    silu = gate * sigma
    act_ref[...] = (silu * up).astype(bf16)
    dgate = (dact * up * sigma * (1.0 + gate * (1.0 - sigma))).astype(bf16)
    dup = (dact * silu).astype(bf16)
    dg_ref[...] = dgate
    du_ref[...] = dup
    acc_ref[...] = dot(dgate, wg_ref[...], NT) + dot(dup, wu_ref[...], NT)
    store_around(acc_ref, dh_refs)


def reduce_kernel(one_ref, two_ref, got_one_ref, got_two_ref, *refs):
    to_one_ref, to_two_ref = refs[-2:]
    half = got_one_ref.shape[0]
    own = 2 * half
    to_one_ref[:half, :] = one_ref[:half, :]
    to_one_ref[half:own, :] = (one_ref[half:, :].astype(f32) + got_two_ref[...].astype(f32)).astype(bf16)
    to_two_ref[:half, :] = (two_ref[:half, :].astype(f32) + got_one_ref[...].astype(f32)).astype(bf16)
    to_two_ref[half:own, :] = two_ref[half:, :]
    if len(refs) > 2:
        to_one_ref[own:, :] = refs[1][:half, :]
        to_two_ref[own:, :] = refs[0][half:, :]


def mid_kernel(g_ref, y_ref, gain_ref, w0_ref, wm_ref, wp_ref, *refs):
    dh_refs, refs = refs[:3], refs[3:]
    dy_ref, dattn_ref, gaing_ref = refs[:3]
    dout_refs = refs[3:]
    dh = sum(ref[...].astype(f32) for ref in dh_refs)
    y = y_ref[...]
    inverse = row_norm(y)
    z = y * inverse
    gaing_ref[...] = jnp.sum(dh * z, axis=0, keepdims=True)
    e = dh * gain_ref[...]
    inner = jnp.mean(e * z, axis=1, keepdims=True)
    dy = g_ref[quarter(0, y_ref.shape[0]), :].astype(f32) + inverse * (e - z * inner)
    dy_ref[...] = dy
    low = dy.astype(bf16)
    dattn_ref[...] = low
    dout_refs[0][...] = dot(low, w0_ref[...], NT).astype(bf16)
    first, second = core_halves(w0_ref.shape[0] // 2)
    for k in range(1, 4):
        dout_refs[k][:, first] = dot(low, wm_ref[k - 1], NT).astype(bf16)
        dout_refs[k][:, second] = dot(low, wp_ref[k - 1], NT).astype(bf16)


def down_kernel(n_tp, act_ref, wd_ref, dattn_ref, *refs):
    out_refs, acc_ref = refs[:n_tp], refs[n_tp]
    own, width = dattn_ref.shape
    acc_ref[...] = dot(act_ref[...], wd_ref[...])
    for k in range(n_tp):
        out_refs[k][:, :width] = acc_ref[quarter(k, own), :].astype(bf16)
        out_refs[k][:, width:] = dattn_ref[:, quarter(k, width // n_tp)]


def layer_kernel(n_tp, y_ref, *refs):
    own, width = y_ref.shape
    out_ref, cut_ref = refs[n_tp:]
    total = y_ref[...]
    for k in range(n_tp):
        total += refs[k][:, :width].astype(f32)
        cut_ref[quarter(k, own), :] = refs[k][:, width:]
    out_ref[...] = total.astype(bf16)


def q_back_kernel(near, dq_ref, qpre_ref, cos_ref, sin_ref, qgain_ref, wq_ref, h_ref, *refs):
    if near:
        dattn_ref, parts, refs = refs[0], around(refs[1:6]), refs[6:]
        odd_ref, even_ref, hp_ref, oall_ref = refs[3:]
    low_ref, gaing_ref, dh_ref = refs[:3]
    total = jnp.zeros((1, 128), f32)
    for half in range(2):
        cut = slice(128 * half, 128 * half + 128)
        x = dq_ref[:, cut].astype(f32)
        dqn = x * cos_ref[...] - swap_halves(x) * sin_ref[...]
        dpre, weighted = head_norm_back(qpre_ref[:, cut], twice(qgain_ref), dqn)
        low_ref[:, cut] = dpre.astype(bf16)
        total += jnp.sum(weighted, axis=0, keepdims=True)
    gaing_ref[...] = total + pltpu.roll(total, 64, 1)
    dh_ref[...] = dot(low_ref[...], wq_ref[...], NT)
    if near:
        mine, place = lax.axis_index("ctx"), lax.axis_index("tp")
        for k, part in enumerate(parts):
            oall_ref[k] = part
        for parity, out_ref in ((1, odd_ref), (0, even_ref)):
            gather_columns(parity, h_ref, hp_ref)
            out_ref[:, :256] = dot(hp_ref[...], low_ref[...], TN).astype(bf16)
            left = columns(dattn_ref, jnp.bitwise_xor(mine % 2, parity)).T
            for at, chip in enumerate(block_order(parity)):
                heads = jnp.bitwise_xor(jnp.bitwise_xor(mine // 2, chip), place)
                out_ref[128 * at : 128 * at + 128, 256:] = dot(left, oall_ref[heads]).astype(bf16)


def k_back_kernel(near, n_parts, *refs):
    parts, refs = refs[:n_parts], refs[n_parts:]
    kpre_ref, cos_ref, sin_ref, kgain_ref, wk_ref, wv_ref, dhq_ref, x_ref, gain2_ref, qg_ref, h_ref = refs[:11]
    low_ref, gains_ref = refs[11:13]
    dh_refs, refs = refs[13:18], refs[18:]
    acc_ref = refs[-1]
    total = parts[0][...].astype(f32)
    for part in parts[1:]:
        total += part[...].astype(f32)
    low = total.astype(bf16)
    x = low[:, :128].astype(f32)
    dkn = x * cos_ref[...] - swap_halves(x) * sin_ref[...]
    dpre, weighted = head_norm_back(kpre_ref[...], twice(kgain_ref), dkn)
    dk = dpre.astype(bf16)
    dv = low[:, 128:]
    low_ref[:, :128] = dk
    low_ref[:, 128:] = dv
    dh = dhq_ref[...] + dot(dk, wk_ref[...], NT) + dot(dv, wv_ref[...], NT)
    acc_ref[...] = dh
    store_around(acc_ref, dh_refs)
    x_in = x_ref[...].astype(f32)
    width = x_in.shape[1]
    lots = width // 128
    gain_one = jnp.sum(dh * (x_in * row_norm(x_in)), axis=0, keepdims=True)
    for i in range(lots):
        gains_ref[i : i + 1, :] = gain_one[:, 128 * i : 128 * i + 128]
        gains_ref[lots + i : lots + i + 1, :] = gain2_ref[:, 128 * i : 128 * i + 128]
    gains = jnp.sum(weighted, axis=0, keepdims=True)
    gains_ref[2 * lots : 2 * lots + 1, :] = qg_ref[...]
    gains_ref[2 * lots + 1 : 2 * lots + 2, :] = gains + pltpu.roll(gains, 64, 1)
    gains_ref[2 * lots + 2 :, :] = jnp.zeros((gains_ref.shape[0] - 2 * lots - 2, 128), f32)
    if near:
        odd_ref, even_ref, hp_ref = refs[:3]
        for parity, out_ref in ((1, odd_ref), (0, even_ref)):
            gather_columns(parity, h_ref, hp_ref)
            out_ref[...] = dot(hp_ref[...], low_ref[...], TN).astype(bf16)


def last_kernel(x_ref, dy_ref, gain_ref, *refs):
    dh_refs, out_ref = refs[:3], refs[3]
    dh = sum(ref[: dy_ref.shape[0], :].astype(f32) for ref in dh_refs)
    x = x_ref[quarter(0, dy_ref.shape[0]), :].astype(f32)
    inverse = row_norm(x)
    z = x * inverse
    e = dh * gain_ref[...]
    inner = jnp.mean(e * z, axis=1, keepdims=True)
    out_ref[...] = (dy_ref[...] + inverse * (e - z * inner)).astype(bf16)


def layer_join_kernel(own_ref, one_ref, two_ref, low_ref, high_ref, out_ref):
    own = own_ref.shape[0]
    for k, ref in enumerate((own_ref, one_ref, two_ref)):
        out_ref[quarter(k, own), :] = ref[...]
    out_ref[quarter(3, own), :] = jnp.concatenate([low_ref[own:, :], high_ref[own:, :]], axis=0)


def join_kernel(*refs):
    out_ref = refs[5]
    for k, part in enumerate(around(refs[:5])):
        out_ref[quarter(k, part.shape[0]), :] = part.astype(out_ref.dtype)


def block_order(parity):
    core = lax.axis_index("ctx") % 2
    first, second = 1 + core, 2 - core
    return (0, first, second, 3) if parity else (0, second, first, 3)


def columns(src_ref, block):
    return src_ref[:, pl.ds(pl.multiple_of(block * 128, 128), 128)]


def gather_columns(parity, src_ref, dst_ref):
    mine = lax.axis_index("ctx")
    for place, chip in enumerate(block_order(parity)):
        dst_ref[:, 128 * place : 128 * place + 128] = columns(src_ref, jnp.bitwise_xor(mine, 2 * chip + parity))


def feed_grad_kernel(h_ref, g_ref, act_ref, dg_ref, du_ref, odd_ref, even_ref, hp_ref, gp_ref):
    units = act_ref.shape[1]
    for parity, out_ref in ((1, odd_ref), (0, even_ref)):
        gather_columns(parity, h_ref, hp_ref)
        gather_columns(parity, g_ref, gp_ref)
        for i, (left_ref, right_ref) in enumerate(((hp_ref, dg_ref), (hp_ref, du_ref), (gp_ref, act_ref))):
            out_ref[:, units * i : units * (i + 1)] = dot(left_ref[...], right_ref[...], TN).astype(bf16)


def feed_grad_sum_kernel(keep_ref, got_ref, gate_ref, up_ref, down_ref):
    units = gate_ref.shape[1]
    for i, out_ref in enumerate((gate_ref, up_ref, down_ref)):
        cut = slice(units * i, units * (i + 1))
        total = keep_ref[:, cut].astype(f32) + got_ref[:, cut].astype(f32)
        out_ref[...] = total.T if i == 2 else total


def attn_grad_chip_kernel(q_ref, q_got_ref, kv_ref, kv_got_ref, here_ref, send_ref):
    half = here_ref.shape[0]
    for i, out_ref in enumerate((here_ref, send_ref)):
        row = slice(half * i, half * (i + 1))
        out_ref[:, :512] = (q_ref[row, :].astype(f32) + q_got_ref[row, :].astype(f32)).astype(bf16)
        out_ref[:, 512:] = (kv_ref[row, :].astype(f32) + kv_got_ref[row, :].astype(f32)).astype(bf16)


def attn_grad_pass_kernel(keep_ref, got_ref, here_ref, send_ref):
    half = here_ref.shape[0]
    for i, out_ref in enumerate((here_ref, send_ref)):
        row = slice(half * i, half * (i + 1))
        out_ref[...] = (keep_ref[row, :].astype(f32) + got_ref[row, :].astype(f32)).astype(bf16)


def attn_grad_sum_kernel(keep_ref, got_ref, q_ref, k_ref, v_ref, o_ref):
    total = keep_ref[...].astype(f32) + got_ref[...].astype(f32)
    q_ref[...] = total[:, :256]
    o_ref[...] = total[:, 256:512].T.astype(bf16)
    k_ref[...] = total[:, 512:640]
    v_ref[...] = total[:, 640:]


def gain_kernel(block, a_ref, b_ref, w_ref, one_ref, two_ref, q_ref, k_ref, out_ref):
    out_ref[...] = w_ref[...].astype(f32)
    total = a_ref[...] + b_ref[...]
    lots = (total.shape[0] - 8) // 2
    q_ref[...] = total[2 * lots : 2 * lots + 1, :64]
    k_ref[...] = total[2 * lots + 1 : 2 * lots + 2, :64]
    mine = lax.axis_index("ctx")
    row = mine * block // 128
    at = lax.broadcasted_iota(jnp.int32, total.shape, 0)
    for i, ref in enumerate((one_ref, two_ref)):
        picked = jnp.sum(jnp.where(at == row + lots * i, total, 0.0), axis=0, keepdims=True)
        if block < 128:
            spots = lax.broadcasted_iota(jnp.int32, (128, block), 0)
            want = lax.broadcasted_iota(jnp.int32, (128, block), 1) + mine * block % 128
            picked = lax.dot_general(
                picked, (spots == want).astype(f32), NN, precision=lax.Precision.HIGHEST
            )
        ref[...] = picked


def swap(x, axis, k):
    size = lax.axis_size(axis)
    return lax.ppermute(x, axis, [(i, i ^ k) for i in range(size)])


def swap_across(x, step):
    size = lax.axis_size("ctx")
    return lax.ppermute(x, "ctx", [(i, i ^ (2 << ((i + step) % 2))) for i in range(size)])


def after(x, *first):
    return lax.optimization_barrier((x, *first))[0]


def shards(
    hidden_in,
    doc_starts,
    norm1_gain,
    w_query,
    w_key,
    w_value,
    query_gain,
    key_gain,
    w_out,
    norm2_gain,
    w_gate,
    w_up,
    w_down,
    out_grad,
):
    rows, width = hidden_in.shape
    n_ctx, n_tp = lax.axis_size("ctx"), lax.axis_size("tp")
    head_dim = query_gain.shape[0]
    scale = head_dim ** (-0.5)
    near = n_ctx == 2 * n_tp and width == 128 * n_ctx
    own = rows // n_tp
    units = w_gate.shape[1]
    others = range(1, n_tp)
    chips = range(1, n_ctx // 2)
    mine, place = lax.axis_index("ctx"), lax.axis_index("tp")
    gain_one, gain_two = norm1_gain[None, :], norm2_gain[None, :]
    q_gain, k_gain = query_gain[None, :], key_gain[None, :]
    frequency = rope_base ** (-2.0 * np.arange(head_dim // 2) / head_dim)
    frequency = jnp.asarray(np.tile(frequency, 4)[None, :], f32)

    def exchange(parts):
        return [parts[0]] + [swap(parts[k], "tp", k) for k in others]

    def gather(x, *first):
        one, two = swap(x, "tp", 1), swap(x, "tp", 2)
        half = x.shape[0] // 2
        from_one, from_two = lax.optimization_barrier((one, two, *first))[:2] if first else (one, two)
        return [x, one, two, swap(from_two[:half], "tp", 1), swap(from_one[half:], "tp", 2)]

    def reduce(parts, *first, riders=()):
        here, one, two, far_low, far_high = parts
        got_one, got_two = swap(far_low, "tp", 1), swap(far_high, "tp", 2)
        if first:
            one = after(one, *first)
        to_one, to_two = call(
            reduce_kernel,
            [one, two, got_one, got_two, *riders],
            [shape((own + (own // 2 if riders else 0), width), bf16)] * 2,
            work=1,
        )
        return [here, swap(to_one, "tp", 1), swap(to_two, "tp", 2)], to_one

    quarters = [shape((own, width), bf16)] * 3 + [shape((own // 2, width), bf16)] * 2

    h_one, kv, key_pre, cosine, sine = call(
        kv_kernel,
        [doc_starts, hidden_in, gain_one, w_key, w_value, frequency, k_gain],
        [
            shape((rows, width), bf16),
            shape((rows, 256), bf16),
            shape((rows, 128), f32),
            shape((rows, 128), f32),
            shape((rows, 128), f32),
        ],
        limit=56,
    )
    if near:
        kv_got = [swap(kv, "ctx", 2 * i) for i in chips]
    else:
        kv_all = [lax.all_gather(kv, "ctx", axis=0, tiled=True)]
    half = w_out.shape[0] // 2
    w_half = lax.dynamic_slice_in_dim(w_out, (mine % 2) * half, half, 0)
    w_around = gather(w_half)
    qpad, query_pre = call(
        q_kernel,
        [h_one, w_query, cosine, sine, q_gain],
        [shape((4 * rows, 128), bf16), shape((rows, 256), f32)],
    )
    if near:
        even = jnp.concatenate([after(kv, qpad, *w_around[1:3]), *kv_got], axis=0)
        kv_all = [even, swap(even, "ctx", 1)]
    attended, attended32, log_mass = call(
        functools.partial(attend_kernel, near, scale),
        [doc_starts, qpad, *kv_all],
        [shape((rows, 256), bf16), shape((rows, 256), f32), shape((2, 2 * rows), f32)],
        [pltpu.VMEM((2, 64, 2 * rows), f32), pltpu.VMEM((2, 2 * rows), f32)],
    )
    o_parts = gather(attended)
    w_around = lax.optimization_barrier((*w_around, attended))[:5]
    w_mine = jnp.stack([*w_around[1:3], jnp.concatenate(w_around[3:], axis=0)])
    w_all = [w_mine, swap(w_mine, "ctx", 1)]
    h_two, mixed_own = call(
        mix_kernel,
        [hidden_in, gain_two, w_out, *w_all, *o_parts],
        [shape((rows, width), bf16), shape((own, width), f32)],
        [pltpu.VMEM((rows, width), f32)],
    )

    got = call(
        feed_kernel,
        [h_two, out_grad, w_gate, w_up, w_down],
        [shape((rows, units), bf16)] * 3 + quarters,
        [pltpu.VMEM((rows, width), f32)],
        limit=24,
    )
    act, gate_grad, up_grad = got[:3]
    two_parts = got[3:]
    block = width // n_ctx
    if near:
        ordered = pltpu.VMEM((rows, 4 * block), bf16)
        feed_odd, feed_even = call(
            feed_grad_kernel,
            [h_two, out_grad, act, gate_grad, up_grad],
            [shape((4 * block, 3 * units), bf16)] * 2,
            [ordered, ordered],
        )
    two_got, _ = reduce(two_parts, *([feed_even] if near else []))
    got = call(
        mid_kernel,
        [out_grad, mixed_own, gain_two, w_out, *w_all, *two_got],
        [shape((own, width), f32), shape((own, width), bf16), shape((1, width), f32)]
        + [shape((own, 256), bf16)] * n_tp,
    )
    mixed_grad, attn_grad, gain_two_part = got[:3]
    dout = exchange(got[3:])

    down = call(
        functools.partial(down_kernel, n_tp),
        [act, w_down, attn_grad],
        [shape((own, width + width // n_tp), bf16)] * n_tp,
        [pltpu.VMEM((rows, width), f32)],
    )
    if near:
        half = 2 * block
        feed_other = swap(feed_odd, "ctx", 1)
        feed_send = feed_even[half:] + feed_other[half:]
        feed_got = swap_across(feed_send, 0)
        qpad = after(qpad, feed_send, down[1])
    down_got = exchange(down)

    got = call(
        functools.partial(attend_back_kernel, near, scale, n_tp),
        [doc_starts, qpad, attended32, log_mass, *kv_all, *dout],
        [shape((rows, 256), bf16)] + [shape(x.shape, bf16) for x in kv_all],
        [
            pltpu.VMEM((rows, 256), f32),
            pltpu.VMEM((4 * rows, 128), bf16),
            pltpu.VMEM((2, 64, 2 * rows), f32),
        ],
    )
    query_low, dkv = got[0], got[1:]
    if near:
        other = swap(after(dkv[1], *down_got[1:]), "ctx", 1)
        pieces = [
            dkv[0][i * rows : (i + 1) * rows] + other[i * rows : (i + 1) * rows] for i in range(n_ctx // 2)
        ]
        kv_parts = [pieces[0]] + [swap(pieces[i], "ctx", 2 * i) for i in chips]
    else:
        kv_parts = [lax.psum_scatter(dkv[0], "ctx", scatter_dimension=0, tiled=True)]
    down_got = list(lax.optimization_barrier((*down_got, query_low))[:n_tp])
    layer_own, attn_grad_cut = call(
        functools.partial(layer_kernel, n_tp),
        [mixed_own, *down_got],
        [shape((own, width), bf16), shape((rows, width // n_tp), bf16)],
        work=1,
    )
    layer_one, layer_two = swap(layer_own, "tp", 1), swap(layer_own, "tp", 2)

    if near:
        feed_parts = lax.optimization_barrier((feed_even, feed_other, feed_got, query_low))[:3]
        feed_here = sum(x[:half].astype(f32) for x in feed_parts).astype(bf16)
        query_low = after(query_low, *pieces)
    more = [attn_grad_cut, *o_parts] if near else []
    got = call(
        functools.partial(q_back_kernel, near),
        [query_low, query_pre, cosine, sine, q_gain, w_query, h_one, *more],
        [shape((rows, 256), bf16), shape((1, 128), f32), shape((rows, width), f32)]
        + ([shape((4 * block, 512), bf16)] * 2 if near else []),
        [ordered, pltpu.VMEM((n_tp, rows, 256), bf16)] if near else [],
        work=1,
    )
    query_pre_low, q_gain_part, one_query = got[:3]
    done = [layer_one, layer_two, feed_here] if near else [layer_one, layer_two]
    if near:
        q_odd, q_even = got[3:]
        q_other = swap(q_odd, "ctx", 1)
        done.append(q_other)
    lots = width // 128
    gain_rows = 2 * lots + 8
    got = call(
        functools.partial(k_back_kernel, near, len(kv_parts)),
        [
            *kv_parts,
            after(key_pre, *done),
            cosine,
            sine,
            k_gain,
            w_key,
            w_value,
            one_query,
            hidden_in,
            gain_two_part,
            q_gain_part,
            h_one,
        ],
        [shape((rows, 256), bf16), shape((gain_rows, 128), f32)]
        + quarters
        + ([shape((4 * block, 256), bf16)] * 2 if near else []),
        ([ordered] if near else []) + [pltpu.VMEM((rows, width), f32)],
    )
    kv_pre_low, gains = got[:2]
    one_parts = got[2:7]
    gains = gains + swap(gains, "tp", 1)
    one_got, token = reduce(one_parts, gains, riders=(layer_one, layer_two))
    gains = gains + swap(gains, "tp", 2)
    mixed_grad = after(mixed_grad, gains)
    if near:
        kv_odd, kv_even = got[7:]
        kv_odd = after(kv_odd, token)
        attn_here, attn_send = call(
            attn_grad_chip_kernel,
            [q_even, q_other, kv_even, swap(kv_odd, "ctx", 1)],
            [shape((2 * block, 768), bf16)] * 2,
            work=1,
        )
        attn_here, attn_send = call(
            attn_grad_pass_kernel,
            [attn_here, swap_across(attn_send, 0)],
            [shape((block, 768), bf16)] * 2,
            work=1,
        )
        mixed_grad = after(mixed_grad, attn_here)
    input_own = call(
        last_kernel,
        [hidden_in, mixed_grad, gain_one, *one_got],
        [shape((own, width), bf16)],
    )[0]
    gains = after(gains, input_own)
    gains = gains + swap(gains, "ctx", 1)
    gains = gains + swap(gains, "ctx", 2)
    input_parts = gather(input_own, gains)
    steps = [1 << i for i in range(2, (n_ctx - 1).bit_length())]
    for k in steps[:-1]:
        gains = gains + swap(gains, "ctx", k)
    last_gains = swap(gains, "ctx", steps[-1])
    layer_parts = [after(layer_own, input_own), layer_one, layer_two, *one_got[1:]]
    layer_out = call(
        layer_join_kernel,
        layer_parts,
        [shape((rows, width), bf16)],
        work=1,
    )[0]
    if near:
        feed_send = after(feed_here[block:], one_parts[0])
        feed_here = feed_here[:block]
        gate_w, up_w, down_w = call(
            feed_grad_sum_kernel,
            [after(feed_here, input_own), swap_across(feed_send, 1)],
            [shape((block, units), f32), shape((block, units), f32), shape((units, block), f32)],
            work=1,
        )
        query_w, key_w, value_w, out_w = call(
            attn_grad_sum_kernel,
            [after(attn_here, input_parts[1]), swap_across(attn_send, 1)],
            [
                shape((block, 256), f32),
                shape((block, 128), f32),
                shape((block, 128), f32),
                shape((256, block), bf16),
            ],
            work=1,
        )
        turn = []
        for a in range(n_tp):
            for b in range(2):
                for t in range(n_tp):
                    turn.append(((2 * a + b) * n_tp + t, (2 * t + b) * n_tp + a))
        out_w = lax.ppermute(out_w, ("ctx", "tp"), turn)
    else:

        def scatter(left, right, dim=0):
            grad = dot(left, right, TN).astype(bf16)
            return lax.psum_scatter(grad, "ctx", scatter_dimension=dim, tiled=True).astype(f32)

        attn_grad_all = lax.all_gather(attn_grad, "tp", axis=0, tiled=True)
        down_w = scatter(act, out_grad, 1)
        gate_w = scatter(h_two, gate_grad)
        up_w = scatter(h_two, up_grad)
        out_w = scatter(attended, attn_grad_all, 1)
        query_w = scatter(h_one, query_pre_low)
        kv_w = scatter(h_one, kv_pre_low)
        key_w, value_w = kv_w[:, :128], kv_w[:, 128:]

    gain_one_sum, gain_two_sum, q_gain_sum, k_gain_sum, out_w = call(
        functools.partial(gain_kernel, block),
        [gains, last_gains, out_w],
        [shape((1, block), f32)] * 2 + [shape((1, 64), f32)] * 2 + [shape(out_w.shape, f32)],
        work=1,
    )
    input_parts[0] = after(input_parts[0], gate_w, layer_out)
    input_grad = call(
        join_kernel, input_parts, [shape((rows, width), f32)]
    )[0]

    return (
        layer_out,
        input_grad,
        gain_one_sum[0],
        query_w,
        key_w,
        value_w,
        q_gain_sum[0],
        k_gain_sum[0],
        out_w,
        gain_two_sum[0],
        gate_w,
        up_w,
        down_w,
    )


def solution(mesh):
    in_specs = (
        P("ctx", None),
        P(),
        P(),
        P(None, "tp"),
        P(None, "tp"),
        P(None, "tp"),
        P(),
        P(),
        P("tp", None),
        P(),
        P(None, "tp"),
        P(None, "tp"),
        P("tp", None),
        P("ctx", None),
    )
    out_specs = (
        P("ctx", None),
        P("ctx", None),
        P("ctx"),
        P("ctx", "tp"),
        P("ctx", "tp"),
        P("ctx", "tp"),
        P(),
        P(),
        P("tp", "ctx"),
        P("ctx"),
        P("ctx", "tp"),
        P("ctx", "tp"),
        P("tp", "ctx"),
    )
    return jax.shard_map(shards, mesh=mesh, in_specs=in_specs, out_specs=out_specs, check_vma=False)
```

```python
import functools
import math

import jax
import jax.numpy as jnp
import numpy as np
from jax import lax
from jax.experimental import pallas as pl
from jax.experimental.pallas import tpu as pltpu
from jax.sharding import PartitionSpec as P

norm_eps = 1e-05
rope_base = 1000000.0
f32 = jnp.float32
bf16 = jnp.bfloat16
NN = (((1,), (0,)), ((), ()))
NT = (((1,), (1,)), ((), ()))
TN = (((0,), (0,)), ((), ()))
VMEM = pl.BlockSpec(memory_space=pltpu.VMEM)
SMEM = pl.BlockSpec(memory_space=pltpu.SMEM)
megabyte = 1024 * 1024
work = 5 * 10**10


def dot(left, right, dims=NN):
    return lax.dot_general(left, right, dims, preferred_element_type=f32)


def call(body, inputs, outs, scratch=(), work=work, limit=18, **kwargs):
    in_specs = kwargs.pop("in_specs", None)
    if in_specs is None:
        in_specs = [
            SMEM if (x.dtype == jnp.int32 and x.ndim == 1) else VMEM for x in inputs
        ]
    out_specs = kwargs.pop("out_specs", [VMEM] * len(outs))
    moved = sum(x.size * x.dtype.itemsize for x in inputs) + sum(
        math.prod(o.shape) * o.dtype.itemsize for o in outs
    )
    return pl.pallas_call(
        body,
        out_shape=outs,
        in_specs=in_specs,
        out_specs=out_specs,
        scratch_shapes=list(scratch),
        compiler_params=pltpu.CompilerParams(vmem_limit_bytes=limit * megabyte),
        cost_estimate=pl.CostEstimate(flops=work, bytes_accessed=moved, transcendentals=0),
        **kwargs,
    )(*inputs)


def shape(dims, dtype):
    return jax.ShapeDtypeStruct(dims, dtype)


def lanes(x):
    return lax.broadcasted_iota(jnp.int32, x.shape, 1)


def head_mean(x):
    first = lanes(x) < 64
    low = jnp.sum(jnp.where(first, x, 0.0), axis=1, keepdims=True)
    high = jnp.sum(jnp.where(first, 0.0, x), axis=1, keepdims=True)
    return jnp.where(first, low, high) * (1.0 / 64.0)


def swap_halves(x):
    return jnp.where(lanes(x) % 64 < 32, pltpu.roll(x, 96, 1), pltpu.roll(x, 32, 1))


def head_norm(pre, gain):
    inverse = lax.rsqrt(head_mean(pre * pre) + norm_eps)
    return pre * inverse * gain


def head_norm_back(pre, gain, grads):
    inverse = lax.rsqrt(head_mean(pre * pre) + norm_eps)
    normed = pre * inverse
    scaled = grads * gain
    inner = head_mean(scaled * normed)
    return inverse * (scaled - normed * inner), grads * normed


def doc_begin(positions, starts_ref):
    begin = jnp.zeros_like(positions)
    for i in range(starts_ref.shape[0]):
        begin = jnp.where(starts_ref[i] <= positions, starts_ref[i], begin)
    return begin


def twice(gain_ref):
    return jnp.concatenate([gain_ref[...], gain_ref[...]], axis=1)


def quarter(partner, size):
    place = jnp.bitwise_xor(lax.axis_index("tp"), partner)
    return pl.ds(pl.multiple_of(place * size, size), size)


def around(refs):
    return [
        refs[0][...],
        refs[1][...],
        refs[2][...],
        jnp.concatenate([refs[3][...], refs[4][...]], axis=0),
    ]


def store_around(acc_ref, refs):
    own = refs[0].shape[0]
    half = own // 2
    for k in range(3):
        refs[k][...] = acc_ref[quarter(k, own), :].astype(bf16)
    far = acc_ref[quarter(3, own), :].astype(bf16)
    refs[3][...] = far[:half]
    refs[4][...] = far[half:]


def row_norm(x):
    return lax.rsqrt(jnp.mean(x * x, axis=1, keepdims=True) + norm_eps)


def kv_kernel(
    starts_ref, x_ref, gain_ref, wk_ref, wv_ref, freq_ref, kgain_ref, h_ref, kv_ref, kpre_ref, cos_ref, sin_ref
):
    rows = x_ref.shape[0]
    positions = lax.axis_index("ctx") * rows + lax.broadcasted_iota(jnp.int32, (rows, 128), 0)
    angles = (positions - doc_begin(positions, starts_ref)).astype(f32) * freq_ref[...]
    cosine, sine = jnp.cos(angles), jnp.sin(angles)
    sine = jnp.where(lanes(sine) % 64 < 32, -sine, sine)
    cos_ref[...] = cosine
    sin_ref[...] = sine
    x = x_ref[...].astype(f32)
    h = (x * row_norm(x) * gain_ref[...]).astype(bf16)
    h_ref[...] = h
    kpre = dot(h, wk_ref[...])
    kpre_ref[...] = kpre
    kn = head_norm(kpre, twice(kgain_ref))
    key = kn * cosine + swap_halves(kn) * sine
    kv_ref[:, :128] = key.astype(bf16)
    kv_ref[:, 128:] = dot(h, wv_ref[...]).astype(bf16)


def spread(x, half, out_ref, base, rows):
    rolled = pltpu.roll(x, 64, 1)
    keep = (lanes(x) < 64) if half == 0 else (lanes(x) >= 64)
    first, second = (x, rolled) if half == 0 else (rolled, x)
    out_ref[pl.ds(base, rows), :] = jnp.where(keep, first, 0.0).astype(bf16)
    out_ref[pl.ds(base + rows, rows), :] = jnp.where(keep, second, 0.0).astype(bf16)


def q_kernel(h_ref, wq_ref, cos_ref, sin_ref, qgain_ref, qpad_ref, qpre_ref):
    rows = h_ref.shape[0]
    qpre = dot(h_ref[...], wq_ref[...])
    qpre_ref[...] = qpre
    for half in range(2):
        qn = head_norm(qpre[:, 128 * half : 128 * half + 128], twice(qgain_ref))
        x = qn * cos_ref[...] + swap_halves(qn) * sin_ref[...]
        spread(x, half, qpad_ref, 2 * half * rows, rows)


def visit_blocks(near, rows, starts_ref, count, lists, visit, skip=None):
    mine = lax.axis_index("ctx")
    first, last = mine * rows, mine * rows + rows - 1
    first_begin, last_begin = doc_begin(first, starts_ref), doc_begin(last, starts_ref)
    for which in range(lists):

        def step(index, carry, which=which):
            block = jnp.bitwise_xor(mine, 2 * index + which) if near else index
            start = block * rows
            seen = (block <= mine) & (start + rows - 1 >= first_begin)
            whole = (block < mine) & (start >= last_begin)

            def mask():
                dims = (rows, 2 * rows)
                key_pos = lax.broadcasted_iota(jnp.int32, dims, 0) + start
                across = lax.broadcasted_iota(jnp.int32, (1, 2 * rows), 1)
                query_pos = first + jnp.where(across < rows, across, across - rows)
                return (key_pos <= query_pos) & (key_pos >= doc_begin(query_pos, starts_ref))

            pl.when(seen & whole)(lambda: visit(which, index, None))
            pl.when(seen & jnp.logical_not(whole))(lambda: visit(which, index, mask))
            if skip is not None:
                pl.when(jnp.logical_not(seen))(lambda: skip(which, index))
            return carry

        lax.fori_loop(0, count, step, 0)


def attend_kernel(near, scale, starts_ref, qpad_ref, *refs):
    lists = 2 if near else 1
    kv_refs = refs[:lists]
    o_ref, o32_ref, lse_ref, acc_ref, mass_ref = refs[lists:]
    rows = o_ref.shape[0]
    acc_ref[...] = jnp.zeros_like(acc_ref)
    mass_ref[...] = jnp.zeros_like(mass_ref)
    factor = scale * math.log2(math.e)

    def visit(which, index, mask):
        at = pl.ds(pl.multiple_of(index * rows, rows), rows)
        keys = kv_refs[which][at, :128]
        values_t = kv_refs[which][at, 128:].T
        for j in range(2):
            p = jnp.exp2(dot(keys, qpad_ref[2 * rows * j : 2 * rows * (j + 1), :], NT) * factor)
            if mask is not None:
                p = jnp.where(mask(), p, 0.0)
            mass_ref[j : j + 1, :] += jnp.sum(p, axis=0, keepdims=True)
            acc_ref[j] += dot(values_t[64 * j : 64 * j + 64, :], p.astype(bf16))

    visit_blocks(near, rows, starts_ref, kv_refs[0].shape[0] // rows, lists, visit)
    mass = mass_ref[...]
    lse_ref[...] = jnp.log2(mass)
    parts = []
    for j in range(2):
        normed = acc_ref[j] / mass[j : j + 1, :]
        parts += [normed[:, :rows], normed[:, rows:]]
    o32 = jnp.concatenate(parts, axis=0).T
    o32_ref[...] = o32
    o_ref[...] = o32.astype(bf16)


def attend_back_kernel(near, scale, n_tp, starts_ref, qpad_ref, o32_ref, lse_ref, *refs):
    lists = 2 if near else 1
    kv_refs, refs = refs[:lists], refs[lists:]
    dout_refs, refs = refs[:n_tp], refs[n_tp:]
    dq_ref, refs = refs[0], refs[1:]
    dkv_refs, refs = refs[:lists], refs[lists:]
    dout_ref, dopad_ref, dqt_ref = refs
    rows = dq_ref.shape[0]
    factor = scale * math.log2(math.e)
    for k in range(n_tp):
        dout_ref[quarter(k, rows // n_tp), :] = dout_refs[k][...].astype(f32)
    dout = dout_ref[...]
    for half in range(2):
        spread(dout[:, 128 * half : 128 * half + 128], half, dopad_ref, 2 * half * rows, rows)
    weighted = (dout * o32_ref[...]).T
    deltas = [jnp.sum(weighted[64 * h : 64 * h + 64], axis=0, keepdims=True) for h in range(4)]
    delta = [jnp.concatenate(deltas[2 * j : 2 * j + 2], axis=1) for j in range(2)]
    dqt_ref[...] = jnp.zeros_like(dqt_ref)

    def visit(which, index, mask):
        at = pl.ds(pl.multiple_of(index * rows, rows), rows)
        keys = kv_refs[which][at, :128]
        values = kv_refs[which][at, 128:]
        keys_t = keys.T
        dk = jnp.zeros((rows, 128), f32)
        dv = jnp.zeros((rows, 128), f32)
        for j in range(2):
            qpad = qpad_ref[2 * rows * j : 2 * rows * (j + 1), :]
            dopad = dopad_ref[2 * rows * j : 2 * rows * (j + 1), :]
            p = jnp.exp2(dot(keys, qpad, NT) * factor - lse_ref[j : j + 1, :])
            if mask is not None:
                p = jnp.where(mask(), p, 0.0)
            ds = (p * (dot(values, dopad, NT) - delta[j])).astype(bf16)
            dv += dot(p.astype(bf16), dopad)
            dk += dot(ds, qpad)
            dqt_ref[j] += dot(keys_t[64 * j : 64 * j + 64, :], ds)
        dkv_refs[which][at, :128] = (dk * scale).astype(bf16)
        dkv_refs[which][at, 128:] = dv.astype(bf16)

    def skip(which, index):
        at = pl.ds(pl.multiple_of(index * rows, rows), rows)
        dkv_refs[which][at, :] = jnp.zeros((rows, 256), bf16)

    visit_blocks(near, rows, starts_ref, kv_refs[0].shape[0] // rows, lists, visit, skip)
    parts = []
    for j in range(2):
        part = dqt_ref[j]
        parts += [part[:, :rows], part[:, rows:]]
    dq_ref[...] = (jnp.concatenate(parts, axis=0).T * scale).astype(bf16)


def core_halves(size):
    core = lax.axis_index("ctx") % 2
    return (
        pl.ds(pl.multiple_of(core * size, size), size),
        pl.ds(pl.multiple_of((1 - core) * size, size), size),
    )


def mix_kernel(x_ref, gain_ref, w0_ref, wm_ref, wp_ref, *refs):
    parts = around(refs[:5])
    h_ref, y_ref, acc_ref = refs[5:]
    acc = x_ref[...].astype(f32) + dot(parts[0], w0_ref[...])
    core = lax.axis_index("ctx") % 2
    half = w0_ref.shape[0] // 2
    for k in range(1, 4):
        low, high = parts[k][:, :half], parts[k][:, half:]
        acc += dot(jnp.where(core == 0, low, high), wm_ref[k - 1])
        acc += dot(jnp.where(core == 0, high, low), wp_ref[k - 1])
    acc_ref[...] = acc
    y_ref[...] = acc_ref[quarter(0, y_ref.shape[0]), :]
    h_ref[...] = (acc * row_norm(acc) * gain_ref[...]).astype(bf16)


def feed_kernel(h_ref, g_ref, wg_ref, wu_ref, wd_ref, act_ref, dg_ref, du_ref, *refs):
    dh_refs, acc_ref = refs[:5], refs[5]
    gate = dot(h_ref[...], wg_ref[...])
    up = dot(h_ref[...], wu_ref[...])
    dact = dot(g_ref[...], wd_ref[...], NT)
    sigma = jax.nn.sigmoid(gate)
    silu = gate * sigma
    act_ref[...] = (silu * up).astype(bf16)
    dgate = (dact * up * sigma * (1.0 + gate * (1.0 - sigma))).astype(bf16)
    dup = (dact * silu).astype(bf16)
    dg_ref[...] = dgate
    du_ref[...] = dup
    acc_ref[...] = dot(dgate, wg_ref[...], NT) + dot(dup, wu_ref[...], NT)
    store_around(acc_ref, dh_refs)


def reduce_kernel(one_ref, two_ref, got_one_ref, got_two_ref, *refs):
    to_one_ref, to_two_ref = refs[-2:]
    half = got_one_ref.shape[0]
    own = 2 * half
    to_one_ref[:half, :] = one_ref[:half, :]
    to_one_ref[half:own, :] = (one_ref[half:, :].astype(f32) + got_two_ref[...].astype(f32)).astype(bf16)
    to_two_ref[:half, :] = (two_ref[:half, :].astype(f32) + got_one_ref[...].astype(f32)).astype(bf16)
    to_two_ref[half:own, :] = two_ref[half:, :]
    if len(refs) > 2:
        to_one_ref[own:, :] = refs[1][:half, :]
        to_two_ref[own:, :] = refs[0][half:, :]


def mid_kernel(g_ref, y_ref, gain_ref, w0_ref, wm_ref, wp_ref, *refs):
    dh_refs, refs = refs[:3], refs[3:]
    dy_ref, dattn_ref, gaing_ref = refs[:3]
    dout_refs = refs[3:]
    dh = sum(ref[...].astype(f32) for ref in dh_refs)
    y = y_ref[...]
    inverse = row_norm(y)
    z = y * inverse
    gaing_ref[...] = jnp.sum(dh * z, axis=0, keepdims=True)
    e = dh * gain_ref[...]
    inner = jnp.mean(e * z, axis=1, keepdims=True)
    dy = g_ref[quarter(0, y_ref.shape[0]), :].astype(f32) + inverse * (e - z * inner)
    dy_ref[...] = dy
    low = dy.astype(bf16)
    dattn_ref[...] = low
    dout_refs[0][...] = dot(low, w0_ref[...], NT).astype(bf16)
    first, second = core_halves(w0_ref.shape[0] // 2)
    for k in range(1, 4):
        dout_refs[k][:, first] = dot(low, wm_ref[k - 1], NT).astype(bf16)
        dout_refs[k][:, second] = dot(low, wp_ref[k - 1], NT).astype(bf16)


def down_kernel(n_tp, act_ref, wd_ref, dattn_ref, *refs):
    out_refs, acc_ref = refs[:n_tp], refs[n_tp]
    own, width = dattn_ref.shape
    acc_ref[...] = dot(act_ref[...], wd_ref[...])
    for k in range(n_tp):
        out_refs[k][:, :width] = acc_ref[quarter(k, own), :].astype(bf16)
        out_refs[k][:, width:] = dattn_ref[:, quarter(k, width // n_tp)]


def layer_kernel(n_tp, y_ref, *refs):
    own, width = y_ref.shape
    out_ref, cut_ref = refs[n_tp:]
    total = y_ref[...]
    for k in range(n_tp):
        total += refs[k][:, :width].astype(f32)
        cut_ref[quarter(k, own), :] = refs[k][:, width:]
    out_ref[...] = total.astype(bf16)


def q_back_kernel(near, dq_ref, qpre_ref, cos_ref, sin_ref, qgain_ref, wq_ref, h_ref, *refs):
    if near:
        dattn_ref, parts, refs = refs[0], around(refs[1:6]), refs[6:]
        odd_ref, even_ref, hp_ref, oall_ref = refs[3:]
    low_ref, gaing_ref, dh_ref = refs[:3]
    total = jnp.zeros((1, 128), f32)
    for half in range(2):
        cut = slice(128 * half, 128 * half + 128)
        x = dq_ref[:, cut].astype(f32)
        dqn = x * cos_ref[...] - swap_halves(x) * sin_ref[...]
        dpre, weighted = head_norm_back(qpre_ref[:, cut], twice(qgain_ref), dqn)
        low_ref[:, cut] = dpre.astype(bf16)
        total += jnp.sum(weighted, axis=0, keepdims=True)
    gaing_ref[...] = total + pltpu.roll(total, 64, 1)
    dh_ref[...] = dot(low_ref[...], wq_ref[...], NT)
    if near:
        mine, place = lax.axis_index("ctx"), lax.axis_index("tp")
        for k, part in enumerate(parts):
            oall_ref[k] = part
        for parity, out_ref in ((1, odd_ref), (0, even_ref)):
            gather_columns(parity, h_ref, hp_ref)
            out_ref[:, :256] = dot(hp_ref[...], low_ref[...], TN).astype(bf16)
            left = columns(dattn_ref, jnp.bitwise_xor(mine % 2, parity)).T
            for at, chip in enumerate(block_order(parity)):
                heads = jnp.bitwise_xor(jnp.bitwise_xor(mine // 2, chip), place)
                out_ref[128 * at : 128 * at + 128, 256:] = dot(left, oall_ref[heads]).astype(bf16)


def k_back_kernel(near, n_parts, *refs):
    parts, refs = refs[:n_parts], refs[n_parts:]
    kpre_ref, cos_ref, sin_ref, kgain_ref, wk_ref, wv_ref, dhq_ref, x_ref, gain2_ref, qg_ref, h_ref = refs[:11]
    low_ref, gains_ref = refs[11:13]
    dh_refs, refs = refs[13:18], refs[18:]
    acc_ref = refs[-1]
    total = parts[0][...].astype(f32)
    for part in parts[1:]:
        total += part[...].astype(f32)
    low = total.astype(bf16)
    x = low[:, :128].astype(f32)
    dkn = x * cos_ref[...] - swap_halves(x) * sin_ref[...]
    dpre, weighted = head_norm_back(kpre_ref[...], twice(kgain_ref), dkn)
    dk = dpre.astype(bf16)
    dv = low[:, 128:]
    low_ref[:, :128] = dk
    low_ref[:, 128:] = dv
    dh = dhq_ref[...] + dot(dk, wk_ref[...], NT) + dot(dv, wv_ref[...], NT)
    acc_ref[...] = dh
    store_around(acc_ref, dh_refs)
    x_in = x_ref[...].astype(f32)
    width = x_in.shape[1]
    lots = width // 128
    gain_one = jnp.sum(dh * (x_in * row_norm(x_in)), axis=0, keepdims=True)
    for i in range(lots):
        gains_ref[i : i + 1, :] = gain_one[:, 128 * i : 128 * i + 128]
        gains_ref[lots + i : lots + i + 1, :] = gain2_ref[:, 128 * i : 128 * i + 128]
    gains = jnp.sum(weighted, axis=0, keepdims=True)
    gains_ref[2 * lots : 2 * lots + 1, :] = qg_ref[...]
    gains_ref[2 * lots + 1 : 2 * lots + 2, :] = gains + pltpu.roll(gains, 64, 1)
    gains_ref[2 * lots + 2 :, :] = jnp.zeros((gains_ref.shape[0] - 2 * lots - 2, 128), f32)
    if near:
        odd_ref, even_ref, hp_ref = refs[:3]
        for parity, out_ref in ((1, odd_ref), (0, even_ref)):
            gather_columns(parity, h_ref, hp_ref)
            out_ref[...] = dot(hp_ref[...], low_ref[...], TN).astype(bf16)


def last_kernel(x_ref, dy_ref, gain_ref, *refs):
    dh_refs, out_ref = refs[:3], refs[3]
    dh = sum(ref[: dy_ref.shape[0], :].astype(f32) for ref in dh_refs)
    x = x_ref[quarter(0, dy_ref.shape[0]), :].astype(f32)
    inverse = row_norm(x)
    z = x * inverse
    e = dh * gain_ref[...]
    inner = jnp.mean(e * z, axis=1, keepdims=True)
    out_ref[...] = (dy_ref[...] + inverse * (e - z * inner)).astype(bf16)


def layer_join_kernel(own_ref, one_ref, two_ref, low_ref, high_ref, out_ref):
    own = own_ref.shape[0]
    for k, ref in enumerate((own_ref, one_ref, two_ref)):
        out_ref[quarter(k, own), :] = ref[...]
    out_ref[quarter(3, own), :] = jnp.concatenate([low_ref[own:, :], high_ref[own:, :]], axis=0)


def join_kernel(*refs):
    out_ref = refs[5]
    for k, part in enumerate(around(refs[:5])):
        out_ref[quarter(k, part.shape[0]), :] = part.astype(out_ref.dtype)


def block_order(parity):
    core = lax.axis_index("ctx") % 2
    first, second = 1 + core, 2 - core
    return (0, first, second, 3) if parity else (0, second, first, 3)


def columns(src_ref, block):
    return src_ref[:, pl.ds(pl.multiple_of(block * 128, 128), 128)]


def gather_columns(parity, src_ref, dst_ref):
    mine = lax.axis_index("ctx")
    for place, chip in enumerate(block_order(parity)):
        dst_ref[:, 128 * place : 128 * place + 128] = columns(src_ref, jnp.bitwise_xor(mine, 2 * chip + parity))


def feed_grad_kernel(h_ref, g_ref, act_ref, dg_ref, du_ref, odd_ref, even_ref, hp_ref, gp_ref):
    units = act_ref.shape[1]
    for parity, out_ref in ((1, odd_ref), (0, even_ref)):
        gather_columns(parity, h_ref, hp_ref)
        gather_columns(parity, g_ref, gp_ref)
        for i, (left_ref, right_ref) in enumerate(((hp_ref, dg_ref), (hp_ref, du_ref), (gp_ref, act_ref))):
            out_ref[:, units * i : units * (i + 1)] = dot(left_ref[...], right_ref[...], TN).astype(bf16)


def feed_grad_sum_kernel(keep_ref, got_ref, gate_ref, up_ref, down_ref):
    units = gate_ref.shape[1]
    for i, out_ref in enumerate((gate_ref, up_ref, down_ref)):
        cut = slice(units * i, units * (i + 1))
        total = keep_ref[:, cut].astype(f32) + got_ref[:, cut].astype(f32)
        out_ref[...] = total.T if i == 2 else total


def attn_grad_chip_kernel(q_ref, q_got_ref, kv_ref, kv_got_ref, here_ref, send_ref):
    half = here_ref.shape[0]
    for i, out_ref in enumerate((here_ref, send_ref)):
        row = slice(half * i, half * (i + 1))
        out_ref[:, :512] = (q_ref[row, :].astype(f32) + q_got_ref[row, :].astype(f32)).astype(bf16)
        out_ref[:, 512:] = (kv_ref[row, :].astype(f32) + kv_got_ref[row, :].astype(f32)).astype(bf16)


def attn_grad_pass_kernel(keep_ref, got_ref, here_ref, send_ref):
    half = here_ref.shape[0]
    for i, out_ref in enumerate((here_ref, send_ref)):
        row = slice(half * i, half * (i + 1))
        out_ref[...] = (keep_ref[row, :].astype(f32) + got_ref[row, :].astype(f32)).astype(bf16)


def attn_grad_sum_kernel(keep_ref, got_ref, q_ref, k_ref, v_ref, o_ref):
    total = keep_ref[...].astype(f32) + got_ref[...].astype(f32)
    q_ref[...] = total[:, :256]
    o_ref[...] = total[:, 256:512].T.astype(bf16)
    k_ref[...] = total[:, 512:640]
    v_ref[...] = total[:, 640:]


def gain_kernel(block, a_ref, b_ref, w_ref, one_ref, two_ref, q_ref, k_ref, out_ref):
    out_ref[...] = w_ref[...].astype(f32)
    total = a_ref[...] + b_ref[...]
    lots = (total.shape[0] - 8) // 2
    q_ref[...] = total[2 * lots : 2 * lots + 1, :64]
    k_ref[...] = total[2 * lots + 1 : 2 * lots + 2, :64]
    mine = lax.axis_index("ctx")
    row = mine * block // 128
    at = lax.broadcasted_iota(jnp.int32, total.shape, 0)
    for i, ref in enumerate((one_ref, two_ref)):
        picked = jnp.sum(jnp.where(at == row + lots * i, total, 0.0), axis=0, keepdims=True)
        if block < 128:
            spots = lax.broadcasted_iota(jnp.int32, (128, block), 0)
            want = lax.broadcasted_iota(jnp.int32, (128, block), 1) + mine * block % 128
            picked = lax.dot_general(
                picked, (spots == want).astype(f32), NN, precision=lax.Precision.HIGHEST
            )
        ref[...] = picked


def swap(x, axis, k):
    size = lax.axis_size(axis)
    return lax.ppermute(x, axis, [(i, i ^ k) for i in range(size)])


def swap_across(x, step):
    size = lax.axis_size("ctx")
    return lax.ppermute(x, "ctx", [(i, i ^ (2 << ((i + step) % 2))) for i in range(size)])


def after(x, *first):
    return lax.optimization_barrier((x, *first))[0]


def shards(
    hidden_in,
    doc_starts,
    norm1_gain,
    w_query,
    w_key,
    w_value,
    query_gain,
    key_gain,
    w_out,
    norm2_gain,
    w_gate,
    w_up,
    w_down,
    out_grad,
):
    rows, width = hidden_in.shape
    n_ctx, n_tp = lax.axis_size("ctx"), lax.axis_size("tp")
    head_dim = query_gain.shape[0]
    scale = head_dim ** (-0.5)
    near = n_ctx == 2 * n_tp and width == 128 * n_ctx
    own = rows // n_tp
    units = w_gate.shape[1]
    others = range(1, n_tp)
    chips = range(1, n_ctx // 2)
    mine, place = lax.axis_index("ctx"), lax.axis_index("tp")
    gain_one, gain_two = norm1_gain[None, :], norm2_gain[None, :]
    q_gain, k_gain = query_gain[None, :], key_gain[None, :]
    frequency = rope_base ** (-2.0 * np.arange(head_dim // 2) / head_dim)
    frequency = jnp.asarray(np.tile(frequency, 4)[None, :], f32)

    def exchange(parts):
        return [parts[0]] + [swap(parts[k], "tp", k) for k in others]

    def gather(x, *first):
        one, two = swap(x, "tp", 1), swap(x, "tp", 2)
        half = x.shape[0] // 2
        from_one, from_two = lax.optimization_barrier((one, two, *first))[:2] if first else (one, two)
        return [x, one, two, swap(from_two[:half], "tp", 1), swap(from_one[half:], "tp", 2)]

    def reduce(parts, *first, riders=()):
        here, one, two, far_low, far_high = parts
        got_one, got_two = swap(far_low, "tp", 1), swap(far_high, "tp", 2)
        if first:
            one = after(one, *first)
        to_one, to_two = call(
            reduce_kernel,
            [one, two, got_one, got_two, *riders],
            [shape((own + (own // 2 if riders else 0), width), bf16)] * 2,
            work=1,
        )
        return [here, swap(to_one, "tp", 1), swap(to_two, "tp", 2)], to_one

    quarters = [shape((own, width), bf16)] * 3 + [shape((own // 2, width), bf16)] * 2

    h_one, kv, key_pre, cosine, sine = call(
        kv_kernel,
        [doc_starts, hidden_in, gain_one, w_key, w_value, frequency, k_gain],
        [
            shape((rows, width), bf16),
            shape((rows, 256), bf16),
            shape((rows, 128), f32),
            shape((rows, 128), f32),
            shape((rows, 128), f32),
        ],
        limit=56,
    )
    if near:
        kv_got = [swap(kv, "ctx", 2 * i) for i in chips]
    else:
        kv_all = [lax.all_gather(kv, "ctx", axis=0, tiled=True)]
    half = w_out.shape[0] // 2
    w_half = lax.dynamic_slice_in_dim(w_out, (mine % 2) * half, half, 0)
    w_around = gather(w_half)
    qpad, query_pre = call(
        q_kernel,
        [h_one, w_query, cosine, sine, q_gain],
        [shape((4 * rows, 128), bf16), shape((rows, 256), f32)],
    )
    if near:
        even = jnp.concatenate([after(kv, qpad, *w_around[1:3]), *kv_got], axis=0)
        kv_all = [even, swap(even, "ctx", 1)]
    attended, attended32, log_mass = call(
        functools.partial(attend_kernel, near, scale),
        [doc_starts, qpad, *kv_all],
        [shape((rows, 256), bf16), shape((rows, 256), f32), shape((2, 2 * rows), f32)],
        [pltpu.VMEM((2, 64, 2 * rows), f32), pltpu.VMEM((2, 2 * rows), f32)],
    )
    o_parts = gather(attended)
    w_around = lax.optimization_barrier((*w_around, attended))[:5]
    w_mine = jnp.stack([*w_around[1:3], jnp.concatenate(w_around[3:], axis=0)])
    w_all = [w_mine, swap(w_mine, "ctx", 1)]
    h_two, mixed_own = call(
        mix_kernel,
        [hidden_in, gain_two, w_out, *w_all, *o_parts],
        [shape((rows, width), bf16), shape((own, width), f32)],
        [pltpu.VMEM((rows, width), f32)],
    )

    got = call(
        feed_kernel,
        [h_two, out_grad, w_gate, w_up, w_down],
        [shape((rows, units), bf16)] * 3 + quarters,
        [pltpu.VMEM((rows, width), f32)],
        limit=24,
    )
    act, gate_grad, up_grad = got[:3]
    two_parts = got[3:]
    block = width // n_ctx
    if near:
        ordered = pltpu.VMEM((rows, 4 * block), bf16)
        feed_odd, feed_even = call(
            feed_grad_kernel,
            [h_two, out_grad, act, gate_grad, up_grad],
            [shape((4 * block, 3 * units), bf16)] * 2,
            [ordered, ordered],
        )
    two_got, _ = reduce(two_parts, *([feed_even] if near else []))
    got = call(
        mid_kernel,
        [out_grad, mixed_own, gain_two, w_out, *w_all, *two_got],
        [shape((own, width), f32), shape((own, width), bf16), shape((1, width), f32)]
        + [shape((own, 256), bf16)] * n_tp,
    )
    mixed_grad, attn_grad, gain_two_part = got[:3]
    dout = exchange(got[3:])

    down = call(
        functools.partial(down_kernel, n_tp),
        [act, w_down, attn_grad],
        [shape((own, width + width // n_tp), bf16)] * n_tp,
        [pltpu.VMEM((rows, width), f32)],
    )
    if near:
        half = 2 * block
        feed_other = swap(feed_odd, "ctx", 1)
        feed_send = feed_even[half:] + feed_other[half:]
        feed_got = swap_across(feed_send, 0)
        qpad = after(qpad, feed_send, down[1])
    down_got = exchange(down)

    got = call(
        functools.partial(attend_back_kernel, near, scale, n_tp),
        [doc_starts, qpad, attended32, log_mass, *kv_all, *dout],
        [shape((rows, 256), bf16)] + [shape(x.shape, bf16) for x in kv_all],
        [
            pltpu.VMEM((rows, 256), f32),
            pltpu.VMEM((4 * rows, 128), bf16),
            pltpu.VMEM((2, 64, 2 * rows), f32),
        ],
    )
    query_low, dkv = got[0], got[1:]
    if near:
        other = swap(after(dkv[1], *down_got[1:]), "ctx", 1)
        pieces = [
            dkv[0][i * rows : (i + 1) * rows] + other[i * rows : (i + 1) * rows] for i in range(n_ctx // 2)
        ]
        kv_parts = [pieces[0]] + [swap(pieces[i], "ctx", 2 * i) for i in chips]
    else:
        kv_parts = [lax.psum_scatter(dkv[0], "ctx", scatter_dimension=0, tiled=True)]
    down_got = list(lax.optimization_barrier((*down_got, query_low))[:n_tp])
    layer_own, attn_grad_cut = call(
        functools.partial(layer_kernel, n_tp),
        [mixed_own, *down_got],
        [shape((own, width), bf16), shape((rows, width // n_tp), bf16)],
        work=1,
    )
    layer_one, layer_two = swap(layer_own, "tp", 1), swap(layer_own, "tp", 2)

    if near:
        feed_parts = lax.optimization_barrier((feed_even, feed_other, feed_got, query_low))[:3]
        feed_here = sum(x[:half].astype(f32) for x in feed_parts).astype(bf16)
        query_low = after(query_low, *pieces)
    more = [attn_grad_cut, *o_parts] if near else []
    got = call(
        functools.partial(q_back_kernel, near),
        [query_low, query_pre, cosine, sine, q_gain, w_query, h_one, *more],
        [shape((rows, 256), bf16), shape((1, 128), f32), shape((rows, width), f32)]
        + ([shape((4 * block, 512), bf16)] * 2 if near else []),
        [ordered, pltpu.VMEM((n_tp, rows, 256), bf16)] if near else [],
        work=1,
    )
    query_pre_low, q_gain_part, one_query = got[:3]
    done = [layer_one, layer_two, feed_here] if near else [layer_one, layer_two]
    if near:
        q_odd, q_even = got[3:]
        q_other = swap(q_odd, "ctx", 1)
        done.append(q_other)
    lots = width // 128
    gain_rows = 2 * lots + 8
    got = call(
        functools.partial(k_back_kernel, near, len(kv_parts)),
        [
            *kv_parts,
            after(key_pre, *done),
            cosine,
            sine,
            k_gain,
            w_key,
            w_value,
            one_query,
            hidden_in,
            gain_two_part,
            q_gain_part,
            h_one,
        ],
        [shape((rows, 256), bf16), shape((gain_rows, 128), f32)]
        + quarters
        + ([shape((4 * block, 256), bf16)] * 2 if near else []),
        ([ordered] if near else []) + [pltpu.VMEM((rows, width), f32)],
    )
    kv_pre_low, gains = got[:2]
    one_parts = got[2:7]
    gains = gains + swap(gains, "tp", 1)
    one_got, token = reduce(one_parts, gains, riders=(layer_one, layer_two))
    gains = gains + swap(gains, "tp", 2)
    mixed_grad = after(mixed_grad, gains)
    if near:
        kv_odd, kv_even = got[7:]
        kv_odd = after(kv_odd, token)
        attn_here, attn_send = call(
            attn_grad_chip_kernel,
            [q_even, q_other, kv_even, swap(kv_odd, "ctx", 1)],
            [shape((2 * block, 768), bf16)] * 2,
            work=1,
        )
        attn_here, attn_send = call(
            attn_grad_pass_kernel,
            [attn_here, swap_across(attn_send, 0)],
            [shape((block, 768), bf16)] * 2,
            work=1,
        )
        mixed_grad = after(mixed_grad, attn_here)
    input_own = call(
        last_kernel,
        [hidden_in, mixed_grad, gain_one, *one_got],
        [shape((own, width), bf16)],
    )[0]
    gains = after(gains, input_own)
    gains = gains + swap(gains, "ctx", 1)
    gains = gains + swap(gains, "ctx", 2)
    input_parts = gather(input_own, gains)
    steps = [1 << i for i in range(2, (n_ctx - 1).bit_length())]
    for k in steps[:-1]:
        gains = gains + swap(gains, "ctx", k)
    last_gains = swap(gains, "ctx", steps[-1])
    layer_parts = [after(layer_own, input_own), layer_one, layer_two, *one_got[1:]]
    layer_out = call(
        layer_join_kernel,
        layer_parts,
        [shape((rows, width), bf16)],
        work=1,
    )[0]
    if near:
        feed_send = after(feed_here[block:], one_parts[0])
        feed_here = feed_here[:block]
        gate_w, up_w, down_w = call(
            feed_grad_sum_kernel,
            [after(feed_here, input_own), swap_across(feed_send, 1)],
            [shape((block, units), f32), shape((block, units), f32), shape((units, block), f32)],
            work=1,
        )
        query_w, key_w, value_w, out_w = call(
            attn_grad_sum_kernel,
            [after(attn_here, input_own), swap_across(attn_send, 1)],
            [
                shape((block, 256), f32),
                shape((block, 128), f32),
                shape((block, 128), f32),
                shape((256, block), bf16),
            ],
            work=1,
        )
        turn = []
        for a in range(n_tp):
            for b in range(2):
                for t in range(n_tp):
                    turn.append(((2 * a + b) * n_tp + t, (2 * t + b) * n_tp + a))
        out_w = lax.ppermute(out_w, ("ctx", "tp"), turn)
    else:

        def scatter(left, right, dim=0):
            grad = dot(left, right, TN).astype(bf16)
            return lax.psum_scatter(grad, "ctx", scatter_dimension=dim, tiled=True).astype(f32)

        attn_grad_all = lax.all_gather(attn_grad, "tp", axis=0, tiled=True)
        down_w = scatter(act, out_grad, 1)
        gate_w = scatter(h_two, gate_grad)
        up_w = scatter(h_two, up_grad)
        out_w = scatter(attended, attn_grad_all, 1)
        query_w = scatter(h_one, query_pre_low)
        kv_w = scatter(h_one, kv_pre_low)
        key_w, value_w = kv_w[:, :128], kv_w[:, 128:]

    gain_one_sum, gain_two_sum, q_gain_sum, k_gain_sum, out_w = call(
        functools.partial(gain_kernel, block),
        [gains, last_gains, out_w],
        [shape((1, block), f32)] * 2 + [shape((1, 64), f32)] * 2 + [shape(out_w.shape, f32)],
        work=1,
    )
    input_parts[0] = after(input_parts[0], gate_w, layer_out)
    input_grad = call(
        join_kernel, input_parts, [shape((rows, width), f32)]
    )[0]

    return (
        layer_out,
        input_grad,
        gain_one_sum[0],
        query_w,
        key_w,
        value_w,
        q_gain_sum[0],
        k_gain_sum[0],
        out_w,
        gain_two_sum[0],
        gate_w,
        up_w,
        down_w,
    )


def solution(mesh):
    in_specs = (
        P("ctx", None),
        P(),
        P(),
        P(None, "tp"),
        P(None, "tp"),
        P(None, "tp"),
        P(),
        P(),
        P("tp", None),
        P(),
        P(None, "tp"),
        P(None, "tp"),
        P("tp", None),
        P("ctx", None),
    )
    out_specs = (
        P("ctx", None),
        P("ctx", None),
        P("ctx"),
        P("ctx", "tp"),
        P("ctx", "tp"),
        P("ctx", "tp"),
        P(),
        P(),
        P("tp", "ctx"),
        P("ctx"),
        P("ctx", "tp"),
        P("ctx", "tp"),
        P("tp", "ctx"),
    )
    return jax.shard_map(shards, mesh=mesh, in_specs=in_specs, out_specs=out_specs, check_vma=False)
```
